32 devices in a mesh: dp: 16 (over z, y, core), mp: 2 (over x).
Axes of the slice: x: 2, y: 2, z: 4, core: 2. Of those that a mesh axis runs over, the one named last changes fastest.
Arguments:
- tokens: bfloat16 [16384, 768], P(('dp', 'mp')), may hold values from -6 to 6
- cotangent: bfloat16 [16384, 768], P(('dp', 'mp')), may hold values from -6 to 6
- segment_ids: int32 [16, 1024], P('dp'), may hold values from 0 to 15, never falling along the last dimension, each value on 1 to 512 neighbouring positions
- key_keep: int32 [16, 1024], P('dp'), may hold values 0 or 1
- in_weight: bfloat16 [768, 3, 768], P(None, None, 'mp'), may hold values from -0.21875 to 0.21875
- out_weight: bfloat16 [768, 768], P('mp'), may hold values from -0.875 to 0.875
- up_weight: bfloat16 [768, 3072], P(None, 'mp'), may hold values from -0.21875 to 0.21875
- down_weight: bfloat16 [3072, 768], P('mp'), may hold values from -0.109375 to 0.109375
- in_master: float32 [768, 3, 768], P('dp', None, 'mp'), may hold values from -0.21875 to 0.21875
- out_master: float32 [768, 768], P(('mp', 'dp')), may hold values from -0.875 to 0.875
- up_master: float32 [768, 3072], P('dp', 'mp'), may hold values from -0.21875 to 0.21875
- down_master: float32 [3072, 768], P(('mp', 'dp')), may hold values from -0.109375 to 0.109375
- in_first: float32 [768, 3, 768], P('dp', None, 'mp'), may hold values from -153.6 to 153.6
- out_first: float32 [768, 768], P(('mp', 'dp')), may hold values from -46.08 to 46.08
- up_first: float32 [768, 3072], P('dp', 'mp'), may hold values from -153.6 to 153.6
- down_first: float32 [3072, 768], P(('mp', 'dp')), may hold values from -307.2 to 307.2
- in_second: float32 [768, 3, 768], P('dp', None, 'mp'), may hold values from 655.36 to 2621.44
- out_second: float32 [768, 768], P(('mp', 'dp')), may hold values from 58.9824 to 235.9296
- up_second: float32 [768, 3072], P('dp', 'mp'), may hold values from 655.36 to 2621.44
- down_second: float32 [3072, 768], P(('mp', 'dp')), may hold values from 2621.44 to 10485.76
- vector_master: float32 [9216], replicated, may hold values from -1.5 to 1.5
- vector_first: float32 [9216], replicated, may hold values from -384 to 384
- vector_second: float32 [9216], replicated, may hold values from 4096 to 16384
Outputs:
- layer_out: bfloat16 [16384, 768], P(('dp', 'mp'))
- token_grad: bfloat16 [16384, 768], P(('dp', 'mp'))
- in_first_next: float32 [768, 3, 768], P('dp', None, 'mp')
- in_second_next: float32 [768, 3, 768], P('dp', None, 'mp')
- in_master_next: float32 [768, 3, 768], P('dp', None, 'mp')
- in_weight_next: bfloat16 [768, 3, 768], P('dp', None, 'mp')
- out_first_next: float32 [768, 768], P(('mp', 'dp'))
- out_second_next: float32 [768, 768], P(('mp', 'dp'))
- out_master_next: float32 [768, 768], P(('mp', 'dp'))
- out_weight_next: bfloat16 [768, 768], P(('mp', 'dp'))
- up_first_next: float32 [768, 3072], P('dp', 'mp')
- up_second_next: float32 [768, 3072], P('dp', 'mp')
- up_master_next: float32 [768, 3072], P('dp', 'mp')
- up_weight_next: bfloat16 [768, 3072], P('dp', 'mp')
- down_first_next: float32 [3072, 768], P(('mp', 'dp'))
- down_second_next: float32 [3072, 768], P(('mp', 'dp'))
- down_master_next: float32 [3072, 768], P(('mp', 'dp'))
- down_weight_next: bfloat16 [3072, 768], P(('mp', 'dp'))
- vector_first_next: float32 [9216], replicated
- vector_second_next: float32 [9216], replicated
- vector_master_next: float32 [9216], replicated
The draws below stay inside these ranges and needn't reach their ends.
Inputs may be any that keep to these rules, and one draw needn't show every extreme that they name: `segment_ids`: in each row ids never fall, every id of 0 to 15 holds 1 to 512 positions, and one holds exactly 512.
All inputs are finite; a program needn't handle non-finite values. No bound on the sum of `key_keep` on one device may be relied on, other than what follows from the above.
Results may differ from the reference program's by a relative error of at most 0.017.
Values may be sent and summed in bfloat16 or wider, within the bound.
No kernel may reach another device: no remote copies, remote signals or barrier semaphores. Data moves between devices by JAX's collectives and lax.ppermute only.
A program may use at most 192 MiB of HBM per device.

```python
import math
import jax
import jax.numpy as jnp
import numpy as np
from jax import lax

D = 768
HEADS = 12
HD = 64
FF = 3072
TOK_DEV = 1024
STEP = 7
SEQ_MOST = 512
SEGS = 16
GROUPS = 16
TOKENS = 16384
N_DP = 16


def draw_vector_master(key, part):
    keys = jax.random.split(key, 6)

    def biases(index, length):
        return 0.3 * jnp.clip(jax.random.normal(keys[index], (length,), jnp.float32), -4.0, 4.0)

    def gains(index, length):
        return jax.random.uniform(keys[index], (length,), jnp.float32, 0.6, 1.4)
    return jnp.concatenate([biases(0, 4 * D), gains(1, D), biases(2, D), gains(3, D), biases(4, D), biases(5, FF)])


def touch_ends(values, own_key, low, largest):
    longest = values.shape.index(max(values.shape))
    spots = []
    for shift in (0, 1):
        where = [jax.random.randint(jax.random.fold_in(own_key, axis), (), 0, length) for axis, length in enumerate(values.shape)]
        where[longest] = (where[longest] + shift) % values.shape[longest]
        spots.append(tuple(where))
    return values.at[spots[0]].set(low).at[spots[1]].set(largest)


def shard_levels(stream_key, extent, cuts, low, high):
    def one(axis_at, shards_of):
        steps = jax.random.uniform(jax.random.fold_in(jax.random.fold_in(stream_key, 6), axis_at), (shards_of,), jnp.float32, low / len(cuts), high / len(cuts))
        return jnp.repeat(jnp.exp(steps), extent[axis_at] // shards_of).reshape((-1,) + (1,) * (len(extent) - axis_at - 1))

    level = one(*cuts[0])
    for cut in cuts[1:]:
        level = level * one(*cut)
    return level


def split_up(amount, total, limit, skew):
    portions = [(1 << 20) // math.isqrt(rank ** skew) + 1 for rank in range(2, amount + 1)]
    surplus, holding = total - limit - (amount - 1), [1] * (amount - 1)
    while surplus > 0:
        candidates = [i for i in range(amount - 1) if holding[i] < limit]
        whole, budget = sum([portions[i] for i in candidates]), surplus
        for i in candidates:
            more = min(limit - holding[i], max(1, budget * portions[i] // whole), surplus)
            holding[i] = holding[i] + more
            surplus = surplus - more
    return np.array([limit] + holding)


def uneven(key, number_of, total, bound, slope):
    if number_of == 2:
        one = jax.random.randint(key, (), max(1, total - bound), min(bound, total - 1) + 1)
        return jnp.stack([one, total - one])
    tallies = jnp.asarray(split_up(number_of, total, bound, slope), jnp.int32)
    twos = (number_of - 1) // 2
    donor, receiver = tallies[1:1 + 2 * twos:2], tallies[2:2 + 2 * twos:2]
    margin = jnp.minimum(donor - 1, bound - receiver)
    shifted = jax.random.randint(jax.random.fold_in(key, 1), (twos,), 0, 1 << 20) % (margin + 1)
    tallies = tallies.at[1:1 + 2 * twos:2].set(donor - shifted).at[2:2 + 2 * twos:2].set(receiver + shifted)
    return tallies[jax.random.permutation(jax.random.fold_in(key, 2), number_of)]


def gaussian(rng, dims, deviation, limit, cuts=(), kind=jnp.bfloat16):
    loudness = shard_levels(rng, dims, cuts, -0.22, 0.18) if cuts else 1.0
    entries = jax.random.normal(rng, dims, jnp.float32) * deviation * loudness
    return jnp.minimum(jnp.maximum(entries, -limit), limit).astype(kind)


def setup_inputs(seed: int = 0) -> dict:
    key_list = jax.random.split(jax.random.key(seed), 24)
    tokens = gaussian(key_list[0], (TOKENS, D), 1.0, 6.0, ((0, 32),))
    cotangent = gaussian(key_list[1], (TOKENS, D), 1.0, 6.0, ((0, 32),))
    segment_ids = jax.vmap(lambda own: jnp.searchsorted(jnp.cumsum(uneven(own, SEGS, TOK_DEV, SEQ_MOST, 2)), jnp.arange(TOK_DEV), side="right"))(jax.random.split(key_list[2], GROUPS)).reshape((GROUPS, TOK_DEV)).astype(jnp.int32)
    key_keep = touch_ends((jax.random.randint(key_list[3], (GROUPS, TOK_DEV), 0, 8) < 7).astype(jnp.int32), jax.random.fold_in(key_list[3], 1), 0, 1)
    in_weight = gaussian(key_list[4], (D, 3, D), D ** -0.5, 0.21875, ((2, 2),))
    out_weight = gaussian(key_list[5], (D, D), (D // 16) ** -0.5, 0.875, ((0, 2),))
    up_weight = gaussian(key_list[6], (D, FF), D ** -0.5, 0.21875, ((1, 2),))
    down_weight = gaussian(key_list[7], (FF, D), FF ** -0.5, 0.109375, ((0, 2),))
    in_master = gaussian(key_list[8], (D, 3, D), D ** -0.5, 0.21875, ((0, 16), (2, 2)), jnp.float32)
    out_master = gaussian(key_list[9], (D, D), (D // 16) ** -0.5, 0.875, ((0, 32),), jnp.float32)
    up_master = gaussian(key_list[10], (D, FF), D ** -0.5, 0.21875, ((0, 16), (1, 2)), jnp.float32)
    down_master = gaussian(key_list[11], (FF, D), FF ** -0.5, 0.109375, ((0, 32),), jnp.float32)
    in_first = gaussian(key_list[12], (D, 3, D), (0.2 * TOKENS ** 0.5), 153.6, ((0, 16), (2, 2)), jnp.float32)
    out_first = gaussian(key_list[13], (D, D), (0.06 * TOKENS ** 0.5), 46.08, ((0, 32),), jnp.float32)
    up_first = gaussian(key_list[14], (D, FF), (0.2 * TOKENS ** 0.5), 153.6, ((0, 16), (1, 2)), jnp.float32)
    down_first = gaussian(key_list[15], (FF, D), (0.4 * TOKENS ** 0.5), 307.2, ((0, 32),), jnp.float32)
    in_second = jnp.clip(jnp.exp(math.log(2621.44) - 1.3862944 * jax.random.uniform(key_list[16], (D, 3, D), jnp.float32) ** shard_levels(key_list[16], (D, 3, D), ((0, 16), (2, 2)), -0.2, 0.2)), 655.36, 2621.44)
    out_second = jnp.clip(jnp.exp(math.log(235.9296) - 1.3862944 * jax.random.uniform(key_list[17], (D, D), jnp.float32) ** shard_levels(key_list[17], (D, D), ((0, 32),), -0.2, 0.2)), 58.9824, 235.9296)
    up_second = jnp.clip(jnp.exp(math.log(2621.44) - 1.3862944 * jax.random.uniform(key_list[18], (D, FF), jnp.float32) ** shard_levels(key_list[18], (D, FF), ((0, 16), (1, 2)), -0.2, 0.2)), 655.36, 2621.44)
    down_second = jnp.clip(jnp.exp(math.log(10485.76) - 1.3862944 * jax.random.uniform(key_list[19], (FF, D), jnp.float32) ** shard_levels(key_list[19], (FF, D), ((0, 32),), -0.2, 0.2)), 2621.44, 10485.76)
    vector_master = draw_vector_master(jax.random.fold_in(key_list[23], 71), 0)
    vector_first = gaussian(key_list[21], (8 * D + FF,), (0.5 * TOKENS ** 0.5), 384.0, (), jnp.float32)
    vector_second = jnp.clip(jnp.exp(jax.random.uniform(key_list[22], (8 * D + FF,), jnp.float32, math.log(4096.0), math.log(16384.0))), 4096.0, 16384.0)
    return dict(tokens=tokens, cotangent=cotangent, segment_ids=segment_ids, key_keep=key_keep, in_weight=in_weight, out_weight=out_weight, up_weight=up_weight, down_weight=down_weight, in_master=in_master, out_master=out_master, up_master=up_master, down_master=down_master, in_first=in_first, out_first=out_first, up_first=up_first, down_first=down_first, in_second=in_second, out_second=out_second, up_second=up_second, down_second=down_second, vector_master=vector_master, vector_first=vector_first, vector_second=vector_second)


HIGH = lax.Precision.HIGHEST
NORM_EPS = 1e-06
SCORE_SCALE = 0.125
NEG_FILL = -1e+30
MOMENT_DECAY = 0.5
SQUARE_DECAY = 0.5
MATRIX_RATE = 0.03
VECTOR_RATE = 0.2
WEIGHT_DECAY = 0.01
ADAM_EPS = 1e-08

@jax.custom_vjp
def low(v):
    return lax.optimization_barrier(v.astype(jnp.bfloat16)).astype(jnp.float32)

@jax.custom_vjp
def low_back(v):
    return v

def low_keep(v):
    return (low(v), None)

def low_pass(kept, grad):
    return (grad,)

def back_keep(v):
    return (v, None)

def back_low(kept, grad):
    return (low(grad),)
low.defvjp(low_keep, low_pass)
low_back.defvjp(back_keep, back_low)

def norm_apply(hidden, gain, shift):
    mean = lax.optimization_barrier(jnp.mean(hidden, axis=-1, keepdims=True))
    centred = hidden - mean
    inverse = lax.rsqrt(lax.optimization_barrier(jnp.mean(centred * centred, axis=-1, keepdims=True)) + NORM_EPS)
    return centred * inverse * gain + shift

def layer(rows_in, in_weight, out_weight, up_weight, down_weight, vector, segments, visible):
    count = rows_in.shape[0]
    bias_query = vector[0:D]
    bias_value = vector[D:2 * D]
    bias_out = vector[2 * D:3 * D]
    bias_down = vector[3 * D:4 * D]
    gain_one = vector[4 * D:5 * D]
    shift_one = vector[5 * D:6 * D]
    gain_two = vector[6 * D:7 * D]
    shift_two = vector[7 * D:8 * D]
    bias_up = vector[8 * D:8 * D + FF]
    projected = low_back(jnp.einsum('td,dcn->tcn', rows_in, in_weight, precision=HIGH))
    projected = projected + jnp.stack([bias_query, jnp.zeros_like(bias_query), bias_value])[None]
    triple = low(projected)
    query = triple[:, 0].reshape(count, HEADS, HD)
    key = triple[:, 1].reshape(count, HEADS, HD)
    value = triple[:, 2].reshape(count, HEADS, HD)
    raw = low_back(jnp.einsum('qhd,khd->hqk', query, key, precision=HIGH)) * SCORE_SCALE
    positions = jnp.arange(count, dtype=jnp.int32)
    allowed = (segments[:, None] == segments[None, :]) & ((visible[None, :] == 1) | (positions[:, None] == positions[None, :]))
    scores = jnp.where(allowed[None], raw, NEG_FILL)
    highest = lax.optimization_barrier(jnp.max(scores, axis=-1, keepdims=True))
    weights = jnp.exp(scores - highest)
    probs = low(weights / lax.optimization_barrier(jnp.sum(weights, axis=-1, keepdims=True)))
    attended = low(low_back(jnp.einsum('hqk,khd->qhd', probs, value, precision=HIGH))).reshape(count, D)
    branch = low_back(jnp.dot(attended, out_weight, precision=HIGH)) + bias_out
    normed_one = norm_apply(rows_in + branch, gain_one, shift_one)
    normed_low = low(normed_one)
    upper = low_back(jnp.dot(normed_low, up_weight, precision=HIGH)) + bias_up
    activation = low(jax.nn.gelu(upper, approximate=False))
    hidden_two = normed_one + low_back(jnp.dot(activation, down_weight, precision=HIGH)) + bias_down
    return norm_apply(hidden_two, gain_two, shift_two)

def adam_step(grad, master, first, second, rate, decay):
    first_next = MOMENT_DECAY * first + (1.0 - MOMENT_DECAY) * grad
    second_next = SQUARE_DECAY * second + (1.0 - SQUARE_DECAY) * grad * grad
    first_fix = 1.0 - MOMENT_DECAY ** STEP
    second_fix = 1.0 - SQUARE_DECAY ** STEP
    update = first_next / first_fix / (jnp.sqrt(second_next / second_fix) + ADAM_EPS)
    master_next = master - rate * (update + decay * master)
    return (first_next, second_next, master_next)

def reference(tokens, cotangent, segment_ids, key_keep, in_weight, out_weight, up_weight, down_weight, in_master, out_master, up_master, down_master, in_first, out_first, up_first, down_first, in_second, out_second, up_second, down_second, vector_master, vector_first, vector_second):
    rows = tokens.astype(jnp.float32).reshape(N_DP, TOK_DEV, D)
    backs = cotangent.astype(jnp.float32).reshape(N_DP, TOK_DEV, D)
    weights = (in_weight.astype(jnp.float32), out_weight.astype(jnp.float32), up_weight.astype(jnp.float32), down_weight.astype(jnp.float32), vector_master)

    def group(carry, items):
        rows_in, back, segments, visible = items

        def forward(inputs, w_in, w_out, w_up, w_down, vector):
            return layer(inputs, w_in, w_out, w_up, w_down, vector, segments, visible)
        result, pull = jax.vjp(forward, rows_in, *weights)
        grads = pull(back)
        carry = tuple((total + grad for total, grad in zip(carry, grads[1:])))
        return (carry, (result.astype(jnp.bfloat16), grads[0].astype(jnp.bfloat16)))
    init = tuple((jnp.zeros_like(weight) for weight in weights))
    sums, (results, input_grads) = lax.scan(group, init, (rows, backs, segment_ids, key_keep))
    grad_in, grad_out, grad_up, grad_down, grad_vector = sums
    in_f, in_s, in_m = adam_step(grad_in, in_master, in_first, in_second, MATRIX_RATE, WEIGHT_DECAY)
    out_f, out_s, out_m = adam_step(grad_out, out_master, out_first, out_second, MATRIX_RATE, WEIGHT_DECAY)
    up_f, up_s, up_m = adam_step(grad_up, up_master, up_first, up_second, MATRIX_RATE, WEIGHT_DECAY)
    down_f, down_s, down_m = adam_step(grad_down, down_master, down_first, down_second, MATRIX_RATE, WEIGHT_DECAY)
    vec_f, vec_s, vec_m = adam_step(grad_vector, vector_master, vector_first, vector_second, VECTOR_RATE, 0.0)
    return (results.reshape(TOKENS, D), input_grads.reshape(TOKENS, D), in_f, in_s, in_m, in_m.astype(jnp.bfloat16), out_f, out_s, out_m, out_m.astype(jnp.bfloat16), up_f, up_s, up_m, up_m.astype(jnp.bfloat16), down_f, down_s, down_m, down_m.astype(jnp.bfloat16), vec_f, vec_s, vec_m)
```

```python
import functools

import jax
import jax.numpy as jnp
from jax import lax
from jax.experimental import pallas as pl
from jax.experimental.pallas import tpu as pltpu
from jax.sharding import PartitionSpec as P

HD = 64
STEP = 7
NORM_EPS = 1e-06
SCORE_SCALE = 0.125
NEG_FILL = -1e30
MOMENT_DECAY = 0.5
SQUARE_DECAY = 0.5
MATRIX_RATE = 0.03
VECTOR_RATE = 0.2
WEIGHT_DECAY = 0.01
ADAM_EPS = 1e-08
LOG2E = 1.4426950408889634
SCALE2 = SCORE_SCALE * LOG2E
F32 = jnp.float32
BF16 = jnp.bfloat16
MIB = 1024 * 1024

NN = (((1,), (0,)), ((), ()))
NT = (((1,), (1,)), ((), ()))
TN = (((0,), (0,)), ((), ()))


def mm(a, b, dims=NN):
    return lax.dot_general(a, b, dims, preferred_element_type=F32)


def call(kernel, outs, args, scratch=(), flops=0, nbytes=0, limit=40, name=None):
    return pl.pallas_call(
        kernel,
        out_shape=[jax.ShapeDtypeStruct(s, d) for s, d in outs],
        scratch_shapes=list(scratch),
        compiler_params=pltpu.CompilerParams(vmem_limit_bytes=limit * MIB),
        cost_estimate=pl.CostEstimate(flops=flops, bytes_accessed=nbytes, transcendentals=0),
        name=name,
    )(*args)


def adam_step(grad, master, first, second, rate, decay):
    first_next = MOMENT_DECAY * first + (1.0 - MOMENT_DECAY) * grad
    second_next = SQUARE_DECAY * second + (1.0 - SQUARE_DECAY) * grad * grad
    first_fix = 1.0 - MOMENT_DECAY**STEP
    second_fix = 1.0 - SQUARE_DECAY**STEP
    update = first_next / first_fix / (jnp.sqrt(second_next / second_fix) + ADAM_EPS)
    master_next = master - rate * (update + decay * master)
    return (first_next, second_next, master_next)


def fill_mask(seg_ref, code_ref, mask_ref):
    rows = mask_ref.shape[0]
    row = lax.broadcasted_iota(jnp.int32, (rows, rows), 0)
    col = lax.broadcasted_iota(jnp.int32, (rows, rows), 1)
    allowed = (seg_ref[...] == code_ref[...]) | (row == col)
    mask_ref[...] = jnp.where(allowed, 0.0, NEG_FILL)


def split_pair(block):
    lane = lax.broadcasted_iota(jnp.int32, block.shape, 1)
    zero = jnp.zeros_like(block)
    return (jnp.where(lane < HD, block, zero), jnp.where(lane < HD, zero, block))


def attend_forward_kernel(
    x_ref, w_ref, b_ref, seg_ref, code_ref, q_ref, k_ref, v_ref, o_ref, lse_ref, mask_ref
):
    rows, width = q_ref.shape
    block = 256
    fill_mask(seg_ref, code_ref, mask_ref)
    x = x_ref[...]
    for part, ref in enumerate((q_ref, k_ref, v_ref)):
        ref[...] = (mm(x, w_ref[part]) + b_ref[part]).astype(BF16)
    lane = lax.broadcasted_iota(jnp.int32, (block, 128), 1)
    lse_ref[...] = jnp.zeros_like(lse_ref)

    def one(step, carry):
        pair = step // (rows // block)
        start = pl.multiple_of((step % (rows // block)) * block, block)
        cols = pl.ds(pl.multiple_of(pair * 128, 128), 128)
        here = pl.ds(start, block)
        q = q_ref[here, cols]
        keys = split_pair(k_ref[:, cols])
        values = split_pair(v_ref[:, cols])
        mask = mask_ref[here, :]
        total = jnp.zeros((block, 128), F32)
        lse = lse_ref[here, :]
        for which in range(2):
            scores = mm(q, keys[which], NT) * SCALE2 + mask
            highest = jnp.max(scores, axis=1, keepdims=True)
            weights = jnp.exp2(scores - highest)
            sums = jnp.sum(weights, axis=1, keepdims=True)
            probs = (weights * (1.0 / sums)).astype(BF16)
            total = total + mm(probs, values[which])
            lse = jnp.where(lane == 2 * pair + which, highest + jnp.log2(sums), lse)
        o_ref[here, cols] = total.astype(BF16)
        lse_ref[here, :] = lse
        return carry

    lax.fori_loop(0, (width // 128) * (rows // block), one, 0)


def attend_backward_kernel(
    last,
    x_ref,
    w_ref,
    q_ref,
    k_ref,
    v_ref,
    do_ref,
    lse_ref,
    seg_ref,
    code_ref,
    base_ref,
    gin_ref,
    tg_ref,
    gb_ref,
    mask_ref,
    dq_ref,
    dk_ref,
    dv_ref,
):
    rows, width = q_ref.shape
    block = 256
    fill_mask(seg_ref, code_ref, mask_ref)
    dk_ref[...] = jnp.zeros_like(dk_ref)
    dv_ref[...] = jnp.zeros_like(dv_ref)
    lane = lax.broadcasted_iota(jnp.int32, (block, 128), 1)

    def one(step, carry):
        pair = step // (rows // block)
        start = pl.multiple_of((step % (rows // block)) * block, block)
        cols = pl.ds(pl.multiple_of(pair * 128, 128), 128)
        here = pl.ds(start, block)
        q = q_ref[here, cols]
        grad = do_ref[here, cols]
        keys = split_pair(k_ref[:, cols])
        values = split_pair(v_ref[:, cols])
        queries = split_pair(q)
        grads = split_pair(grad)
        mask = mask_ref[here, :]
        lse_all = lse_ref[here, :]
        dq = jnp.zeros((block, 128), F32)
        dk = dk_ref[:, cols]
        dv = dv_ref[:, cols]
        for which in range(2):
            scores = mm(q, keys[which], NT) * SCALE2 + mask
            lse = jnp.sum(jnp.where(lane == 2 * pair + which, lse_all, 0.0), axis=1, keepdims=True)
            probs = jnp.exp2(scores - lse)
            gprobs = mm(grad, values[which], NT)
            weighted = probs * gprobs
            delta = jnp.sum(weighted, axis=1, keepdims=True)
            gscores = ((weighted - probs * delta) * SCORE_SCALE).astype(BF16)
            dq = dq + mm(gscores, keys[which])
            dk = dk + mm(gscores, queries[which], TN)
            dv = dv + mm(probs.astype(BF16), grads[which], TN)
        dq_ref[here, cols] = dq
        dk_ref[:, cols] = dk
        dv_ref[:, cols] = dv
        return carry

    lax.fori_loop(0, (width // 128) * (rows // block), one, 0)
    x = x_ref[...]
    total = base_ref[...]
    for part, ref in enumerate((dq_ref, dk_ref, dv_ref)):
        grad = ref[...]
        gb_ref[part] = jnp.sum(grad, axis=0, keepdims=True)
        grad_low = grad.astype(BF16)
        gin_ref[part] = mm(x, grad_low, TN).astype(BF16)
        total = total + mm(grad_low, w_ref[part], NT)
    tg_ref[...] = total.astype(tg_ref.dtype)


def norm_stats(hidden):
    mean = jnp.mean(hidden, axis=1, keepdims=True)
    centred = hidden - mean
    inverse = lax.rsqrt(jnp.mean(centred * centred, axis=1, keepdims=True) + NORM_EPS)
    return centred * inverse, inverse


def out_norm_kernel(tok_ref, oa_ref, ob_ref, wa_ref, wb_ref, vec_ref, unit_ref, inv_ref, low_ref):
    hidden = tok_ref[...].astype(F32) + (mm(oa_ref[...], wa_ref[...]) + mm(ob_ref[...], wb_ref[...]))
    unit, inverse = norm_stats(hidden + vec_ref[0:1, :])
    unit_ref[...] = unit
    inv_ref[...] = inverse
    low_ref[...] = (unit * vec_ref[1:2, :] + vec_ref[2:3, :]).astype(BF16)


def gelu_parts(x):
    size = jnp.abs(x) * 0.7071067811865476
    bell = jnp.exp2(x * x * (-0.5 * LOG2E))
    t = 1.0 / (1.0 + 0.3275911 * size)
    poly = t * (
        0.254829592 + t * (-0.284496736 + t * (1.421413741 + t * (-1.453152027 + t * 1.061405429)))
    )
    tail = 0.5 * poly * bell
    below = jnp.where(x >= 0.0, 1.0 - tail, tail)
    return x * below, below + x * bell * 0.3989422804014327


def ffn_up_half(low_ref, up_ref, down_ref, b_ref, act_ref, pull_ref, total_ref):
    tile = 256
    low = low_ref[...]

    def one(step, carry):
        cols = pl.ds(pl.multiple_of(step * tile, tile), tile)
        upper = mm(low, up_ref[:, cols]) + b_ref[:, cols]
        value, pull = gelu_parts(upper)
        value = value.astype(BF16)
        act_ref[:, cols] = value
        pull_ref[:, cols] = pull
        total_ref[...] += mm(value, down_ref[cols, :])
        return carry

    lax.fori_loop(0, up_ref.shape[1] // tile, one, 0)


def ffn_forward_kernel(low_ref, up_ref, down_ref, b_ref, act_ref, pull_ref, total_ref):
    total_ref[...] = jnp.zeros_like(total_ref)
    ffn_up_half(low_ref, up_ref, down_ref, b_ref, act_ref, pull_ref, total_ref)


def ffn_forward_last_kernel(
    low_ref,
    up_ref,
    down_ref,
    b_ref,
    part_ref,
    unit_ref,
    vec_ref,
    cot_ref,
    act_ref,
    pull_ref,
    out_ref,
    grad_ref,
    glow_ref,
    sums_ref,
    total_ref,
):
    total_ref[...] = part_ref[...]
    ffn_up_half(low_ref, up_ref, down_ref, b_ref, act_ref, pull_ref, total_ref)
    normed = unit_ref[...] * vec_ref[1:2, :] + vec_ref[2:3, :]
    unit, inverse = norm_stats(normed + total_ref[...] + vec_ref[3:4, :])
    gain = vec_ref[4:5, :]
    out_ref[...] = (unit * gain + vec_ref[5:6, :]).astype(BF16)
    cot = cot_ref[...].astype(F32)
    sums_ref[...] = jnp.zeros_like(sums_ref)
    sums_ref[1:2, :] = jnp.sum(cot * unit, axis=0, keepdims=True)
    sums_ref[2:3, :] = jnp.sum(cot, axis=0, keepdims=True)
    scaled = cot * gain
    grad = inverse * (
        scaled
        - jnp.mean(scaled, axis=1, keepdims=True)
        - unit * jnp.mean(scaled * unit, axis=1, keepdims=True)
    )
    sums_ref[0:1, :] = jnp.sum(grad, axis=0, keepdims=True)
    grad_ref[...] = grad
    glow_ref[...] = grad.astype(BF16)


def ffn_backward_kernel(
    low_ref, glow_ref, act_ref, pull_ref, up_ref, down_ref, base_ref, gdown_ref, gup_ref, gn_ref, gb_ref
):
    tile = 256
    low = low_ref[...]
    glow = glow_ref[...]
    gn_ref[...] = base_ref[...]

    def one(step, carry):
        cols = pl.ds(pl.multiple_of(step * tile, tile), tile)
        gdown_ref[cols, :] = mm(act_ref[:, cols], glow, TN).astype(BF16)
        gupper = mm(glow, down_ref[cols, :], NT) * pull_ref[:, cols]
        gb_ref[:, cols] = jnp.sum(gupper, axis=0, keepdims=True)
        gupper = gupper.astype(BF16)
        gup_ref[:, cols] = mm(low, gupper, TN).astype(BF16)
        gn_ref[...] += mm(gupper, up_ref[:, cols], NT)
        return carry

    lax.fori_loop(0, up_ref.shape[1] // tile, one, 0)


def norm_back_kernel(
    gn_ref, unit_ref, inv_ref, vec_ref, oa_ref, ob_ref, wa_ref, wb_ref, grad_ref, ga_ref, gb_ref, goa_ref, gob_ref, sums_ref
):
    gn = gn_ref[...]
    unit = unit_ref[...]
    sums_ref[...] = jnp.zeros_like(sums_ref)
    sums_ref[1:2, :] = jnp.sum(gn * unit, axis=0, keepdims=True)
    sums_ref[2:3, :] = jnp.sum(gn, axis=0, keepdims=True)
    scaled = gn * vec_ref[1:2, :]
    grad = inv_ref[...] * (
        scaled
        - jnp.mean(scaled, axis=1, keepdims=True)
        - unit * jnp.mean(scaled * unit, axis=1, keepdims=True)
    )
    sums_ref[0:1, :] = jnp.sum(grad, axis=0, keepdims=True)
    grad_ref[...] = grad
    low = grad.astype(BF16)
    ga_ref[...] = mm(low, wa_ref[...], NT).astype(BF16)
    gb_ref[...] = mm(low, wb_ref[...], NT).astype(BF16)
    goa_ref[...] = mm(oa_ref[...], low, TN).astype(BF16)
    gob_ref[...] = mm(ob_ref[...], low, TN).astype(BF16)


def flip(values, axis, bit, count):
    pairs = [(i, i ^ (1 << bit)) for i in range(count)]
    return lax.ppermute(values, axis, pairs)


def fetch_other(own, dp_index, dp_count):
    quarter = own.shape[0] // 4
    place = dp_index % 4
    mine = lax.dynamic_slice_in_dim(own, place * quarter, quarter, 0)
    first = flip(mine, "mp", 0, 2)
    second = flip(first, "dp", 1, dp_count)
    pair = jnp.concatenate([first, second], axis=0)
    other = flip(pair, "dp", 0, dp_count)
    stack = jnp.concatenate([first, other[:quarter], second, other[quarter:]], axis=0)
    parts = [
        lax.dynamic_slice_in_dim(stack, (place ^ k) * quarter, quarter, 0) for k in range(4)
    ]
    return jnp.concatenate(parts, axis=0)


def halve(values, bit):
    split = values.reshape((values.shape[0] // 2, 2) + values.shape[1:])
    keep = lax.dynamic_index_in_dim(split, bit, 1, keepdims=False)
    send = lax.dynamic_index_in_dim(split, 1 - bit, 1, keepdims=False)
    return keep, send


def reduce_owned(own, other, dp_index, dp_count, order):
    bits = dp_count.bit_length() - 1
    done = 0
    final = len(order) - 1
    for place, name in enumerate(order):
        kind = F32 if place == final else BF16
        if name == "x":
            got = flip(other, "mp", 0, 2)
            own = (own.astype(F32) + got.astype(F32)).astype(kind)
            other = None
            continue
        bit = (dp_index >> done) & 1
        joined = []
        for values in (own, other):
            if values is None:
                joined.append(None)
                continue
            keep, send = halve(values, bit)
            got = flip(send, "dp", done, dp_count)
            joined.append((keep.astype(F32) + got.astype(F32)).astype(kind))
        own, other = joined
        done += 1
    assert done == bits
    return own.reshape(own.shape[1:])


def sum_all(values, dp_count):
    values = values + flip(values, "mp", 0, 2)
    for bit in range(dp_count.bit_length() - 1):
        values = values + flip(values, "dp", bit, dp_count)
    return values


def body(
    tokens,
    cotangent,
    segment_ids,
    key_keep,
    in_weight,
    out_weight,
    up_weight,
    down_weight,
    in_master,
    out_master,
    up_master,
    down_master,
    in_first,
    out_first,
    up_first,
    down_first,
    in_second,
    out_second,
    up_second,
    down_second,
    vector_master,
    vector_first,
    vector_second,
):
    rows, width = tokens.shape
    m = lax.axis_index("mp")
    d = lax.axis_index("dp")
    dp_count = lax.axis_size("dp")
    hw = in_weight.shape[2]
    fw = up_weight.shape[1]
    half = rows // 2

    seg = segment_ids[0]
    keep = key_keep[0]
    spot = lax.iota(jnp.int32, rows + 1)
    place = jnp.sum(jnp.where(seg[: rows + 1] == seg[rows - 1 :], spot, 0))
    late = place > half
    low_row = jnp.where(late, half, 0)
    local = lax.iota(jnp.int32, rows)
    swapped = jnp.where(late, local >= place, local < place)
    window = lax.dynamic_slice_in_dim(swapped, low_row, half, 0)[:, None]

    def swap_rows(values):
        mine = lax.dynamic_slice_in_dim(values, low_row, half, 0)
        got = flip(mine, "mp", 0, 2)
        return lax.dynamic_update_slice_in_dim(values, jnp.where(window, got, mine), low_row, 0)

    def mine_of(line):
        own = lax.dynamic_slice_in_dim(line, m * rows, rows, 0)
        other = lax.dynamic_slice_in_dim(line, (1 - m) * rows, rows, 0)
        return jnp.where(swapped, other, own)

    seg_here = mine_of(seg)
    code = jnp.where(mine_of(keep) == 1, seg_here, -1)[None, :]
    seg_here = seg_here[:, None]

    x = swap_rows(tokens)
    in_own = jnp.transpose(in_weight, (1, 0, 2))
    in_other = jnp.transpose(
        fetch_other(jnp.transpose(in_own, (1, 0, 2)).reshape(width, 3 * hw), d, dp_count).reshape(width, 3, hw),
        (1, 0, 2),
    )
    out_other = fetch_other(out_weight, d, dp_count)
    up_other = fetch_other(up_weight, d, dp_count)
    down_other = fetch_other(down_weight, d, dp_count)
    cot = swap_rows(cotangent)

    def half_of(offset, size, which):
        return lax.dynamic_slice_in_dim(vector_master, offset + which * size, size)[None, :]

    rest = vector_master[2 * width : 8 * width].reshape(6, width)
    vec = jnp.stack([rest[0], rest[2], rest[3], rest[1], rest[4], rest[5], rest[0], rest[0]])

    def qkv_bias(which):
        q = half_of(0, hw, which)
        return jnp.stack([q, jnp.zeros_like(q), half_of(width, hw, which)])

    attn_flops = 2 * rows * width * 3 * hw + 4 * rows * rows * hw * 4
    wide = (rows, width)
    narrow = (rows, hw)

    def attend(w, which):
        return call(
            attend_forward_kernel,
            [(narrow, BF16)] * 4 + [((rows, 128), F32)],
            (x, w, qkv_bias(which), seg_here, code),
            [pltpu.VMEM((rows, rows), F32)],
            flops=attn_flops,
            nbytes=8 * MIB,
            name="attend_forward",
        )

    q_a, k_a, v_a, o_a, lse_a = attend(in_own, m)
    q_b, k_b, v_b, o_b, lse_b = attend(in_other, 1 - m)
    unit, inverse, low = call(
        out_norm_kernel,
        [(wide, F32), ((rows, 1), F32), (wide, BF16)],
        (x, o_a, o_b, out_weight, out_other, vec),
        flops=2 * rows * width * width,
        nbytes=4 * MIB,
        name="out_norm",
    )
    hidden = (rows, fw)
    ffn_flops = 4 * rows * width * fw
    act_a, pull_a, part = call(
        ffn_forward_kernel,
        [(hidden, BF16), (hidden, F32), (wide, F32)],
        (low, up_weight, down_weight, half_of(8 * width, fw, m)),
        flops=ffn_flops * 3,
        nbytes=8 * MIB,
        name="ffn_forward_own",
    )
    act_b, pull_b, layer_out, grad_two, glow, sums_two = call(
        ffn_forward_last_kernel,
        [(hidden, BF16), (hidden, F32), (wide, BF16), (wide, F32), (wide, BF16), ((8, width), F32)],
        (low, up_other, down_other, half_of(8 * width, fw, 1 - m), part, unit, vec, cot),
        [pltpu.VMEM(wide, F32)],
        flops=ffn_flops * 3,
        nbytes=8 * MIB,
        name="ffn_forward_other",
    )
    layer_out = swap_rows(layer_out)

    def ffn_back(act, pull, up, down, base, name):
        return call(
            ffn_backward_kernel,
            [((fw, width), BF16), ((width, fw), BF16), (wide, F32), ((1, fw), F32)],
            (low, glow, act, pull, up, down, base),
            flops=2 * ffn_flops,
            nbytes=12 * MIB,
            name=name,
        )

    gdown_b, gup_b, gn, gb1_b = ffn_back(act_b, pull_b, up_other, down_other, grad_two, "ffn_backward_other")
    gdown_a, gup_a, gn, gb1_a = ffn_back(act_a, pull_a, up_weight, down_weight, gn, "ffn_backward_own")
    grad_one, gatt_a, gatt_b, gout_a, gout_b, sums_one = call(
        norm_back_kernel,
        [(wide, F32), (narrow, BF16), (narrow, BF16), ((hw, width), BF16), ((hw, width), BF16), ((8, width), F32)],
        (gn, unit, inverse, vec, o_a, o_b, out_weight, out_other),
        flops=4 * rows * width * width,
        nbytes=6 * MIB,
        name="norm_back",
    )

    def attend_back(w, q, k, v, gatt, lse, base, kind, name):
        return call(
            functools.partial(attend_backward_kernel, kind == BF16),
            [((3, width, hw), BF16), (wide, kind), ((3, 1, hw), F32)],
            (x, w, q, k, v, gatt, lse, seg_here, code, base),
            [pltpu.VMEM((rows, rows), F32)] + [pltpu.VMEM(narrow, F32)] * 3,
            flops=3 * attn_flops,
            nbytes=10 * MIB,
            name=name,
        )

    gin_b, tg, gb_b = attend_back(in_other, q_b, k_b, v_b, gatt_b, lse_b, grad_one, F32, "attend_backward_other")
    gin_a, tg, gb_a = attend_back(in_own, q_a, k_a, v_a, gatt_a, lse_a, tg, BF16, "attend_backward_own")
    token_grad = swap_rows(tg)

    bits = dp_count.bit_length() - 1
    x_early = ["d", "x"] + ["d"] * (bits - 1)
    x_later = ["d", "d", "x"] + ["d"] * (bits - 2)

    def rows_of(values, count=dp_count):
        return values.reshape(count, values.shape[0] // count, values.shape[1])

    grad_down = reduce_owned(rows_of(gdown_a), rows_of(gdown_b), d, dp_count, x_early)
    grad_up = reduce_owned(rows_of(gup_a), rows_of(gup_b), d, dp_count, x_later)
    grad_out = reduce_owned(rows_of(gout_a), rows_of(gout_b), d, dp_count, x_later)

    def gin_rows(values):
        return jnp.transpose(values.reshape(3, dp_count, width // dp_count, hw), (1, 0, 2, 3)).reshape(
            dp_count, 3 * width // dp_count, hw
        )

    grad_in = reduce_owned(gin_rows(gin_a), gin_rows(gin_b), d, dp_count, x_early)
    grad_in = jnp.transpose(grad_in.reshape(3, width // dp_count, hw), (1, 0, 2))

    def both(a, b):
        pair = jnp.stack([a.reshape(-1), b.reshape(-1)])
        return jnp.where(m == 0, pair, pair[::-1]).reshape(-1)

    grad_vector = jnp.concatenate(
        [
            both(gb_a[0], gb_b[0]),
            both(gb_a[2], gb_b[2]),
            sums_one[0],
            sums_two[0],
            sums_one[1],
            sums_one[2],
            sums_two[1],
            sums_two[2],
            both(gb1_a, gb1_b),
        ]
    )
    grad_vector = sum_all(grad_vector, dp_count)

    def matrix_step(grad, master, first, second):
        f, s, n = adam_step(grad, master, first, second, MATRIX_RATE, WEIGHT_DECAY)
        return (f, s, n, n.astype(BF16))

    return (
        layer_out,
        token_grad,
        *matrix_step(grad_in, in_master, in_first, in_second),
        *matrix_step(grad_out, out_master, out_first, out_second),
        *matrix_step(grad_up, up_master, up_first, up_second),
        *matrix_step(grad_down, down_master, down_first, down_second),
        *adam_step(grad_vector, vector_master, vector_first, vector_second, VECTOR_RATE, 0.0),
    )


def solution(mesh):
    tok = P(("dp", "mp"), None)
    line = P("dp", None)
    in_state = P("dp", None, "mp")
    out_state = P(("mp", "dp"), None)
    up_state = P("dp", "mp")
    states = (in_state, out_state, up_state, out_state)
    in_specs = (
        (tok, tok, line, line, P(None, None, "mp"), P("mp", None), P(None, "mp"), P("mp", None))
        + states * 3
        + (P(), P(), P())
    )
    out_specs = (
        (tok, tok)
        + (in_state,) * 4
        + (out_state,) * 4
        + (up_state,) * 4
        + (out_state,) * 4
        + (P(), P(), P())
    )
    return jax.shard_map(body, mesh=mesh, in_specs=in_specs, out_specs=out_specs, check_vma=False)
```

```python
import functools
import math

import jax
import jax.numpy as jnp
from jax import lax
from jax.experimental import pallas as pl
from jax.experimental.pallas import tpu as pltpu
from jax.sharding import PartitionSpec as P

HD = 64
STEP = 7
NORM_EPS = 1e-06
SCORE_SCALE = 0.125
NEG_FILL = -1e30
MOMENT_DECAY = 0.5
SQUARE_DECAY = 0.5
MATRIX_RATE = 0.03
VECTOR_RATE = 0.2
WEIGHT_DECAY = 0.01
ADAM_EPS = 1e-08
LOG2E = 1.4426950408889634
SCALE2 = SCORE_SCALE * LOG2E
F32 = jnp.float32
BF16 = jnp.bfloat16
MIB = 1024 * 1024
WORK = 1e6
SLACK = 8

NN = (((1,), (0,)), ((), ()))
NT = (((1,), (1,)), ((), ()))
TN = (((0,), (0,)), ((), ()))


def mm(a, b, dims=NN):
    return lax.dot_general(a, b, dims, preferred_element_type=F32)


def padded_bytes(shape, dtype):
    rows = shape[-2] if len(shape) > 1 else 1
    tiles = -(-rows // 8) * 8 * -(-shape[-1] // 128) * 128
    return math.prod(shape[:-2]) * tiles * jnp.dtype(dtype).itemsize


def call(kernel, outs, args, scratch=(), limit=None, name=None, after=(), through=(), places=None, out_places=None, us=1):
    count = len(args)
    places = places or {}
    out_places = out_places or {}
    anywhere = pl.BlockSpec(memory_space=pl.ANY)
    specs = [pl.BlockSpec(memory_space=places.get(i, pltpu.VMEM)) for i in range(count)]
    specs += [anywhere] * (len(through) + len(after))
    made = len(outs)
    if limit is None:
        held = [v for i, v in enumerate(args) if places.get(i, pltpu.VMEM) == pltpu.VMEM]
        held = [(v.shape, v.dtype) for v in held] + [v for i, v in enumerate(outs) if i not in out_places]
        held += [(v.shape, v.dtype) for v in scratch if v.memory_space == pltpu.VMEM]
        limit = sum(padded_bytes(*v) for v in held) // MIB + SLACK

    def run(*refs):
        own = refs[count + len(through) + len(after) :]
        kernel(*refs[:count], *own[:made], *own[made + len(through) :])

    return pl.pallas_call(
        run,
        out_shape=[jax.ShapeDtypeStruct(s, d) for s, d in outs]
        + [jax.ShapeDtypeStruct(v.shape, v.dtype) for v in through],
        in_specs=specs,
        out_specs=[pl.BlockSpec(memory_space=out_places.get(i, pltpu.VMEM)) for i in range(made)] + [anywhere] * len(through),
        scratch_shapes=list(scratch),
        input_output_aliases={count + i: made + i for i in range(len(through))},
        compiler_params=pltpu.CompilerParams(vmem_limit_bytes=limit * MIB),
        cost_estimate=pl.CostEstimate(flops=int(us * WORK), bytes_accessed=0, transcendentals=0),
        name=name,
    )(*args, *through, *after)


def adam_step(grad, master, first, second, rate, decay):
    first_next = MOMENT_DECAY * first + (1.0 - MOMENT_DECAY) * grad
    second_next = SQUARE_DECAY * second + (1.0 - SQUARE_DECAY) * grad * grad
    first_fix = 1.0 - MOMENT_DECAY**STEP
    second_fix = 1.0 - SQUARE_DECAY**STEP
    update = first_next / first_fix / (jnp.sqrt(second_next / second_fix) + ADAM_EPS)
    master_next = master - rate * (update + decay * master)
    return (first_next, second_next, master_next)


def prepare_kernel(
    tok_ref,
    cot_ref,
    in_ref,
    out_ref,
    up_ref,
    down_ref,
    seg_ref,
    keep_ref,
    stok_ref,
    scot_ref,
    sin_ref,
    sout_ref,
    sup_ref,
    sdown_ref,
    segcol_ref,
    code_ref,
    info_ref,
    sems,
):
    rows = tok_ref.shape[0]
    half = rows // 2
    m = lax.axis_index("mp")
    copies = []
    for i, (source, dest, axis, bit) in enumerate(
        ((in_ref, sin_ref, 1, 1), (out_ref, sout_ref, 0, 2), (down_ref, sdown_ref, 0, 2), (up_ref, sup_ref, 1, 1))
    ):
        size = dest.shape[axis]
        spot = pl.ds(pl.multiple_of(quarter_place(bit) * size, size), size)
        view = source.at[spot] if axis == 0 else source.at[:, spot]
        copies.append(pltpu.make_async_copy(view, dest, sems.at[i]))
    for copy in copies:
        copy.start()
    seg = seg_ref[...]
    spot = lax.broadcasted_iota(jnp.int32, seg.shape, 1)
    later = jnp.roll(seg, rows + 1, axis=1)
    begin = jnp.sum(jnp.where((seg == later) & (spot <= rows), spot, 0))
    late = begin > half
    first = jnp.where(late, half, 0)
    info_ref[0] = begin
    info_ref[1] = first
    window = pl.ds(pl.multiple_of(first, half), half)
    for i, (source, dest) in enumerate(((tok_ref, stok_ref), (cot_ref, scot_ref))):
        copy = pltpu.make_async_copy(source.at[window], dest, sems.at[4 + i])
        copy.start()
        copies.append(copy)
    own = pl.ds(pl.multiple_of(m * rows, rows), rows)
    other = pl.ds(pl.multiple_of((1 - m) * rows, rows), rows)
    local = lax.broadcasted_iota(jnp.int32, (1, rows), 1)
    swapped = jnp.where(late, local - begin, begin - 1 - local) >= 0
    mine = jnp.where(swapped, seg_ref[:, other], seg_ref[:, own])
    kept = jnp.where(swapped, keep_ref[:, other], keep_ref[:, own])
    code_ref[...] = jnp.where(kept == 1, mine, -1)
    column = jnp.broadcast_to(mine.astype(F32), (8, rows)).T
    segcol_ref[...] = column[:, 0:1].astype(jnp.int32)
    for copy in copies:
        copy.wait()


def swapped_rows(info_ref, shape):
    begin = info_ref[0]
    first = info_ref[1]
    local = first + lax.broadcasted_iota(jnp.int32, shape, 0)
    return jnp.where(first > 0, local - begin, begin - 1 - local) >= 0


def exchange_rows(info_ref, source_ref, got_ref, dest_ref):
    half = got_ref.shape[0]
    window = pl.ds(pl.multiple_of(info_ref[1], half), half)
    dest_ref[...] = source_ref[...]
    dest_ref[window, :] = jnp.where(swapped_rows(info_ref, got_ref.shape), got_ref[...], source_ref[window, :])


def fill_mask(seg_ref, code_ref, mask_ref):
    rows = mask_ref.shape[0]
    row = lax.broadcasted_iota(jnp.int32, (rows, rows), 0)
    col = lax.broadcasted_iota(jnp.int32, (rows, rows), 1)
    allowed = (seg_ref[...] == code_ref[...]) | (row == col)
    mask_ref[...] = jnp.where(allowed, 0.0, NEG_FILL)


def split_pair(block):
    lane = lax.broadcasted_iota(jnp.int32, block.shape, 1)
    zero = jnp.zeros_like(block)
    return (jnp.where(lane < HD, block, zero), jnp.where(lane < HD, zero, block))


def quarter_place(bit):
    d = lax.axis_index("dp")
    return 2 * ((d >> bit) % 2) + d % 2


def place_quarters(pieces, dest_ref, axis, bit):
    place = quarter_place(bit)
    for i, piece in enumerate(pieces):
        size = piece.shape[axis]
        spot = pl.ds(pl.multiple_of((place ^ i) * size, size), size)
        if axis == 0:
            dest_ref[spot, :] = piece[...]
        else:
            dest_ref[:, spot, :] = piece[...]


def attend_forward(which, width, x_ref, w_ref, vec_ref, seg_ref, code_ref, q_ref, k_ref, v_ref, o_ref, lse_ref, mask_ref):
    rows, hw = q_ref.shape
    block = 256
    fill_mask(seg_ref, code_ref, mask_ref)
    x = x_ref[...]
    for part, ref in enumerate((q_ref, k_ref, v_ref)):
        out = mm(x, w_ref[part])
        if part != 1:
            spot = pl.multiple_of((part // 2) * width + which * hw, 128)
            out = out + vec_ref[:, pl.ds(spot, hw)]
        ref[...] = out.astype(BF16)
    lane = lax.broadcasted_iota(jnp.int32, (block, 128), 1)
    lse_ref[...] = jnp.zeros_like(lse_ref)

    def one(step, carry):
        pair = step // (rows // block)
        start = pl.multiple_of((step % (rows // block)) * block, block)
        cols = pl.ds(pl.multiple_of(pair * 128, 128), 128)
        here = pl.ds(start, block)
        q = q_ref[here, cols]
        keys = split_pair(k_ref[:, cols])
        values = split_pair(v_ref[:, cols])
        mask = mask_ref[here, :]
        total = jnp.zeros((block, 128), F32)
        lse = lse_ref[here, :]
        for head in range(2):
            scores = mm(q, keys[head], NT) * SCALE2 + mask
            highest = jnp.max(scores, axis=1, keepdims=True)
            weights = jnp.exp2(scores - highest)
            sums = jnp.sum(weights, axis=1, keepdims=True)
            probs = (weights * (1.0 / sums)).astype(BF16)
            total = total + mm(probs, values[head])
            lse = jnp.where(lane == 2 * pair + head, highest + jnp.log2(sums), lse)
        o_ref[here, cols] = total.astype(BF16)
        lse_ref[here, :] = lse
        return carry

    lax.fori_loop(0, (hw // 128) * (rows // block), one, 0)


def attend_forward_own_kernel(
    tok_ref, got_ref, info_ref, w_ref, vec_ref, seg_ref, code_ref, x_ref, q_ref, k_ref, v_ref, o_ref, lse_ref, mask_ref
):
    exchange_rows(info_ref, tok_ref, got_ref, x_ref)
    which = lax.axis_index("mp")
    attend_forward(
        which, x_ref.shape[1], x_ref, w_ref, vec_ref, seg_ref, code_ref, q_ref, k_ref, v_ref, o_ref, lse_ref, mask_ref
    )


def attend_forward_other_kernel(
    x_ref, wa_ref, wb_ref, wc_ref, wd_ref, vec_ref, seg_ref, code_ref, q_ref, k_ref, v_ref, o_ref, lse_ref, w_ref, mask_ref
):
    place_quarters((wa_ref, wb_ref, wc_ref, wd_ref), w_ref, 1, 1)
    which = 1 - lax.axis_index("mp")
    attend_forward(
        which, x_ref.shape[1], x_ref, w_ref, vec_ref, seg_ref, code_ref, q_ref, k_ref, v_ref, o_ref, lse_ref, mask_ref
    )


def emit(value, index, keep_ref, send_ref, where):
    parity = lax.axis_index("dp") % 2
    for j in range(len(value) // 2):
        even, odd = value[2 * j], value[2 * j + 1]
        keep_ref[(index + j,) + where] = jnp.where(parity == 0, even, odd)
        send_ref[(index + j,) + where] = jnp.where(parity == 0, odd, even)


def attend_backward_kernel(q_ref, k_ref, v_ref, do_ref, lse_ref, seg_ref, code_ref, dq_ref, dk_ref, dv_ref, mask_ref):
    rows, hw = q_ref.shape
    block = 256
    fill_mask(seg_ref, code_ref, mask_ref)
    dk_ref[...] = jnp.zeros_like(dk_ref)
    dv_ref[...] = jnp.zeros_like(dv_ref)
    lane = lax.broadcasted_iota(jnp.int32, (block, 128), 1)

    def one(step, carry):
        pair = step // (rows // block)
        start = pl.multiple_of((step % (rows // block)) * block, block)
        cols = pl.ds(pl.multiple_of(pair * 128, 128), 128)
        here = pl.ds(start, block)
        q = q_ref[here, cols]
        grad = do_ref[here, cols]
        keys = split_pair(k_ref[:, cols])
        values = split_pair(v_ref[:, cols])
        queries = split_pair(q)
        grads = split_pair(grad)
        mask = mask_ref[here, :]
        lse_all = lse_ref[here, :]
        dq = jnp.zeros((block, 128), F32)
        dk = dk_ref[:, cols]
        dv = dv_ref[:, cols]
        for head in range(2):
            scores = mm(q, keys[head], NT) * SCALE2 + mask
            lse = jnp.sum(jnp.where(lane == 2 * pair + head, lse_all, 0.0), axis=1, keepdims=True)
            probs = jnp.exp2(scores - lse)
            gprobs = mm(grad, values[head], NT)
            weighted = probs * gprobs
            delta = jnp.sum(weighted, axis=1, keepdims=True)
            gscores = ((weighted - probs * delta) * SCORE_SCALE).astype(BF16)
            dq = dq + mm(gscores, keys[head])
            dk = dk + mm(gscores, queries[head], TN)
            dv = dv + mm(probs.astype(BF16), grads[head], TN)
        dq_ref[here, cols] = dq
        dk_ref[:, cols] = dk
        dv_ref[:, cols] = dv
        return carry

    lax.fori_loop(0, (hw // 128) * (rows // block), one, 0)


def project_backward_kernel(
    split, side, x_ref, w_ref, dq_ref, dk_ref, dv_ref, base_ref, sums_in_ref, info_ref, layer_ref, *rest
):
    if split:
        gout_refs, rest = rest[:2], rest[2:]
    outs = 2 if split else 1
    gin_refs = rest[:outs]
    tg_ref, back_ref, sums_ref = rest[outs:]
    hw = dq_ref.shape[1]
    width = x_ref.shape[1]
    half = back_ref.shape[1]
    if split:
        for dest, source in zip(gin_refs, gout_refs):
            for j in range(dest.shape[0]):
                dest[j, 3] = source[j]
    sums_ref[...] = sums_in_ref[...]
    m = lax.axis_index("mp")
    which = m if side == 0 else 1 - m
    x = x_ref[...]
    total = base_ref[...]
    for part, ref in enumerate((dq_ref, dk_ref, dv_ref)):
        grad = ref[...]
        if part != 1:
            spot = pl.multiple_of((part // 2) * width + which * hw, 128)
            sums_ref[:, pl.ds(spot, hw)] = jnp.sum(grad, axis=0, keepdims=True)
        grad_low = grad.astype(BF16)
        gin = mm(x, grad_low, TN).astype(BF16)
        if split:
            keep_ref, send_ref = gin_refs
            size = keep_ref.shape[2]
            emit([gin[i * size : (i + 1) * size] for i in range(width // size)], 0, keep_ref, send_ref, (part,))
        else:
            gin_refs[0][part] = gin
        total = total + mm(grad_low, w_ref[part], NT)
    tg_ref[...] = total.astype(tg_ref.dtype)
    if side == 0:
        window = pl.ds(pl.multiple_of(info_ref[1], half), half)
        back_ref[0] = layer_ref[window, :]
        back_ref[1] = tg_ref[window, :]
    else:
        back_ref[...] = jnp.zeros_like(back_ref)


def norm_stats(hidden):
    mean = jnp.mean(hidden, axis=1, keepdims=True)
    centred = hidden - mean
    inverse = lax.rsqrt(jnp.mean(centred * centred, axis=1, keepdims=True) + NORM_EPS)
    return centred * inverse, inverse


def out_norm_kernel(tok_ref, oa_ref, ob_ref, wo_ref, wa_ref, wb_ref, wc_ref, wd_ref, vec_ref, unit_ref, inv_ref, low_ref, w_ref):
    width = tok_ref.shape[1]
    place_quarters((wa_ref, wb_ref, wc_ref, wd_ref), w_ref, 0, 2)
    hidden = tok_ref[...].astype(F32) + (mm(oa_ref[...], wo_ref[...]) + mm(ob_ref[...], w_ref[...]))
    unit, inverse = norm_stats(hidden + vec_ref[:, 2 * width : 3 * width])
    unit_ref[...] = unit
    inv_ref[...] = inverse
    low_ref[...] = (unit * vec_ref[:, 4 * width : 5 * width] + vec_ref[:, 5 * width : 6 * width]).astype(BF16)


def gelu_parts(x):
    size = jnp.abs(x) * 0.7071067811865476
    bell = jnp.exp2(x * x * (-0.5 * LOG2E))
    t = 1.0 / (1.0 + 0.3275911 * size)
    poly = t * (
        0.254829592 + t * (-0.284496736 + t * (1.421413741 + t * (-1.453152027 + t * 1.061405429)))
    )
    tail = 0.5 * poly * bell
    below = jnp.where(x >= 0.0, 1.0 - tail, tail)
    return x * below, below + x * bell * 0.3989422804014327


def ffn_up(low, up, bias, act_ref, pull_ref, cols):
    upper = mm(low, up) + bias
    value, pull = gelu_parts(upper)
    act_ref[:, cols] = value.astype(BF16)
    pull_ref[:, cols] = pull


def ffn_own_kernel(low_ref, up_ref, down_ref, vec_ref, act_ref, pull_ref, total_ref):
    tile = 256
    width, fw = up_ref.shape
    low = low_ref[...]
    base = 8 * width + lax.axis_index("mp") * fw
    total_ref[...] = jnp.zeros_like(total_ref)

    def one(step, carry):
        cols = pl.ds(pl.multiple_of(step * tile, tile), tile)
        bias = vec_ref[:, pl.ds(pl.multiple_of(base + step * tile, tile), tile)]
        ffn_up(low, up_ref[:, cols], bias, act_ref, pull_ref, cols)
        total_ref[...] += mm(act_ref[:, cols], down_ref[cols, :])
        return carry

    lax.fori_loop(0, fw // tile, one, 0)


def ffn_other_kernel(low_ref, ua_ref, ub_ref, uc_ref, ud_ref, vec_ref, act_ref, pull_ref):
    width, tile = ua_ref.shape
    low = low_ref[...]
    place = quarter_place(1)
    base = 8 * width + (1 - lax.axis_index("mp")) * 4 * tile
    for i, up_ref in enumerate((ua_ref, ub_ref, uc_ref, ud_ref)):
        spot = (place ^ i) * tile
        bias = vec_ref[:, pl.ds(pl.multiple_of(base + spot, 128), tile)]
        ffn_up(low, up_ref[...], bias, act_ref, pull_ref, pl.ds(pl.multiple_of(spot, 128), tile))


def ffn_finish_kernel(
    act_ref,
    da_ref,
    db_ref,
    dc_ref,
    dd_ref,
    part_ref,
    unit_ref,
    vec_ref,
    cot_ref,
    got_ref,
    info_ref,
    out_ref,
    grad_ref,
    glow_ref,
    sums_ref,
    total_ref,
    cots_ref,
):
    width = part_ref.shape[1]
    half = got_ref.shape[0]
    tile = da_ref.shape[0]
    place = quarter_place(2)
    total_ref[...] = part_ref[...]
    for i, down_ref in enumerate((da_ref, db_ref, dc_ref, dd_ref)):
        spot = pl.multiple_of((place ^ i) * tile, 128)
        total_ref[...] += mm(act_ref[:, pl.ds(spot, tile)], down_ref[...])
    exchange_rows(info_ref, cot_ref, got_ref, cots_ref)
    normed = unit_ref[...] * vec_ref[:, 4 * width : 5 * width] + vec_ref[:, 5 * width : 6 * width]
    unit, inverse = norm_stats(normed + total_ref[...] + vec_ref[:, 3 * width : 4 * width])
    gain = vec_ref[:, 6 * width : 7 * width]
    out_ref[...] = (unit * gain + vec_ref[:, 7 * width : 8 * width]).astype(BF16)
    cot = cots_ref[...].astype(F32)
    sums_ref[...] = jnp.zeros_like(sums_ref)
    sums_ref[:, 6 * width : 7 * width] = jnp.sum(cot * unit, axis=0, keepdims=True)
    sums_ref[:, 7 * width : 8 * width] = jnp.sum(cot, axis=0, keepdims=True)
    scaled = cot * gain
    grad = inverse * (
        scaled
        - jnp.mean(scaled, axis=1, keepdims=True)
        - unit * jnp.mean(scaled * unit, axis=1, keepdims=True)
    )
    sums_ref[:, 3 * width : 4 * width] = jnp.sum(grad, axis=0, keepdims=True)
    grad_ref[...] = grad
    glow_ref[...] = grad.astype(BF16)


def ffn_backward_kernel(split, side, low_ref, glow_ref, act_ref, pull_ref, base_ref, sums_in_ref, *rest):
    pieces = 4 if side else 1
    up_refs, down_refs, rest = rest[:pieces], rest[pieces : 2 * pieces], rest[2 * pieces :]
    outs = 2 if split else 1
    gdown_refs, gup_refs, (gn_ref, sums_ref) = rest[:outs], rest[outs : 2 * outs], rest[2 * outs : 2 * outs + 2]
    rows, width = low_ref.shape
    fw = act_ref.shape[1]
    tile = 384
    low = low_ref[...]
    glow = glow_ref[...]
    gn_ref[...] = base_ref[...]
    sums_ref[...] = sums_in_ref[...]
    m = lax.axis_index("mp")
    base = 8 * width + (1 - m if side else m) * fw

    def down_part(number, down):
        spot = pl.multiple_of(number * tile, 128)
        cols = pl.ds(spot, tile)
        gdown = mm(act_ref[:, cols], glow, TN).astype(BF16)
        if split:
            keep_ref, send_ref = gdown_refs
            size = keep_ref.shape[1]
            per = tile // size
            emit([gdown[i * size : (i + 1) * size] for i in range(per)], number * (per // 2), keep_ref, send_ref, ())
        else:
            gdown_refs[0][cols, :] = gdown
        gupper = mm(glow, down, NT) * pull_ref[:, cols]
        sums_ref[:, pl.ds(pl.multiple_of(base + spot, 128), tile)] = jnp.sum(gupper, axis=0, keepdims=True)
        return gupper.astype(BF16)

    def up_part(number, gupper, up):
        cols = pl.ds(pl.multiple_of(number * tile, 128), tile)
        gup = mm(low, gupper, TN).astype(BF16)
        if split:
            keep_ref, send_ref = gup_refs
            size = keep_ref.shape[1] // 2
            shards = [gup[i * size : (i + 1) * size] for i in range(width // size)]
            under = pl.ds(pl.multiple_of((number // 2) * size, 16), size)
            beside = pl.ds(pl.multiple_of((number % 2) * tile, 128), tile)
            emit(shards, 0, keep_ref, send_ref, (under, beside))
        else:
            gup_refs[0][:, cols] = gup
        gn_ref[...] += mm(gupper, up, NT)

    if side:
        gupper_ref = rest[2 * outs + 2]
        for i in range(4):
            number = quarter_place(2) ^ i
            cols = pl.ds(pl.multiple_of(number * tile, 128), tile)
            gupper_ref[:, cols] = down_part(number, down_refs[i][...])
        for i in range(4):
            number = quarter_place(1) ^ i
            cols = pl.ds(pl.multiple_of(number * tile, 128), tile)
            up_part(number, gupper_ref[:, cols], up_refs[i][...])
    else:

        def step(number, carry):
            cols = pl.ds(pl.multiple_of(number * tile, 128), tile)
            up_part(number, down_part(number, down_refs[0][cols, :]), up_refs[0][:, cols])
            return carry

        lax.fori_loop(0, fw // tile, step, 0)


def norm_back_kernel(
    split,
    gn_ref,
    unit_ref,
    inv_ref,
    vec_ref,
    oa_ref,
    ob_ref,
    wa_ref,
    wb_ref,
    sums_in_ref,
    grad_ref,
    ga_ref,
    gb_ref,
    *rest,
):
    sums_ref = rest[-1]
    width = gn_ref.shape[1]
    gn = gn_ref[...]
    unit = unit_ref[...]
    sums_ref[...] = sums_in_ref[...]
    sums_ref[:, 4 * width : 5 * width] = jnp.sum(gn * unit, axis=0, keepdims=True)
    sums_ref[:, 5 * width : 6 * width] = jnp.sum(gn, axis=0, keepdims=True)
    scaled = gn * vec_ref[:, 4 * width : 5 * width]
    grad = inv_ref[...] * (
        scaled
        - jnp.mean(scaled, axis=1, keepdims=True)
        - unit * jnp.mean(scaled * unit, axis=1, keepdims=True)
    )
    sums_ref[:, 2 * width : 3 * width] = jnp.sum(grad, axis=0, keepdims=True)
    grad_ref[...] = grad
    low = grad.astype(BF16)
    ga_ref[...] = mm(low, wa_ref[...], NT).astype(BF16)
    gb_ref[...] = mm(low, wb_ref[...], NT).astype(BF16)
    for i, o_ref in enumerate((oa_ref, ob_ref)):
        gout = mm(o_ref[...], low, TN)
        if split:
            keep_ref, send_ref = rest[2 * i], rest[2 * i + 1]
            size = keep_ref.shape[1] // 2
            shards = []
            for j in range(gout.shape[0] // size):
                rows = gout[j * size : (j + 1) * size]
                shards.append(jnp.concatenate([rows[:, : width // 2], rows[:, width // 2 :]], axis=0).astype(BF16))
            emit(shards, 0, keep_ref, send_ref, ())
        else:
            rest[i][...] = gout.astype(BF16)


def combine_kernel(plans, *refs):
    total = sum(terms for pieces, _, _, _ in plans for terms, _ in pieces)
    ins, outs = refs[:total], refs[total:]
    for pieces, bit, where, count in plans:
        dests, outs = outs[:count], outs[count:]
        row = 0
        for terms, lanes in pieces:
            here, ins = ins[:terms], ins[terms:]
            for j in range(dests[0].shape[0]):
                for number, dest in enumerate(dests):
                    spot = j
                    if count == 2:
                        odd = (lax.axis_index("dp") >> bit) % 2
                        side = odd if number == 0 else 1 - odd
                        spot = ((j >> where) << (where + 1)) + (side << where) + (j & ((1 << where) - 1))

                    def read(term):
                        cut = lanes is not None and term.shape[-1] > lanes[1]
                        part = term[spot, :, lanes[0] : lanes[0] + lanes[1]] if cut else term[spot]
                        return part.astype(F32)

                    value = read(here[0])
                    for term in here[1:]:
                        value = value + read(term)
                    value = value.astype(dest.dtype)
                    if len(pieces) == 1:
                        dest[j] = value
                    else:
                        size = value.shape[0]
                        if size % 16 == 8:
                            value = jnp.concatenate([value, jnp.zeros_like(value[:8])], axis=0)
                        dest[j, row : row + value.shape[0], :] = value
            row += -(-here[0].shape[1] // 16) * 16


def unswap_kernel(layer_ref, grad_ref, got_ref, info_ref, layer_out_ref, grad_out_ref):
    exchange_rows(info_ref, layer_ref, got_ref.at[0], layer_out_ref)
    exchange_rows(info_ref, grad_ref, got_ref.at[1], grad_out_ref)


def flip(values, axis, bit, count):
    pairs = [(i, i ^ (1 << bit)) for i in range(count)]
    return lax.ppermute(values, axis, pairs)


def halve(values, bit):
    split = values.reshape((values.shape[0] // 2, 2) + values.shape[1:])
    keep = lax.dynamic_index_in_dim(split, bit, 1, keepdims=False)
    send = lax.dynamic_index_in_dim(split, 1 - bit, 1, keepdims=False)
    return keep, send


def body(
    tokens,
    cotangent,
    segment_ids,
    key_keep,
    in_weight,
    out_weight,
    up_weight,
    down_weight,
    in_master,
    out_master,
    up_master,
    down_master,
    in_first,
    out_first,
    up_first,
    down_first,
    in_second,
    out_second,
    up_second,
    down_second,
    vector_master,
    vector_first,
    vector_second,
):
    rows, width = tokens.shape
    d = lax.axis_index("dp")
    dp_count = lax.axis_size("dp")
    bits = dp_count.bit_length() - 1
    hw = in_weight.shape[2]
    fw = up_weight.shape[1]
    half = rows // 2
    smem = pltpu.SMEM
    length = vector_master.shape[0]
    vec = vector_master.reshape(1, length)
    in_own = jnp.transpose(in_weight, (1, 0, 2))
    split = (width // dp_count) % 16 == 0

    state = {"last": None}

    def run(kernel, outs, args, through=(), after=(), **options):
        before = () if state["last"] is None else (state["last"],)
        res = call(kernel, outs, args, after=tuple(after) + before, through=tuple(through), **options)
        state["last"] = res[-1] if through else res[0]
        return res

    s_tok, s_cot, s_in, s_out, s_up, s_down, seg, code, info = run(
        prepare_kernel,
        [
            ((half, width), BF16),
            ((half, width), BF16),
            ((3, width // 4, hw), BF16),
            ((hw // 4, width), BF16),
            ((width, fw // 4), BF16),
            ((fw // 4, width), BF16),
            ((rows, 1), jnp.int32),
            ((1, rows), jnp.int32),
            ((8,), jnp.int32),
        ],
        (tokens, cotangent, in_own, out_weight, up_weight, down_weight, segment_ids, key_keep),
        scratch=[pltpu.SemaphoreType.DMA((6,))],
        limit=60,
        name="prepare",
        us=2,
        places={i: pltpu.HBM for i in range(6)},
        out_places={8: smem},
    )

    def relay(arrays, name, after=()):
        return run(lambda *refs: None, [], (), through=arrays, after=after, limit=4, name=name)

    def x_hop(values):
        return flip(values, "mp", 0, 2)

    def dp_hop(values, bit):
        return flip(values, "dp", bit, dp_count)

    def xz_hop(values):
        pairs = [(i, i ^ 9) for i in range(2 * dp_count)]
        return lax.ppermute(values, ("dp", "mp"), pairs)

    attn_flops = 2 * rows * width * 3 * hw + 4 * rows * rows * hw * 4
    wide = (rows, width)
    narrow = (rows, hw)
    hidden = (rows, fw)
    ffn_flops = 4 * rows * width * fw
    line = (1, length)
    attend_outs = [(narrow, BF16)] * 4 + [((rows, 128), F32)]
    square = pltpu.VMEM((rows, rows), F32)

    got_tok = x_hop(s_tok)
    in_0 = x_hop(s_in)
    out_0 = x_hop(s_out)
    x, q_a, k_a, v_a, o_a, lse_a, s_up, s_down, s_cot = run(
        attend_forward_own_kernel,
        [(wide, BF16)] + attend_outs,
        (tokens, got_tok, info, in_own, vec, seg, code),
        through=(s_up, s_down, s_cot),
        scratch=[square],
        name="attend_forward_own",
        us=6,
        places={2: smem},
    )
    up_0 = x_hop(s_up)
    in_0, out_0, s_down = relay((in_0, out_0, s_down), "relay_one")
    in_2 = dp_hop(in_0, 1)
    out_2 = dp_hop(out_0, 2)
    in_1 = dp_hop(in_0, 0)
    down_0 = x_hop(s_down)
    in_2, out_2, up_0, out_0 = relay((in_2, out_2, up_0, out_0), "relay_two")
    in_3 = dp_hop(in_2, 0)
    up_2 = dp_hop(up_0, 1)
    q_b, k_b, v_b, o_b, lse_b, in_other, up_0, s_cot, out_0, out_2 = run(
        attend_forward_other_kernel,
        attend_outs + [((3, width, hw), BF16)],
        (x, in_0, in_1, in_2, in_3, vec, seg, code),
        through=(up_0, s_cot, out_0, out_2),
        scratch=[square],
        name="attend_forward_other",
        us=6,
    )
    down_0, s_cot = relay((down_0, s_cot), "relay_three")
    out_1 = dp_hop(out_0, 0)
    out_3 = dp_hop(out_2, 0)
    down_2 = dp_hop(down_0, 2)
    got_cot = x_hop(s_cot)
    unit, inverse, low, out_other = run(
        out_norm_kernel,
        [(wide, F32), ((rows, 1), F32), (wide, BF16), ((hw, width), BF16)],
        (x, o_a, o_b, out_weight, out_0, out_1, out_2, out_3, vec),
        name="out_norm",
        us=1.5,
    )
    act_a, pull_a, part = run(
        ffn_own_kernel,
        [(hidden, BF16), (hidden, F32), (wide, F32)],
        (low, up_weight, down_weight, vec),
        name="ffn_own",
        us=8,
    )
    up_2, down_0, up_0, got_cot = relay((up_2, down_0, up_0, got_cot), "relay_four")
    up_1 = dp_hop(up_0, 0)
    up_3 = dp_hop(up_2, 0)
    down_1 = dp_hop(down_0, 0)
    act_b, pull_b = run(
        ffn_other_kernel,
        [(hidden, BF16), (hidden, F32)],
        (low, up_0, up_1, up_2, up_3, vec),
        name="ffn_other",
        us=5,
    )
    (down_2,) = relay((down_2,), "relay_five")
    down_3 = dp_hop(down_2, 0)
    ups = (up_0, up_1, up_2, up_3)
    downs = (down_0, down_1, down_2, down_3)
    out_work, grad_two, glow, sums = run(
        ffn_finish_kernel,
        [(wide, BF16), (wide, F32), (wide, BF16), (line, F32)],
        (act_b, *downs, part, unit, vec, cotangent, got_cot, info),
        scratch=[pltpu.VMEM(wide, F32), pltpu.VMEM(wide, BF16)],
        name="ffn_finish",
        us=5,
        places={10: smem},
    )

    count = dp_count // 2
    down_shape = (fw // dp_count, width)
    up_shape = (2 * (width // dp_count), fw // 2)
    in_shape = (4, width // dp_count, hw)
    out_shape = (2 * (hw // dp_count), width // 2)

    def parts(shape):
        return [((count,) + shape, BF16)] * 2

    def ffn_back(side, act, pull, ups, downs, base, sums, name, after=()):
        kinds = parts(down_shape) + parts(up_shape) if split else [((fw, width), BF16), ((width, fw), BF16)]
        res = run(
            functools.partial(ffn_backward_kernel, split, side),
            kinds + [(wide, F32), (line, F32)],
            (low, glow, act, pull, base, sums, *ups, *downs),
            scratch=[pltpu.VMEM(hidden, BF16)] if side else [],
            name=name,
            us=10.5,
            after=after,
        )
        gn, sums = res[-2:]
        if split:
            return tuple(res[0:2]), tuple(res[2:4]), gn, sums
        down = halve(res[0].reshape((dp_count,) + down_shape), d & 1)
        up = jnp.transpose(res[1].reshape(dp_count, width // dp_count, 2, fw // 2), (0, 2, 1, 3))
        up = halve(up.reshape((dp_count,) + up_shape), d & 1)
        return down, up, gn, sums

    def pieces_of(terms):
        return terms if isinstance(terms, list) else [(terms, None)]

    def shape_of(pieces):
        rows = [t[0].shape[1] for t, _ in pieces]
        shape = pieces[0][0][0].shape
        if len(pieces) > 1:
            return (shape[0], sum(-(-r // 16) * 16 for r in rows), shape[2])
        lanes = pieces[0][1]
        return shape if lanes is None else shape[:2] + (lanes[1],)

    def halves(terms, bit, where=0, kinds=(F32, BF16)):
        pieces = pieces_of(terms)
        shape = shape_of(pieces)
        shape = (shape[0] // 2,) + shape[1:]
        return (pieces, bit, where, [(shape, kind) for kind in kinds])

    def whole(terms, kind=BF16):
        pieces = pieces_of(terms)
        return (pieces, None, 0, [(shape_of(pieces), kind)])

    def combine(name, tensors, through=(), after=()):
        plans = tuple(
            (tuple((len(t), lanes) for t, lanes in pieces), bit, where, len(o)) for pieces, bit, where, o in tensors
        )
        res = run(
            functools.partial(combine_kernel, plans),
            [o for t in tensors for o in t[3]],
            [v for pieces, _, _, _ in tensors for t, _ in pieces for v in t],
            name=name,
            through=through,
            after=after,
        )
        res = list(res)
        made = []
        for t in tensors:
            made.append(tuple(res[: len(t[3])]) if len(t[3]) == 2 else res[0])
            res = res[len(t[3]) :]
        return made + res

    down_b, up_b, gn, sums = ffn_back(1, act_b, pull_b, ups, downs, grad_two, sums, "ffn_backward_other")
    core_down_b = dp_hop(down_b[1], 0)
    core_up_b = dp_hop(up_b[1], 0)
    down_a, up_a, gn, sums = ffn_back(
        0, act_a, pull_a, (up_weight,), (down_weight,), gn, sums, "ffn_backward_own"
    )
    core_down_a = dp_hop(down_a[1], 0)
    core_up_a = dp_hop(up_a[1], 0)
    sum_down_b, (up_b_keep, up_b_send) = combine(
        "combine_ffn_other", [whole((down_b[0], core_down_b)), halves((up_b[0], core_up_b), 1)]
    )
    x_down = x_hop(sum_down_b)
    y_up_b = dp_hop(up_b_send, 1)

    kinds = parts(out_shape) * 2 if split else [((hw, width), BF16)] * 2
    grad_one, gatt_a, gatt_b, *gout, sums = run(
        functools.partial(norm_back_kernel, split),
        [(wide, F32), (narrow, BF16), (narrow, BF16)] + kinds + [(line, F32)],
        (gn, unit, inverse, vec, o_a, o_b, out_weight, out_other, sums),
        name="norm_back",
        us=2.5,
    )
    ((up_a_keep, up_a_send),) = combine("combine_up_own", [halves((up_a[0], core_up_a), 1)], after=(core_down_a,))
    y_up_a = dp_hop(up_a_send, 1)

    def attend_back(q, k, v, gatt, lse, name):
        return run(
            attend_backward_kernel,
            [(narrow, F32)] * 3,
            (q, k, v, gatt, lse, seg, code),
            scratch=[square],
            name=name,
            us=9,
        )

    def project_back(side, w, grads, base, kind, sums, gout, name, after=()):
        kinds = parts(in_shape) if split else [((3, width, hw), BF16)]
        res = run(
            functools.partial(project_backward_kernel, split, side),
            kinds + [(wide, kind), ((2, half, width), BF16), (line, F32)],
            (x, w, *grads, base, sums, info, out_work) + (tuple(gout) if split else ()),
            name=name,
            us=3,
            after=after,
            places={7: smem},
        )
        tg, back, sums = res[-3:]
        if split:
            return tuple(res[0:2]), tg, back, sums
        part = (dp_count, width // dp_count, hw)
        gout = jnp.transpose(gout[0].reshape(dp_count, hw // dp_count, 2, width // 2), (0, 2, 1, 3)).reshape(part)
        grads = jnp.concatenate([res[0].reshape((3,) + part), gout[None]])
        return halve(jnp.transpose(grads, (1, 0, 2, 3)), d & 1), tg, back, sums

    grads_b = attend_back(q_b, k_b, v_b, gatt_b, lse_b, "attend_backward_other")
    (sum_up_b,) = combine("combine_up_x", [whole((up_b_keep, y_up_b))])
    x_up = x_hop(sum_up_b)
    grads_a = attend_back(q_a, k_a, v_a, gatt_a, lse_a, "attend_backward_own")
    gout_a, gout_b = (gout[:2], gout[2:]) if split else (gout[:1], gout[1:])
    in_b, tg, _, sums = project_back(1, in_other, grads_b, grad_one, F32, sums, gout_b, "project_backward_other")
    core_in_b = dp_hop(in_b[1], 0)
    ((down_keep, down_send),) = combine(
        "combine_down", [halves((down_a[0], core_down_a, x_down), 1)], after=(y_up_a, x_up)
    )
    y_down = dp_hop(down_send, 1)
    in_a, tg, back, sums = project_back(0, in_own, grads_a, tg, BF16, sums, gout_a, "project_backward_own")
    core_in_a = dp_hop(in_a[1], 0)
    sums = sums.reshape(1, length // 128, 128)
    core_sums = dp_hop(sums, 0)

    (in_keep, in_z), (in_x, in_xz), sums = combine(
        "tail_core",
        [
            halves((in_a[0], core_in_a), 2, 1),
            halves((in_b[0], core_in_b), 2, 1, kinds=(BF16, BF16)),
            whole((sums, core_sums), F32),
        ],
    )
    in_terms = [in_keep, dp_hop(in_z, 2), x_hop(in_x), xz_hop(in_xz)]
    big = [((down_keep, y_down), None), ((up_a_keep, y_up_a, x_up), None)]
    big_t, back, sums = combine("tail_z", [halves(big, 2)], through=(back, sums))
    big = [big_t[0], dp_hop(big_t[1], 2)]
    sum_terms = [sums, dp_hop(sums, 1)]
    sum_hops = ["x"] + list(range(2, bits))

    def more(name, tensor, through=()):
        made = combine(name, [tensor] + ([whole(tuple(sum_terms), F32)] if len(sum_terms) > 1 else []), through=through)
        if len(sum_terms) > 1:
            sum_terms[:] = [made.pop(1)]
        if sum_hops:
            hop = sum_hops.pop(0)
            sum_terms.append(x_hop(sum_terms[0]) if hop == "x" else dp_hop(sum_terms[0], hop))
        return made

    in_t, back = more("tail_in", halves(tuple(in_terms), 1), (back,))
    in_terms = [in_t[0], dp_hop(in_t[1], 1)]
    got_back = x_hop(back)
    for bit in range(3, bits):
        (in_t,) = more("tail_in_more", halves(tuple(in_terms), bit))
        in_terms = [in_t[0], dp_hop(in_t[1], bit)]
        (big_t,) = more("tail_more", halves(tuple(big), bit))
        big = [big_t[0], dp_hop(big_t[1], bit)]
    layer_out, token_grad = run(
        unswap_kernel, [(wide, BF16)] * 2, (out_work, tg, got_back, info), name="unswap", places={3: smem}
    )

    def total(pair):
        keep, got = pair
        return (keep.astype(F32) + got.astype(F32)).reshape(keep.shape[1:])

    spot = 0
    grads = []
    for shape in (down_shape, up_shape):
        cut = tuple(v[:, spot : spot + shape[0]] for v in big)
        grads.append(total(cut))
        spot += -(-shape[0] // 16) * 16
    grad_down, grad_up = grads
    size = width // dp_count
    grad_up = jnp.concatenate([grad_up[:size], grad_up[size:]], axis=1)
    grad_in = total(in_terms)
    size = hw // dp_count
    grad_out = jnp.concatenate([grad_in[3, :size], grad_in[3, size:]], axis=1)
    grad_in = jnp.transpose(grad_in[:3], (1, 0, 2))
    grad_vector = sum(sum_terms).reshape(length)

    def matrix_step(grad, master, first, second):
        f, s, n = adam_step(grad, master, first, second, MATRIX_RATE, WEIGHT_DECAY)
        return (f, s, n, n.astype(BF16))

    return (
        layer_out,
        token_grad,
        *matrix_step(grad_in, in_master, in_first, in_second),
        *matrix_step(grad_out, out_master, out_first, out_second),
        *matrix_step(grad_up, up_master, up_first, up_second),
        *matrix_step(grad_down, down_master, down_first, down_second),
        *adam_step(grad_vector, vector_master, vector_first, vector_second, VECTOR_RATE, 0.0),
    )


def solution(mesh):
    tok = P(("dp", "mp"), None)
    line = P("dp", None)
    in_state = P("dp", None, "mp")
    out_state = P(("mp", "dp"), None)
    up_state = P("dp", "mp")
    states = (in_state, out_state, up_state, out_state)
    in_specs = (
        (tok, tok, line, line, P(None, None, "mp"), P("mp", None), P(None, "mp"), P("mp", None))
        + states * 3
        + (P(), P(), P())
    )
    out_specs = (
        (tok, tok)
        + (in_state,) * 4
        + (out_state,) * 4
        + (up_state,) * 4
        + (out_state,) * 4
        + (P(), P(), P())
    )
    return jax.shard_map(body, mesh=mesh, in_specs=in_specs, out_specs=out_specs, check_vma=False)
```

```python
import functools
import math

import jax
import jax.numpy as jnp
from jax import lax
from jax.experimental import pallas as pl
from jax.experimental.pallas import tpu as pltpu
from jax.sharding import PartitionSpec as P

HD = 64
STEP = 7
NORM_EPS = 1e-06
SCORE_SCALE = 0.125
NEG_FILL = -1e30
MOMENT_DECAY = 0.5
SQUARE_DECAY = 0.5
MATRIX_RATE = 0.03
VECTOR_RATE = 0.2
WEIGHT_DECAY = 0.01
ADAM_EPS = 1e-08
LOG2E = 1.4426950408889634
SCALE2 = SCORE_SCALE * LOG2E
F32 = jnp.float32
BF16 = jnp.bfloat16
MIB = 1024 * 1024
WORK = 1e6
SLACK = 8
OWN_LIMIT = 60

NN = (((1,), (0,)), ((), ()))
NT = (((1,), (1,)), ((), ()))
TN = (((0,), (0,)), ((), ()))


def mm(a, b, dims=NN):
    return lax.dot_general(a, b, dims, preferred_element_type=F32)


def padded_bytes(shape, dtype):
    rows = shape[-2] if len(shape) > 1 else 1
    tiles = -(-rows // 8) * 8 * -(-shape[-1] // 128) * 128
    return math.prod(shape[:-2]) * tiles * jnp.dtype(dtype).itemsize


def call(kernel, outs, args, scratch=(), limit=None, name=None, after=(), through=(), places=None, out_places=None, us=1):
    count = len(args)
    places = places or {}
    out_places = out_places or {}
    anywhere = pl.BlockSpec(memory_space=pl.ANY)
    specs = [pl.BlockSpec(memory_space=places.get(i, pltpu.VMEM)) for i in range(count)]
    specs += [anywhere] * (len(through) + len(after))
    made = len(outs)
    if limit is None:
        held = [v for i, v in enumerate(args) if places.get(i, pltpu.VMEM) == pltpu.VMEM]
        held = [(v.shape, v.dtype) for v in held] + [v for i, v in enumerate(outs) if i not in out_places]
        held += [(v.shape, v.dtype) for v in scratch if v.memory_space == pltpu.VMEM]
        limit = sum(padded_bytes(*v) for v in held) // MIB + SLACK

    def run(*refs):
        own = refs[count + len(through) + len(after) :]
        kernel(*refs[:count], *own[:made], *own[made + len(through) :])

    return pl.pallas_call(
        run,
        out_shape=[jax.ShapeDtypeStruct(s, d) for s, d in outs]
        + [jax.ShapeDtypeStruct(v.shape, v.dtype) for v in through],
        in_specs=specs,
        out_specs=[pl.BlockSpec(memory_space=out_places.get(i, pltpu.VMEM)) for i in range(made)] + [anywhere] * len(through),
        scratch_shapes=list(scratch),
        input_output_aliases={count + i: made + i for i in range(len(through))},
        compiler_params=pltpu.CompilerParams(vmem_limit_bytes=limit * MIB),
        cost_estimate=pl.CostEstimate(flops=int(us * WORK), bytes_accessed=0, transcendentals=0),
        name=name,
    )(*args, *through, *after)


def adam_step(grad, master, first, second, rate, decay):
    first_next = MOMENT_DECAY * first + (1.0 - MOMENT_DECAY) * grad
    second_next = SQUARE_DECAY * second + (1.0 - SQUARE_DECAY) * grad * grad
    first_fix = 1.0 - MOMENT_DECAY**STEP
    second_fix = 1.0 - SQUARE_DECAY**STEP
    update = first_next / first_fix / (jnp.sqrt(second_next / second_fix) + ADAM_EPS)
    master_next = master - rate * (update + decay * master)
    return (first_next, second_next, master_next)


def prepare_kernel(
    tok_ref,
    cot_ref,
    in_ref,
    out_ref,
    up_ref,
    down_ref,
    seg_ref,
    keep_ref,
    stok_ref,
    scot_ref,
    sin_ref,
    sout_ref,
    sup_ref,
    sdown_ref,
    segrow_ref,
    code_ref,
    info_ref,
    sems,
):
    rows = tok_ref.shape[0]
    half = rows // 2
    m = lax.axis_index("mp")
    copies = []
    for i, (source, dest, axis, bit) in enumerate(
        ((in_ref, sin_ref, 1, 1), (out_ref, sout_ref, 0, 2), (down_ref, sdown_ref, 0, 2), (up_ref, sup_ref, 1, 1))
    ):
        size = dest.shape[axis]
        spot = pl.ds(pl.multiple_of(quarter_place(bit) * size, size), size)
        view = source.at[spot] if axis == 0 else source.at[:, spot]
        copies.append(pltpu.make_async_copy(view, dest, sems.at[i]))
    for copy in copies:
        copy.start()
    seg = seg_ref[...]
    spot = lax.broadcasted_iota(jnp.int32, seg.shape, 1)
    later = jnp.roll(seg, rows + 1, axis=1)
    begin = jnp.sum(jnp.where((seg == later) & (spot <= rows), spot, 0))
    late = begin > half
    first = jnp.where(late, half, 0)
    info_ref[0] = begin
    info_ref[1] = first
    window = pl.ds(pl.multiple_of(first, half), half)
    for i, (source, dest) in enumerate(((tok_ref, stok_ref), (cot_ref, scot_ref))):
        copy = pltpu.make_async_copy(source.at[window], dest, sems.at[4 + i])
        copy.start()
        copies.append(copy)
    own = pl.ds(pl.multiple_of(m * rows, rows), rows)
    other = pl.ds(pl.multiple_of((1 - m) * rows, rows), rows)
    local = lax.broadcasted_iota(jnp.int32, (1, rows), 1)
    swapped = jnp.where(late, local - begin, begin - 1 - local) >= 0
    mine = jnp.where(swapped, seg_ref[:, other], seg_ref[:, own])
    kept = jnp.where(swapped, keep_ref[:, other], keep_ref[:, own])
    segrow_ref[...] = mine
    code = jnp.where(kept == 1, mine, -1)
    code_ref[...] = jnp.broadcast_to(code.astype(F32), (8, rows)).T[:, 0:1].astype(jnp.int32)
    for copy in copies:
        copy.wait()


def swapped_rows(info_ref, shape):
    begin = info_ref[0]
    first = info_ref[1]
    local = first + lax.broadcasted_iota(jnp.int32, shape, 0)
    return jnp.where(first > 0, local - begin, begin - 1 - local) >= 0


def exchange_rows(info_ref, source_ref, got_ref, dest_ref):
    half = got_ref.shape[0]
    window = pl.ds(pl.multiple_of(info_ref[1], half), half)
    dest_ref[...] = source_ref[...]
    dest_ref[window, :] = jnp.where(swapped_rows(info_ref, got_ref.shape), got_ref[...], source_ref[window, :])


def fill_mask(seg_ref, code_ref, mask_ref):
    rows = mask_ref.shape[0]
    row = lax.broadcasted_iota(jnp.int32, (rows, rows), 0)
    col = lax.broadcasted_iota(jnp.int32, (rows, rows), 1)
    allowed = (code_ref[...] == seg_ref[...]) | (row == col)
    mask_ref[...] = jnp.where(allowed, 0.0, NEG_FILL)


def split_pair(block):
    lane = lax.broadcasted_iota(jnp.int32, block.shape, 1)
    zero = jnp.zeros_like(block)
    return (jnp.where(lane < HD, block, zero), jnp.where(lane < HD, zero, block))


def quarter_place(bit):
    d = lax.axis_index("dp")
    return 2 * ((d >> bit) % 2) + d % 2


def place_quarters(pieces, dest_ref, axis, bit):
    place = quarter_place(bit)
    for i, piece in enumerate(pieces):
        size = piece.shape[axis]
        spot = pl.ds(pl.multiple_of((place ^ i) * size, size), size)
        if axis == 0:
            dest_ref[spot, :] = piece[...]
        else:
            dest_ref[:, spot, :] = piece[...]


def attend_forward(which, width, x_ref, w_ref, vec_ref, seg_ref, code_ref, q_ref, k_ref, v_ref, o_ref, lse_ref, mask_ref):
    rows, hw = q_ref.shape
    fill_mask(seg_ref, code_ref, mask_ref)
    x = x_ref[...]
    for part, ref in enumerate((q_ref, k_ref, v_ref)):
        out = mm(x, w_ref[part])
        if part != 1:
            spot = pl.multiple_of((part // 2) * width + which * hw, 128)
            out = out + vec_ref[:, pl.ds(spot, hw)]
        ref[...] = out.astype(BF16)
    lse_ref[...] = jnp.zeros_like(lse_ref)
    for pair in range(hw // 128):
        cols = slice(pair * 128, (pair + 1) * 128)
        q = q_ref[:, cols]
        keys = split_pair(k_ref[:, cols])
        values = split_pair(v_ref[:, cols])
        mask = mask_ref[...]
        total = jnp.zeros((128, rows), F32)
        for head in range(2):
            scores = mm(keys[head], q, NT) * SCALE2 + mask
            highest = jnp.max(scores, axis=0, keepdims=True)
            weights = jnp.exp2(scores - highest)
            sums = jnp.sum(weights, axis=0, keepdims=True)
            probs = (weights * (1.0 / sums)).astype(BF16)
            total = total + mm(turned(values[head]), probs)
            lse_ref[2 * pair + head : 2 * pair + head + 1, :] = highest + jnp.log2(sums)
        o_ref[:, cols] = total.T.astype(BF16)


def attend_forward_own_kernel(
    tok_ref, got_ref, info_ref, w_ref, vec_ref, seg_ref, code_ref, x_ref, q_ref, k_ref, v_ref, o_ref, lse_ref, mask_ref
):
    exchange_rows(info_ref, tok_ref, got_ref, x_ref)
    which = lax.axis_index("mp")
    attend_forward(
        which, x_ref.shape[1], x_ref, w_ref, vec_ref, seg_ref, code_ref, q_ref, k_ref, v_ref, o_ref, lse_ref, mask_ref
    )


def attend_forward_other_kernel(
    x_ref, wa_ref, wb_ref, wc_ref, wd_ref, vec_ref, seg_ref, code_ref, q_ref, k_ref, v_ref, o_ref, lse_ref, w_ref, mask_ref
):
    place_quarters((wa_ref, wb_ref, wc_ref, wd_ref), w_ref, 1, 1)
    which = 1 - lax.axis_index("mp")
    attend_forward(
        which, x_ref.shape[1], x_ref, w_ref, vec_ref, seg_ref, code_ref, q_ref, k_ref, v_ref, o_ref, lse_ref, mask_ref
    )


def emit(value, index, keep_ref, send_ref, where):
    parity = lax.axis_index("dp") % 2
    for j in range(len(value) // 2):
        even, odd = value[2 * j], value[2 * j + 1]
        keep_ref[(index + j,) + where] = jnp.where(parity == 0, even, odd)
        send_ref[(index + j,) + where] = jnp.where(parity == 0, odd, even)


def turned(block):
    return block.astype(F32).T.astype(BF16)


def attend_backward_kernel(q_ref, k_ref, v_ref, do_ref, lse_ref, seg_ref, code_ref, dq_ref, dk_ref, dv_ref, mask_ref):
    rows, hw = q_ref.shape
    fill_mask(seg_ref, code_ref, mask_ref)
    for pair in range(hw // 128):
        cols = slice(pair * 128, (pair + 1) * 128)
        q = q_ref[:, cols]
        grad = do_ref[:, cols]
        keys = split_pair(k_ref[:, cols])
        values = split_pair(v_ref[:, cols])
        queries = split_pair(q)
        grads = split_pair(grad)
        mask = mask_ref[...]
        dq = jnp.zeros((128, rows), F32)
        dk = jnp.zeros((rows, 128), F32)
        dv = jnp.zeros((rows, 128), F32)
        for head in range(2):
            scores = mm(keys[head], q, NT) * SCALE2 + mask
            probs = jnp.exp2(scores - lse_ref[2 * pair + head : 2 * pair + head + 1, :])
            gprobs = mm(values[head], grad, NT)
            weighted = probs * gprobs
            delta = jnp.sum(weighted, axis=0, keepdims=True)
            gscores = ((weighted - probs * delta) * SCORE_SCALE).astype(BF16)
            dq = dq + mm(turned(keys[head]), gscores)
            dk = dk + mm(gscores, queries[head])
            dv = dv + mm(probs.astype(BF16), grads[head])
        dq_ref[:, cols] = dq.T
        dk_ref[:, cols] = dk
        dv_ref[:, cols] = dv


def project_backward_kernel(
    split, side, x_ref, w_ref, dq_ref, dk_ref, dv_ref, base_ref, sums_in_ref, info_ref, *rest
):
    if split:
        gout_refs, rest = rest[:2], rest[2:]
    outs = 2 if split else 1
    gin_refs = rest[:outs]
    tg_ref, back_ref, sums_ref = rest[outs:]
    hw = dq_ref.shape[1]
    width = x_ref.shape[1]
    half = back_ref.shape[0]
    if split:
        for dest, source in zip(gin_refs, gout_refs):
            for j in range(dest.shape[0]):
                dest[j, 3] = source[j]
    sums_ref[...] = sums_in_ref[...]
    m = lax.axis_index("mp")
    which = m if side == 0 else 1 - m
    x = x_ref[...]
    total = base_ref[...]
    for part, ref in enumerate((dq_ref, dk_ref, dv_ref)):
        grad = ref[...]
        if part != 1:
            spot = pl.multiple_of((part // 2) * width + which * hw, 128)
            sums_ref[:, pl.ds(spot, hw)] = jnp.sum(grad, axis=0, keepdims=True)
        grad_low = grad.astype(BF16)
        gin = mm(x, grad_low, TN).astype(BF16)
        if split:
            keep_ref, send_ref = gin_refs
            size = keep_ref.shape[2]
            emit([gin[i * size : (i + 1) * size] for i in range(width // size)], 0, keep_ref, send_ref, (part,))
        else:
            gin_refs[0][part] = gin
        total = total + mm(grad_low, w_ref[part], NT)
    tg_ref[...] = total.astype(tg_ref.dtype)
    if side == 0:
        window = pl.ds(pl.multiple_of(info_ref[1], half), half)
        back_ref[...] = tg_ref[window, :]
    else:
        back_ref[...] = jnp.zeros_like(back_ref)


def norm_stats(hidden):
    mean = jnp.mean(hidden, axis=1, keepdims=True)
    centred = hidden - mean
    inverse = lax.rsqrt(jnp.mean(centred * centred, axis=1, keepdims=True) + NORM_EPS)
    return centred * inverse, inverse


def out_norm_kernel(tok_ref, oa_ref, ob_ref, wo_ref, wa_ref, wb_ref, wc_ref, wd_ref, vec_ref, unit_ref, inv_ref, low_ref, w_ref):
    width = tok_ref.shape[1]
    place_quarters((wa_ref, wb_ref, wc_ref, wd_ref), w_ref, 0, 2)
    hidden = tok_ref[...].astype(F32) + (mm(oa_ref[...], wo_ref[...]) + mm(ob_ref[...], w_ref[...]))
    unit, inverse = norm_stats(hidden + vec_ref[:, 2 * width : 3 * width])
    unit_ref[...] = unit
    inv_ref[...] = inverse
    low_ref[...] = (unit * vec_ref[:, 4 * width : 5 * width] + vec_ref[:, 5 * width : 6 * width]).astype(BF16)


def gelu_parts(x):
    size = jnp.abs(x) * 0.7071067811865476
    bell = jnp.exp2(x * x * (-0.5 * LOG2E))
    t = 1.0 / (1.0 + 0.3275911 * size)
    poly = t * (
        0.254829592 + t * (-0.284496736 + t * (1.421413741 + t * (-1.453152027 + t * 1.061405429)))
    )
    tail = 0.5 * poly * bell
    below = jnp.where(x >= 0.0, 1.0 - tail, tail)
    return x * below, below + x * bell * 0.3989422804014327


def ffn_up(low, up, bias, act_ref, pull_ref, cols):
    upper = mm(low, up) + bias
    value, pull = gelu_parts(upper)
    act_ref[:, cols] = value.astype(BF16)
    pull_ref[:, cols] = pull


def ffn_own_kernel(low_ref, up_ref, down_ref, vec_ref, act_ref, pull_ref, total_ref):
    tile = 384
    width, fw = up_ref.shape
    low = low_ref[...]
    base = 8 * width + lax.axis_index("mp") * fw
    for step in range(fw // tile):
        cols = slice(step * tile, (step + 1) * tile)
        bias = vec_ref[:, pl.ds(pl.multiple_of(base + step * tile, 128), tile)]
        ffn_up(low, up_ref[:, cols], bias, act_ref, pull_ref, cols)
    total_ref[...] = mm(act_ref[...], down_ref[...])


def ffn_other_kernel(low_ref, ua_ref, ub_ref, uc_ref, ud_ref, vec_ref, act_ref, pull_ref):
    width, tile = ua_ref.shape
    low = low_ref[...]
    place = quarter_place(1)
    base = 8 * width + (1 - lax.axis_index("mp")) * 4 * tile
    for i, up_ref in enumerate((ua_ref, ub_ref, uc_ref, ud_ref)):
        spot = (place ^ i) * tile
        bias = vec_ref[:, pl.ds(pl.multiple_of(base + spot, 128), tile)]
        ffn_up(low, up_ref[...], bias, act_ref, pull_ref, pl.ds(pl.multiple_of(spot, 128), tile))


def ffn_finish_kernel(
    act_ref,
    da_ref,
    db_ref,
    dc_ref,
    dd_ref,
    part_ref,
    unit_ref,
    vec_ref,
    cot_ref,
    got_ref,
    info_ref,
    out_ref,
    send_ref,
    grad_ref,
    glow_ref,
    sums_ref,
    total_ref,
    cots_ref,
):
    width = part_ref.shape[1]
    half = got_ref.shape[0]
    tile = da_ref.shape[0]
    place = quarter_place(2)
    total_ref[...] = part_ref[...]
    for i, down_ref in enumerate((da_ref, db_ref, dc_ref, dd_ref)):
        spot = pl.multiple_of((place ^ i) * tile, 128)
        total_ref[...] += mm(act_ref[:, pl.ds(spot, tile)], down_ref[...])
    exchange_rows(info_ref, cot_ref, got_ref, cots_ref)
    normed = unit_ref[...] * vec_ref[:, 4 * width : 5 * width] + vec_ref[:, 5 * width : 6 * width]
    unit, inverse = norm_stats(normed + total_ref[...] + vec_ref[:, 3 * width : 4 * width])
    gain = vec_ref[:, 6 * width : 7 * width]
    out_ref[...] = (unit * gain + vec_ref[:, 7 * width : 8 * width]).astype(BF16)
    send_ref[...] = out_ref[pl.ds(pl.multiple_of(info_ref[1], half), half), :]
    cot = cots_ref[...].astype(F32)
    sums_ref[...] = jnp.zeros_like(sums_ref)
    sums_ref[:, 6 * width : 7 * width] = jnp.sum(cot * unit, axis=0, keepdims=True)
    sums_ref[:, 7 * width : 8 * width] = jnp.sum(cot, axis=0, keepdims=True)
    scaled = cot * gain
    grad = inverse * (
        scaled
        - jnp.mean(scaled, axis=1, keepdims=True)
        - unit * jnp.mean(scaled * unit, axis=1, keepdims=True)
    )
    sums_ref[:, 3 * width : 4 * width] = jnp.sum(grad, axis=0, keepdims=True)
    grad_ref[...] = grad
    glow_ref[...] = grad.astype(BF16)


def aligned(value, to=128):
    return value if isinstance(value, int) else pl.multiple_of(value, to)


def ffn_backward_kernel(split, side, low_ref, glow_ref, act_ref, pull_ref, base_ref, sums_in_ref, *rest):
    pieces = 4 if side else 1
    up_refs, down_refs, rest = rest[:pieces], rest[pieces : 2 * pieces], rest[2 * pieces :]
    outs = 2 if split else 1
    gdown_refs, gup_refs, (gn_ref, sums_ref) = rest[:outs], rest[outs : 2 * outs], rest[2 * outs : 2 * outs + 2]
    rows, width = low_ref.shape
    fw = act_ref.shape[1]
    tile = 384
    low = low_ref[...]
    glow = glow_ref[...]
    gn_ref[...] = base_ref[...]
    sums_ref[...] = sums_in_ref[...]
    m = lax.axis_index("mp")
    base = 8 * width + (1 - m if side else m) * fw

    def down_part(number, down):
        spot = aligned(number * tile)
        cols = pl.ds(spot, tile)
        gdown = mm(act_ref[:, cols], glow, TN).astype(BF16)
        if split:
            keep_ref, send_ref = gdown_refs
            size = keep_ref.shape[1]
            per = tile // size
            emit([gdown[i * size : (i + 1) * size] for i in range(per)], number * (per // 2), keep_ref, send_ref, ())
        else:
            gdown_refs[0][cols, :] = gdown
        gupper = mm(glow, down, NT) * pull_ref[:, cols]
        sums_ref[:, pl.ds(pl.multiple_of(base + spot, 128), tile)] = jnp.sum(gupper, axis=0, keepdims=True)
        return gupper.astype(BF16)

    def up_part(number, gupper, up):
        cols = pl.ds(aligned(number * tile), tile)
        gup = mm(low, gupper, TN).astype(BF16)
        if split:
            keep_ref, send_ref = gup_refs
            size = keep_ref.shape[1] // 2
            shards = [gup[i * size : (i + 1) * size] for i in range(width // size)]
            under = pl.ds(aligned((number // 2) * size, 16), size)
            beside = pl.ds(aligned((number % 2) * tile), tile)
            emit(shards, 0, keep_ref, send_ref, (under, beside))
        else:
            gup_refs[0][:, cols] = gup
        gn_ref[...] += mm(gupper, up, NT)

    if side:
        gupper_ref = rest[2 * outs + 2]
        for i in range(4):
            number = quarter_place(2) ^ i
            cols = pl.ds(aligned(number * tile), tile)
            gupper_ref[:, cols] = down_part(number, down_refs[i][...])
        for i in range(4):
            number = quarter_place(1) ^ i
            cols = pl.ds(aligned(number * tile), tile)
            up_part(number, gupper_ref[:, cols], up_refs[i][...])
    else:

        for number in range(fw // tile):
            cols = slice(number * tile, (number + 1) * tile)
            up_part(number, down_part(number, down_refs[0][cols, :]), up_refs[0][:, cols])


def norm_back_kernel(
    split,
    gn_ref,
    unit_ref,
    inv_ref,
    vec_ref,
    oa_ref,
    ob_ref,
    wa_ref,
    wb_ref,
    sums_in_ref,
    grad_ref,
    ga_ref,
    gb_ref,
    *rest,
):
    sums_ref = rest[-1]
    width = gn_ref.shape[1]
    gn = gn_ref[...]
    unit = unit_ref[...]
    sums_ref[...] = sums_in_ref[...]
    sums_ref[:, 4 * width : 5 * width] = jnp.sum(gn * unit, axis=0, keepdims=True)
    sums_ref[:, 5 * width : 6 * width] = jnp.sum(gn, axis=0, keepdims=True)
    scaled = gn * vec_ref[:, 4 * width : 5 * width]
    grad = inv_ref[...] * (
        scaled
        - jnp.mean(scaled, axis=1, keepdims=True)
        - unit * jnp.mean(scaled * unit, axis=1, keepdims=True)
    )
    sums_ref[:, 2 * width : 3 * width] = jnp.sum(grad, axis=0, keepdims=True)
    grad_ref[...] = grad
    low = grad.astype(BF16)
    ga_ref[...] = mm(low, wa_ref[...], NT).astype(BF16)
    gb_ref[...] = mm(low, wb_ref[...], NT).astype(BF16)
    for i, o_ref in enumerate((oa_ref, ob_ref)):
        gout = mm(o_ref[...], low, TN)
        if split:
            keep_ref, send_ref = rest[2 * i], rest[2 * i + 1]
            size = keep_ref.shape[1] // 2
            shards = []
            for j in range(gout.shape[0] // size):
                rows = gout[j * size : (j + 1) * size]
                shards.append(jnp.concatenate([rows[:, : width // 2], rows[:, width // 2 :]], axis=0).astype(BF16))
            emit(shards, 0, keep_ref, send_ref, ())
        else:
            rest[i][...] = gout.astype(BF16)


def combine_kernel(plans, *refs):
    total = sum(terms for pieces, _, _, _ in plans for terms, _ in pieces)
    ins, outs = refs[:total], refs[total:]
    for pieces, bit, where, count in plans:
        dests, outs = outs[:count], outs[count:]
        row = 0
        for terms, rows in pieces:
            here, ins = ins[:terms], ins[terms:]
            for j in range(dests[0].shape[0]):
                for number, dest in enumerate(dests):
                    spot = j + where
                    if count == 2:
                        odd = (lax.axis_index("dp") >> bit) % 2
                        side = odd if number == 0 else 1 - odd
                        spot = ((j >> where) << (where + 1)) + (side << where) + (j & ((1 << where) - 1))

                    def read(term):
                        cut = rows is not None and term.shape[1] > rows[1]
                        part = term[spot, rows[0] : rows[0] + rows[1], :] if cut else term[spot]
                        return part.astype(F32)

                    value = read(here[0])
                    for term in here[1:]:
                        value = value + read(term)
                    value = value.astype(dest.dtype)
                    if len(pieces) == 1:
                        dest[j] = value
                    else:
                        dest[j, row : row + value.shape[0], :] = value
            row += -(-(here[0].shape[1] if rows is None else rows[1]) // 16) * 16


def unswap_kernel(work_ref, got_ref, info_ref, out_ref):
    exchange_rows(info_ref, work_ref, got_ref, out_ref)


def flip(values, axis, bit, count):
    pairs = [(i, i ^ (1 << bit)) for i in range(count)]
    return lax.ppermute(values, axis, pairs)


def halve(values, bit):
    split = values.reshape((values.shape[0] // 2, 2) + values.shape[1:])
    keep = lax.dynamic_index_in_dim(split, bit, 1, keepdims=False)
    send = lax.dynamic_index_in_dim(split, 1 - bit, 1, keepdims=False)
    return keep, send


def body(
    tokens,
    cotangent,
    segment_ids,
    key_keep,
    in_weight,
    out_weight,
    up_weight,
    down_weight,
    in_master,
    out_master,
    up_master,
    down_master,
    in_first,
    out_first,
    up_first,
    down_first,
    in_second,
    out_second,
    up_second,
    down_second,
    vector_master,
    vector_first,
    vector_second,
):
    rows, width = tokens.shape
    d = lax.axis_index("dp")
    dp_count = lax.axis_size("dp")
    bits = dp_count.bit_length() - 1
    hw = in_weight.shape[2]
    fw = up_weight.shape[1]
    half = rows // 2
    smem = pltpu.SMEM
    length = vector_master.shape[0]
    vec = vector_master.reshape(1, length)
    in_own = jnp.transpose(in_weight, (1, 0, 2))
    split = (width // dp_count) % 16 == 0

    state = {"last": None}

    def run(kernel, outs, args, through=(), after=(), **options):
        before = () if state["last"] is None else (state["last"],)
        res = call(kernel, outs, args, after=tuple(after) + before, through=tuple(through), **options)
        state["last"] = res[-1] if through else res[0]
        return res

    s_tok, s_cot, s_in, s_out, s_up, s_down, seg, code, info = run(
        prepare_kernel,
        [
            ((half, width), BF16),
            ((half, width), BF16),
            ((3, width // 4, hw), BF16),
            ((hw // 4, width), BF16),
            ((width, fw // 4), BF16),
            ((fw // 4, width), BF16),
            ((1, rows), jnp.int32),
            ((rows, 1), jnp.int32),
            ((8,), jnp.int32),
        ],
        (tokens, cotangent, in_own, out_weight, up_weight, down_weight, segment_ids, key_keep),
        scratch=[pltpu.SemaphoreType.DMA((6,))],
        limit=60,
        name="prepare",
        us=2,
        places={i: pltpu.HBM for i in range(6)},
        out_places={8: smem},
    )

    def relay(arrays, name, after=()):
        return run(lambda *refs: None, [], (), through=arrays, after=after, limit=4, name=name)

    def x_hop(values):
        return flip(values, "mp", 0, 2)

    def dp_hop(values, bit):
        return flip(values, "dp", bit, dp_count)

    def xy_hop(values):
        pairs = [(i, i ^ 5) for i in range(2 * dp_count)]
        return lax.ppermute(values, ("dp", "mp"), pairs)

    attn_flops = 2 * rows * width * 3 * hw + 4 * rows * rows * hw * 4
    wide = (rows, width)
    narrow = (rows, hw)
    hidden = (rows, fw)
    ffn_flops = 4 * rows * width * fw
    line = (1, length)
    attend_outs = [(narrow, BF16)] * 4 + [((8, rows), F32)]
    square = pltpu.VMEM((rows, rows), F32)

    got_tok = x_hop(s_tok)
    in_0 = x_hop(s_in)
    out_0 = x_hop(s_out)
    x, q_a, k_a, v_a, o_a, lse_a, s_up, s_down, s_cot = run(
        attend_forward_own_kernel,
        [(wide, BF16)] + attend_outs,
        (tokens, got_tok, info, in_own, vec, seg, code),
        through=(s_up, s_down, s_cot),
        scratch=[square],
        name="attend_forward_own",
        us=6,
        limit=OWN_LIMIT,
        places={2: smem},
    )
    up_0 = x_hop(s_up)
    in_0, out_0, s_down = relay((in_0, out_0, s_down), "relay_one")
    in_2 = dp_hop(in_0, 1)
    out_2 = dp_hop(out_0, 2)
    in_1 = dp_hop(in_0, 0)
    down_0 = x_hop(s_down)
    in_2, out_2, up_0, out_0 = relay((in_2, out_2, up_0, out_0), "relay_two")
    in_3 = dp_hop(in_2, 0)
    up_2 = dp_hop(up_0, 1)
    q_b, k_b, v_b, o_b, lse_b, in_other, s_cot, up_0, out_0, out_2 = run(
        attend_forward_other_kernel,
        attend_outs + [((3, width, hw), BF16)],
        (x, in_0, in_1, in_2, in_3, vec, seg, code),
        through=(s_cot, up_0, out_0, out_2),
        scratch=[square],
        name="attend_forward_other",
        us=6,
    )
    out_1 = dp_hop(out_0, 0)
    out_3 = dp_hop(out_2, 0)
    unit, inverse, low, out_other = run(
        out_norm_kernel,
        [(wide, F32), ((rows, 1), F32), (wide, BF16), ((hw, width), BF16)],
        (x, o_a, o_b, out_weight, out_0, out_1, out_2, out_3, vec),
        name="out_norm",
        us=1.5,
    )
    down_0, s_cot, up_0, up_2 = relay((down_0, s_cot, up_0, up_2), "relay_down")
    up_1 = dp_hop(up_0, 0)
    up_3 = dp_hop(up_2, 0)
    down_2 = dp_hop(down_0, 2)
    got_cot = x_hop(s_cot)
    act_a, pull_a, part = run(
        ffn_own_kernel,
        [(hidden, BF16), (hidden, F32), (wide, F32)],
        (low, up_weight, down_weight, vec),
        name="ffn_own",
        us=8,
    )
    act_b, pull_b = run(
        ffn_other_kernel,
        [(hidden, BF16), (hidden, F32)],
        (low, up_0, up_1, up_2, up_3, vec),
        name="ffn_other",
        us=5,
    )
    down_2, down_0 = relay((down_2, down_0), "relay_five", (got_cot,))
    down_1 = dp_hop(down_0, 0)
    down_3 = dp_hop(down_2, 0)
    ups = (up_0, up_1, up_2, up_3)
    downs = (down_0, down_1, down_2, down_3)
    out_work, s_layer, grad_two, glow, sums = run(
        ffn_finish_kernel,
        [(wide, BF16), ((half, width), BF16), (wide, F32), (wide, BF16), (line, F32)],
        (act_b, *downs, part, unit, vec, cotangent, got_cot, info),
        scratch=[pltpu.VMEM(wide, F32), pltpu.VMEM(wide, BF16)],
        name="ffn_finish",
        us=5,
        places={10: smem},
    )

    got_layer = x_hop(s_layer)

    def unswap(work, got, name):
        return run(unswap_kernel, [(wide, BF16)], (work, got, info), name=name, places={2: smem})[0]

    count = dp_count // 2
    down_shape = (fw // dp_count, width)
    up_shape = (2 * (width // dp_count), fw // 2)
    in_shape = (4, width // dp_count, hw)
    out_shape = (2 * (hw // dp_count), width // 2)

    def parts(shape):
        return [((count,) + shape, BF16)] * 2

    def ffn_back(side, act, pull, ups, downs, base, sums, name, after=()):
        kinds = parts(down_shape) + parts(up_shape) if split else [((fw, width), BF16), ((width, fw), BF16)]
        res = run(
            functools.partial(ffn_backward_kernel, split, side),
            kinds + [(wide, F32), (line, F32)],
            (low, glow, act, pull, base, sums, *ups, *downs),
            scratch=[pltpu.VMEM(hidden, BF16)] if side else [],
            name=name,
            us=10.5,
            after=after,
        )
        gn, sums = res[-2:]
        if split:
            return tuple(res[0:2]), tuple(res[2:4]), gn, sums
        down = halve(res[0].reshape((dp_count,) + down_shape), d & 1)
        up = jnp.transpose(res[1].reshape(dp_count, width // dp_count, 2, fw // 2), (0, 2, 1, 3))
        up = halve(up.reshape((dp_count,) + up_shape), d & 1)
        return down, up, gn, sums

    def pieces_of(terms):
        return terms if isinstance(terms, list) else [(terms, None)]

    def shape_of(pieces):
        rows = [t[0].shape[1] if r is None else r[1] for t, r in pieces]
        shape = pieces[0][0][0].shape
        if len(pieces) > 1:
            return (shape[0], sum(-(-r // 16) * 16 for r in rows), shape[2])
        return shape if pieces[0][1] is None else (shape[0], rows[0], shape[2])

    def halves(terms, bit, where=0, kinds=(F32, BF16)):
        pieces = pieces_of(terms)
        shape = shape_of(pieces)
        shape = (shape[0] // 2,) + shape[1:]
        return (pieces, bit, where, [(shape, kind) for kind in kinds])

    def whole(terms, kind=BF16, window=None):
        pieces = pieces_of(terms)
        shape = shape_of(pieces)
        if window is not None:
            shape = (window[1],) + shape[1:]
        return (pieces, None, 0 if window is None else window[0], [(shape, kind)])

    def combine(name, tensors, through=(), after=()):
        plans = tuple(
            (tuple((len(t), r) for t, r in pieces), bit, where, len(o)) for pieces, bit, where, o in tensors
        )
        res = run(
            functools.partial(combine_kernel, plans),
            [o for t in tensors for o in t[3]],
            [v for pieces, _, _, _ in tensors for t, _ in pieces for v in t],
            name=name,
            through=through,
            after=after,
        )
        res = list(res)
        made = []
        for t in tensors:
            made.append(tuple(res[: len(t[3])]) if len(t[3]) == 2 else res[0])
            res = res[len(t[3]) :]
        return made + res

    down_b, up_b, gn, sums = ffn_back(1, act_b, pull_b, ups, downs, grad_two, sums, "ffn_backward_other")
    core_down_b = dp_hop(down_b[1], 0)
    core_up_b = dp_hop(up_b[1], 0)
    down_a, up_a, gn, sums = ffn_back(
        0, act_a, pull_a, (up_weight,), (down_weight,), gn, sums, "ffn_backward_own"
    )
    core_down_a = dp_hop(down_a[1], 0)
    core_up_a = dp_hop(up_a[1], 0)
    (down_b_keep, down_b_send), (up_b_keep, up_b_send) = combine(
        "combine_ffn_other", [halves((down_b[0], core_down_b), 1), halves((up_b[0], core_up_b), 2, 1)]
    )
    y_down_b = dp_hop(down_b_send, 1)
    z_up_b = dp_hop(up_b_send, 2)

    kinds = parts(out_shape) * 2 if split else [((hw, width), BF16)] * 2
    grad_one, gatt_a, gatt_b, *gout, sums = run(
        functools.partial(norm_back_kernel, split),
        [(wide, F32), (narrow, BF16), (narrow, BF16)] + kinds + [(line, F32)],
        (gn, unit, inverse, vec, o_a, o_b, out_weight, out_other, sums),
        name="norm_back",
        us=2.5,
    )
    (down_a_keep, down_a_send), (up_a_keep, up_a_send) = combine(
        "combine_ffn_own", [halves((down_a[0], core_down_a), 1), halves((up_a[0], core_up_a), 2, 1)]
    )
    y_down_a = dp_hop(down_a_send, 1)
    z_up_a = dp_hop(up_a_send, 2)

    def attend_back(q, k, v, gatt, lse, name):
        return run(
            attend_backward_kernel,
            [(narrow, F32)] * 3,
            (q, k, v, gatt, lse, seg, code),
            scratch=[square],
            name=name,
            us=9,
        )

    def project_back(side, w, grads, base, kind, sums, gout, name, after=()):
        kinds = parts(in_shape) if split else [((3, width, hw), BF16)]
        res = run(
            functools.partial(project_backward_kernel, split, side),
            kinds + [(wide, kind), ((half, width), BF16), (line, F32)],
            (x, w, *grads, base, sums, info) + (tuple(gout) if split else ()),
            name=name,
            us=3,
            after=after,
            places={7: smem},
        )
        tg, back, sums = res[-3:]
        if split:
            return tuple(res[0:2]), tg, back, sums
        part = (dp_count, width // dp_count, hw)
        gout = jnp.transpose(gout[0].reshape(dp_count, hw // dp_count, 2, width // 2), (0, 2, 1, 3)).reshape(part)
        grads = jnp.concatenate([res[0].reshape((3,) + part), gout[None]])
        return halve(jnp.transpose(grads, (1, 0, 2, 3)), d & 1), tg, back, sums

    grads_b = attend_back(q_b, k_b, v_b, gatt_b, lse_b, "attend_backward_other")
    (sum_b,) = combine(
        "combine_ffn_x",
        [whole([((down_b_keep, y_down_b), None), ((up_b_keep, z_up_b), None)])],
        after=(got_layer,),
    )
    x_ffn = x_hop(sum_b)
    grads_a = attend_back(q_a, k_a, v_a, gatt_a, lse_a, "attend_backward_own")
    gout_a, gout_b = (gout[:2], gout[2:]) if split else (gout[:1], gout[1:])
    in_b, tg, _, sums = project_back(
        1, in_other, grads_b, grad_one, F32, sums, gout_b, "project_backward_other"
    )
    core_in_b = dp_hop(in_b[1], 0)
    in_a, tg, back, sums = project_back(0, in_own, grads_a, tg, BF16, sums, gout_a, "project_backward_own", (y_down_a, z_up_a))
    core_in_a = dp_hop(in_a[1], 0)
    sums = sums.reshape(1, length // 128, 128)
    z_sums = dp_hop(sums, 2)
    layer_out = unswap(out_work, got_layer, "unswap_out")
    (sums,) = combine("sums_z", [whole((sums, z_sums), F32)])
    for bit in range(4, bits):
        z_sums = dp_hop(sums, bit)
        (sums,) = combine("sums_z", [whole((sums, z_sums), F32)])
    z_sums = dp_hop(sums, 3)

    down_size, up_size = down_shape[0], up_shape[0]
    up_start = -(-down_size // 16) * 16
    down_t, up_t = combine(
        "tail_ffn",
        [
            halves([((down_a_keep, y_down_a, x_ffn), (0, down_size))], 2),
            halves([((up_a_keep, z_up_a, x_ffn), (up_start, up_size))], 1),
        ],
    )
    big = [((down_t[0], dp_hop(down_t[1], 2)), None), ((up_t[0], dp_hop(up_t[1], 1)), None)]
    (in_keep, in_y), (in_x, in_xy), sums = combine(
        "tail_core",
        [
            halves((in_a[0], core_in_a), 1),
            halves((in_b[0], core_in_b), 1, kinds=(BF16, BF16)),
            whole((sums, z_sums), F32),
        ],
    )
    in_terms = (in_keep, dp_hop(in_y, 1), x_hop(in_x), xy_hop(in_xy))
    for bit in range(2, bits):
        if bit == 2:
            in_t, sums = combine("tail_in", [halves(in_terms, bit)], through=(sums,))
            x_sums = x_hop(sums)
            in_terms = (in_t[0], dp_hop(in_t[1], bit))
            big_t, sums, back = combine(
                "tail_more", [halves(big, bit + 1), whole((sums, x_sums), F32)], through=(back,)
            )
            core_sums = dp_hop(sums, 0)
            big = (big_t[0], dp_hop(big_t[1], bit + 1))
            got_back = x_hop(back)
        else:
            if bit == 3:
                in_t, sums = combine("tail_in_more", [halves(in_terms, bit), whole((sums, core_sums), F32)])
            else:
                in_t, big_t = combine("tail_in_more", [halves(in_terms, bit), halves(big, bit)])
                big = (big_t[0], dp_hop(big_t[1], bit))
            in_terms = (in_t[0], dp_hop(in_t[1], bit))
    sums = sums + dp_hop(sums, 1)
    token_grad = unswap(tg, got_back, "unswap_grad")

    def total(pair):
        keep, got = pair
        return (keep.astype(F32) + got.astype(F32)).reshape(keep.shape[1:])

    spot = 0
    grads = []
    for shape in (down_shape, up_shape):
        cut = tuple(v[:, spot : spot + shape[0]] for v in big)
        grads.append(total(cut))
        spot += -(-shape[0] // 16) * 16
    grad_down, grad_up = grads
    size = width // dp_count
    grad_up = jnp.concatenate([grad_up[:size], grad_up[size:]], axis=1)
    grad_in = total(in_terms)
    size = hw // dp_count
    grad_out = jnp.concatenate([grad_in[3, :size], grad_in[3, size:]], axis=1)
    grad_in = jnp.transpose(grad_in[:3], (1, 0, 2))
    grad_vector = sums.reshape(length)

    def matrix_step(grad, master, first, second):
        f, s, n = adam_step(grad, master, first, second, MATRIX_RATE, WEIGHT_DECAY)
        return (f, s, n, n.astype(BF16))

    return (
        layer_out,
        token_grad,
        *matrix_step(grad_in, in_master, in_first, in_second),
        *matrix_step(grad_out, out_master, out_first, out_second),
        *matrix_step(grad_up, up_master, up_first, up_second),
        *matrix_step(grad_down, down_master, down_first, down_second),
        *adam_step(grad_vector, vector_master, vector_first, vector_second, VECTOR_RATE, 0.0),
    )


def solution(mesh):
    tok = P(("dp", "mp"), None)
    line = P("dp", None)
    in_state = P("dp", None, "mp")
    out_state = P(("mp", "dp"), None)
    up_state = P("dp", "mp")
    states = (in_state, out_state, up_state, out_state)
    in_specs = (
        (tok, tok, line, line, P(None, None, "mp"), P("mp", None), P(None, "mp"), P("mp", None))
        + states * 3
        + (P(), P(), P())
    )
    out_specs = (
        (tok, tok)
        + (in_state,) * 4
        + (out_state,) * 4
        + (up_state,) * 4
        + (out_state,) * 4
        + (P(), P(), P())
    )
    return jax.shard_map(body, mesh=mesh, in_specs=in_specs, out_specs=out_specs, check_vma=False)
```

```python
import functools
import math

import jax
import jax.numpy as jnp
from jax import lax
from jax.experimental import pallas as pl
from jax.experimental.pallas import tpu as pltpu
from jax.sharding import PartitionSpec as P

HD = 64
STEP = 7
NORM_EPS = 1e-06
SCORE_SCALE = 0.125
NEG_FILL = -1e30
MOMENT_DECAY = 0.5
SQUARE_DECAY = 0.5
MATRIX_RATE = 0.03
VECTOR_RATE = 0.2
WEIGHT_DECAY = 0.01
ADAM_EPS = 1e-08
LOG2E = 1.4426950408889634
SCALE2 = SCORE_SCALE * LOG2E
F32 = jnp.float32
BF16 = jnp.bfloat16
MIB = 1024 * 1024
WORK = 1e6
SLACK = 16
OWN_LIMIT = 60
DOWN_PAD = 16

NN = (((1,), (0,)), ((), ()))
NT = (((1,), (1,)), ((), ()))
TN = (((0,), (0,)), ((), ()))


def mm(a, b, dims=NN):
    return lax.dot_general(a, b, dims, preferred_element_type=F32)


def padded_bytes(shape, dtype):
    rows = shape[-2] if len(shape) > 1 else 1
    tiles = -(-rows // 8) * 8 * -(-shape[-1] // 128) * 128
    return math.prod(shape[:-2]) * tiles * jnp.dtype(dtype).itemsize


def call(kernel, outs, args, scratch=(), limit=None, name=None, after=(), through=(), places=None, out_places=None, us=1):
    count = len(args)
    places = places or {}
    out_places = out_places or {}
    anywhere = pl.BlockSpec(memory_space=pl.ANY)
    specs = [pl.BlockSpec(memory_space=places.get(i, pltpu.VMEM)) for i in range(count)]
    specs += [anywhere] * (len(through) + len(after))
    made = len(outs)
    if limit is None:
        held = [(v.shape, v.dtype) for v in scratch if v.memory_space == pltpu.VMEM]
        limit = sum(padded_bytes(*v) for v in held) // MIB + SLACK

    def run(*refs):
        own = refs[count + len(through) + len(after) :]
        kernel(*refs[:count], *own[:made], *own[made + len(through) :])

    return pl.pallas_call(
        run,
        out_shape=[jax.ShapeDtypeStruct(s, d) for s, d in outs]
        + [jax.ShapeDtypeStruct(v.shape, v.dtype) for v in through],
        in_specs=specs,
        out_specs=[pl.BlockSpec(memory_space=out_places.get(i, pltpu.VMEM)) for i in range(made)] + [anywhere] * len(through),
        scratch_shapes=list(scratch),
        input_output_aliases={count + i: made + i for i in range(len(through))},
        compiler_params=pltpu.CompilerParams(vmem_limit_bytes=limit * MIB),
        cost_estimate=pl.CostEstimate(flops=int(us * WORK), bytes_accessed=0, transcendentals=0),
        name=name,
    )(*args, *through, *after)


def adam_step(grad, master, first, second, rate, decay):
    first_next = MOMENT_DECAY * first + (1.0 - MOMENT_DECAY) * grad
    second_next = SQUARE_DECAY * second + (1.0 - SQUARE_DECAY) * grad * grad
    first_fix = 1.0 - MOMENT_DECAY**STEP
    second_fix = 1.0 - SQUARE_DECAY**STEP
    update = first_next / first_fix / (jnp.sqrt(second_next / second_fix) + ADAM_EPS)
    master_next = master - rate * (update + decay * master)
    return (first_next, second_next, master_next)


def send_copies(pieces, sems):
    copies = []
    for i, (source, dest, axis, bit) in enumerate(pieces):
        size = source.shape[axis] // 4
        spot = pl.ds(pl.multiple_of(quarter_place(bit) * size, size), size)
        view = source.at[spot] if axis == 0 else source.at[:, spot]
        copies.append(pltpu.make_async_copy(view, dest.at[pl.ds(0, size)] if axis == 0 else dest, sems.at[i]))
    return copies


def prepare_kernel(tok_ref, in_ref, seg_ref, keep_ref, stok_ref, sin_ref, segrow_ref, code_ref, info_ref, sems):
    rows = tok_ref.shape[0]
    half = rows // 2
    m = lax.axis_index("mp")
    copies = send_copies([(in_ref, sin_ref, 1, 1)], sems)
    copies[0].start()
    seg = seg_ref[...]
    spot = lax.broadcasted_iota(jnp.int32, seg.shape, 1)
    later = jnp.roll(seg, rows + 1, axis=1)
    begin = jnp.sum(jnp.where((seg == later) & (spot <= rows), spot, 0))
    late = begin > half
    first = jnp.where(late, half, 0)
    info_ref[0] = begin
    info_ref[1] = first
    window = pl.ds(pl.multiple_of(first, half), half)
    copies.append(pltpu.make_async_copy(tok_ref.at[window], stok_ref, sems.at[1]))
    copies[1].start()
    own = pl.ds(pl.multiple_of(m * rows, rows), rows)
    other = pl.ds(pl.multiple_of((1 - m) * rows, rows), rows)
    local = lax.broadcasted_iota(jnp.int32, (1, rows), 1)
    swapped = jnp.where(late, local - begin, begin - 1 - local) >= 0
    mine = jnp.where(swapped, seg_ref[:, other], seg_ref[:, own])
    kept = jnp.where(swapped, keep_ref[:, other], keep_ref[:, own])
    segrow_ref[...] = mine
    code = jnp.where(kept == 1, mine, -1)
    code_ref[...] = jnp.broadcast_to(code.astype(F32), (8, rows)).T[:, 0:1].astype(jnp.int32)
    for copy in copies:
        copy.wait()


def prepare_rest_kernel(
    cot_ref, out_ref, up_ref, down_ref, info_ref, scot_ref, sout_ref, sup_ref, sdown_ref, sems
):
    half = scot_ref.shape[0]
    copies = send_copies([(out_ref, sout_ref, 0, 2), (down_ref, sdown_ref, 0, 2), (up_ref, sup_ref, 1, 1)], sems)
    window = pl.ds(pl.multiple_of(info_ref[1], half), half)
    copies.append(pltpu.make_async_copy(cot_ref.at[window], scot_ref, sems.at[3]))
    for copy in copies:
        copy.start()
    for copy in copies:
        copy.wait()


def swapped_rows(info_ref, shape):
    begin = info_ref[0]
    first = info_ref[1]
    local = first + lax.broadcasted_iota(jnp.int32, shape, 0)
    return jnp.where(first > 0, local - begin, begin - 1 - local) >= 0


def exchange_rows(info_ref, source_ref, got_ref, dest_ref):
    half = got_ref.shape[0]
    window = pl.ds(pl.multiple_of(info_ref[1], half), half)
    dest_ref[...] = source_ref[...]
    dest_ref[window, :] = jnp.where(swapped_rows(info_ref, got_ref.shape), got_ref[...], source_ref[window, :])


def fill_mask(seg_ref, code_ref, mask_ref):
    rows = mask_ref.shape[0]
    row = lax.broadcasted_iota(jnp.int32, (rows, rows), 0)
    col = lax.broadcasted_iota(jnp.int32, (rows, rows), 1)
    allowed = (code_ref[...] == seg_ref[...]) | (row == col)
    mask_ref[...] = jnp.where(allowed, 0.0, NEG_FILL)


def split_pair(block):
    lane = lax.broadcasted_iota(jnp.int32, block.shape, 1)
    zero = jnp.zeros_like(block)
    return (jnp.where(lane < HD, block, zero), jnp.where(lane < HD, zero, block))


def quarter_place(bit):
    d = lax.axis_index("dp")
    return 2 * ((d >> bit) % 2) + d % 2


def place_quarters(pieces, dest_ref, axis, bit):
    place = quarter_place(bit)
    for i, piece in enumerate(pieces):
        size = piece.shape[axis]
        spot = pl.ds(pl.multiple_of((place ^ i) * size, size), size)
        if axis == 0:
            dest_ref[spot, :] = piece[...]
        else:
            dest_ref[:, spot, :] = piece[...]


def attend_forward(which, width, x_ref, w_ref, vec_ref, seg_ref, code_ref, q_ref, k_ref, v_ref, o_ref, lse_ref, mask_ref):
    rows, hw = q_ref.shape
    fill_mask(seg_ref, code_ref, mask_ref)
    x = x_ref[...]
    for part, ref in enumerate((q_ref, k_ref, v_ref)):
        out = mm(x, w_ref[part])
        if part != 1:
            spot = pl.multiple_of((part // 2) * width + which * hw, 128)
            out = out + vec_ref[:, pl.ds(spot, hw)]
        ref[...] = out.astype(BF16)
    lse_ref[...] = jnp.zeros_like(lse_ref)
    for pair in range(hw // 128):
        cols = slice(pair * 128, (pair + 1) * 128)
        q = q_ref[:, cols]
        keys = split_pair(k_ref[:, cols])
        values = split_pair(v_ref[:, cols])
        mask = mask_ref[...]
        total = jnp.zeros((128, rows), F32)
        for head in range(2):
            scores = mm(keys[head], q, NT) * SCALE2 + mask
            highest = jnp.max(scores, axis=0, keepdims=True)
            weights = jnp.exp2(scores - highest)
            sums = jnp.sum(weights, axis=0, keepdims=True)
            probs = (weights * (1.0 / sums)).astype(BF16)
            total = total + mm(turned(values[head]), probs)
            lse_ref[2 * pair + head : 2 * pair + head + 1, :] = highest + jnp.log2(sums)
        o_ref[:, cols] = total.T.astype(BF16)


def attend_forward_own_kernel(
    tok_ref, got_ref, info_ref, w_ref, vec_ref, seg_ref, code_ref, x_ref, q_ref, k_ref, v_ref, o_ref, lse_ref, mask_ref
):
    exchange_rows(info_ref, tok_ref, got_ref, x_ref)
    which = lax.axis_index("mp")
    attend_forward(
        which, x_ref.shape[1], x_ref, w_ref, vec_ref, seg_ref, code_ref, q_ref, k_ref, v_ref, o_ref, lse_ref, mask_ref
    )


def attend_forward_other_kernel(
    x_ref, wa_ref, wb_ref, wc_ref, wd_ref, vec_ref, seg_ref, code_ref, q_ref, k_ref, v_ref, o_ref, lse_ref, w_ref, mask_ref
):
    place_quarters((wa_ref, wb_ref, wc_ref, wd_ref), w_ref, 1, 1)
    which = 1 - lax.axis_index("mp")
    attend_forward(
        which, x_ref.shape[1], x_ref, w_ref, vec_ref, seg_ref, code_ref, q_ref, k_ref, v_ref, o_ref, lse_ref, mask_ref
    )


def emit(value, index, keep_ref, send_ref, where):
    parity = lax.axis_index("dp") % 2
    for j in range(len(value) // 2):
        even, odd = value[2 * j], value[2 * j + 1]
        keep_ref[(index + j,) + where] = jnp.where(parity == 0, even, odd)
        send_ref[(index + j,) + where] = jnp.where(parity == 0, odd, even)


def turned(block):
    return block.astype(F32).T.astype(BF16)


def attend_backward_kernel(q_ref, k_ref, v_ref, do_ref, lse_ref, seg_ref, code_ref, dq_ref, dk_ref, dv_ref, mask_ref):
    rows, hw = q_ref.shape
    fill_mask(seg_ref, code_ref, mask_ref)
    for pair in range(hw // 128):
        cols = slice(pair * 128, (pair + 1) * 128)
        q = q_ref[:, cols]
        grad = do_ref[:, cols]
        keys = split_pair(k_ref[:, cols])
        values = split_pair(v_ref[:, cols])
        queries = split_pair(q)
        grads = split_pair(grad)
        mask = mask_ref[...]
        dq = jnp.zeros((128, rows), F32)
        dk = jnp.zeros((rows, 128), F32)
        dv = jnp.zeros((rows, 128), F32)
        for head in range(2):
            scores = mm(keys[head], q, NT) * SCALE2 + mask
            probs = jnp.exp2(scores - lse_ref[2 * pair + head : 2 * pair + head + 1, :])
            gprobs = mm(values[head], grad, NT)
            weighted = probs * gprobs
            delta = jnp.sum(weighted, axis=0, keepdims=True)
            gscores = ((weighted - probs * delta) * SCORE_SCALE).astype(BF16)
            dq = dq + mm(turned(keys[head]), gscores)
            dk = dk + mm(gscores, queries[head])
            dv = dv + mm(probs.astype(BF16), grads[head])
        dq_ref[:, cols] = dq.T
        dk_ref[:, cols] = dk
        dv_ref[:, cols] = dv


def project_backward_kernel(
    split, side, x_ref, w_ref, dq_ref, dk_ref, dv_ref, base_ref, sums_in_ref, info_ref, *rest
):
    if split:
        gout_refs, rest = rest[:2], rest[2:]
    outs = 2 if split else 1
    gin_refs = rest[:outs]
    tg_ref, back_ref, sums_ref = rest[outs:]
    hw = dq_ref.shape[1]
    width = x_ref.shape[1]
    half = back_ref.shape[0]
    if split:
        for dest, source in zip(gin_refs, gout_refs):
            for j in range(dest.shape[0]):
                dest[j, 3] = source[j]
    sums_ref[...] = sums_in_ref[...]
    m = lax.axis_index("mp")
    which = m if side == 0 else 1 - m
    x = x_ref[...]
    total = base_ref[...]
    for part, ref in enumerate((dq_ref, dk_ref, dv_ref)):
        grad = ref[...]
        if part != 1:
            spot = pl.multiple_of((part // 2) * width + which * hw, 128)
            sums_ref[:, pl.ds(spot, hw)] = jnp.sum(grad, axis=0, keepdims=True)
        grad_low = grad.astype(BF16)
        gin = mm(x, grad_low, TN).astype(BF16)
        if split:
            keep_ref, send_ref = gin_refs
            size = keep_ref.shape[2]
            emit([gin[i * size : (i + 1) * size] for i in range(width // size)], 0, keep_ref, send_ref, (part,))
        else:
            gin_refs[0][part] = gin
        total = total + mm(grad_low, w_ref[part], NT)
    tg_ref[...] = total.astype(tg_ref.dtype)
    if side == 0:
        window = pl.ds(pl.multiple_of(info_ref[1], half), half)
        back_ref[...] = tg_ref[window, :]
    else:
        back_ref[...] = jnp.zeros_like(back_ref)


def norm_stats(hidden):
    mean = jnp.mean(hidden, axis=1, keepdims=True)
    centred = hidden - mean
    inverse = lax.rsqrt(jnp.mean(centred * centred, axis=1, keepdims=True) + NORM_EPS)
    return centred * inverse, inverse


def out_norm_kernel(tok_ref, oa_ref, ob_ref, wo_ref, wa_ref, wb_ref, wc_ref, wd_ref, vec_ref, unit_ref, inv_ref, low_ref, w_ref):
    width = tok_ref.shape[1]
    place_quarters((wa_ref, wb_ref, wc_ref, wd_ref), w_ref, 0, 2)
    hidden = tok_ref[...].astype(F32) + (mm(oa_ref[...], wo_ref[...]) + mm(ob_ref[...], w_ref[...]))
    unit, inverse = norm_stats(hidden + vec_ref[:, 2 * width : 3 * width])
    unit_ref[...] = unit
    inv_ref[...] = inverse
    low_ref[...] = (unit * vec_ref[:, 4 * width : 5 * width] + vec_ref[:, 5 * width : 6 * width]).astype(BF16)


def gelu_parts(x):
    size = jnp.abs(x) * 0.7071067811865476
    bell = jnp.exp2(x * x * (-0.5 * LOG2E))
    t = 1.0 / (1.0 + 0.3275911 * size)
    poly = t * (
        0.254829592 + t * (-0.284496736 + t * (1.421413741 + t * (-1.453152027 + t * 1.061405429)))
    )
    tail = 0.5 * poly * bell
    below = jnp.where(x >= 0.0, 1.0 - tail, tail)
    return x * below, below + x * bell * 0.3989422804014327


def ffn_up(low, up, bias, act_ref, pull_ref, cols):
    upper = mm(low, up) + bias
    value, pull = gelu_parts(upper)
    act_ref[:, cols] = value.astype(BF16)
    pull_ref[:, cols] = pull


def ffn_own_kernel(low_ref, up_ref, down_ref, vec_ref, act_ref, pull_ref, total_ref):
    tile = 384
    width, fw = up_ref.shape
    low = low_ref[...]
    base = 8 * width + lax.axis_index("mp") * fw
    for step in range(fw // tile):
        cols = slice(step * tile, (step + 1) * tile)
        bias = vec_ref[:, pl.ds(pl.multiple_of(base + step * tile, 128), tile)]
        ffn_up(low, up_ref[:, cols], bias, act_ref, pull_ref, cols)
    total_ref[...] = mm(act_ref[...], down_ref[...])


def ffn_other_kernel(low_ref, ua_ref, ub_ref, uc_ref, ud_ref, vec_ref, act_ref, pull_ref):
    width, tile = ua_ref.shape
    low = low_ref[...]
    place = quarter_place(1)
    base = 8 * width + (1 - lax.axis_index("mp")) * 4 * tile
    for i, up_ref in enumerate((ua_ref, ub_ref, uc_ref, ud_ref)):
        spot = (place ^ i) * tile
        bias = vec_ref[:, pl.ds(pl.multiple_of(base + spot, 128), tile)]
        ffn_up(low, up_ref[...], bias, act_ref, pull_ref, pl.ds(pl.multiple_of(spot, 128), tile))


def ffn_finish_kernel(
    act_ref,
    da_ref,
    db_ref,
    dc_ref,
    dd_ref,
    part_ref,
    unit_ref,
    vec_ref,
    cot_ref,
    got_ref,
    info_ref,
    out_ref,
    send_ref,
    grad_ref,
    glow_ref,
    sums_ref,
    total_ref,
    cots_ref,
):
    width = part_ref.shape[1]
    half = got_ref.shape[0]
    tile = act_ref.shape[1] // 4
    place = quarter_place(2)
    total_ref[...] = part_ref[...]
    for i, down_ref in enumerate((da_ref, db_ref, dc_ref, dd_ref)):
        spot = pl.multiple_of((place ^ i) * tile, 128)
        total_ref[...] += mm(act_ref[:, pl.ds(spot, tile)], down_ref[0:tile, :])
    exchange_rows(info_ref, cot_ref, got_ref, cots_ref)
    normed = unit_ref[...] * vec_ref[:, 4 * width : 5 * width] + vec_ref[:, 5 * width : 6 * width]
    unit, inverse = norm_stats(normed + total_ref[...] + vec_ref[:, 3 * width : 4 * width])
    gain = vec_ref[:, 6 * width : 7 * width]
    out_ref[...] = (unit * gain + vec_ref[:, 7 * width : 8 * width]).astype(BF16)
    send_ref[...] = out_ref[pl.ds(pl.multiple_of(info_ref[1], half), half), :]
    cot = cots_ref[...].astype(F32)
    sums_ref[...] = jnp.zeros_like(sums_ref)
    sums_ref[:, 6 * width : 7 * width] = jnp.sum(cot * unit, axis=0, keepdims=True)
    sums_ref[:, 7 * width : 8 * width] = jnp.sum(cot, axis=0, keepdims=True)
    scaled = cot * gain
    grad = inverse * (
        scaled
        - jnp.mean(scaled, axis=1, keepdims=True)
        - unit * jnp.mean(scaled * unit, axis=1, keepdims=True)
    )
    sums_ref[:, 3 * width : 4 * width] = jnp.sum(grad, axis=0, keepdims=True)
    grad_ref[...] = grad
    glow_ref[...] = grad.astype(BF16)


def aligned(value, to=128):
    return value if isinstance(value, int) else pl.multiple_of(value, to)


def ffn_backward_kernel(split, side, low_ref, glow_ref, act_ref, pull_ref, base_ref, sums_in_ref, *rest):
    pieces = 4 if side else 1
    up_refs, down_refs, rest = rest[:pieces], rest[pieces : 2 * pieces], rest[2 * pieces :]
    outs = 2 if split else 1
    gdown_refs, gup_refs, (gn_ref, sums_ref) = rest[:outs], rest[outs : 2 * outs], rest[2 * outs : 2 * outs + 2]
    rows, width = low_ref.shape
    fw = act_ref.shape[1]
    tile = 384
    low = low_ref[...]
    glow = glow_ref[...]
    gn_ref[...] = base_ref[...]
    sums_ref[...] = sums_in_ref[...]
    m = lax.axis_index("mp")
    base = 8 * width + (1 - m if side else m) * fw

    def down_part(number, down):
        spot = aligned(number * tile)
        cols = pl.ds(spot, tile)
        gdown = mm(act_ref[:, cols], glow, TN).astype(BF16)
        if split:
            keep_ref, send_ref = gdown_refs
            size = keep_ref.shape[1]
            per = tile // size
            emit([gdown[i * size : (i + 1) * size] for i in range(per)], number * (per // 2), keep_ref, send_ref, ())
        else:
            gdown_refs[0][cols, :] = gdown
        gupper = mm(glow, down, NT) * pull_ref[:, cols]
        sums_ref[:, pl.ds(pl.multiple_of(base + spot, 128), tile)] = jnp.sum(gupper, axis=0, keepdims=True)
        return gupper.astype(BF16)

    def up_part(number, gupper, up):
        cols = pl.ds(aligned(number * tile), tile)
        gup = mm(low, gupper, TN).astype(BF16)
        if split:
            keep_ref, send_ref = gup_refs
            size = keep_ref.shape[1] // 2
            shards = [gup[i * size : (i + 1) * size] for i in range(width // size)]
            under = pl.ds(aligned((number // 2) * size, 16), size)
            beside = pl.ds(aligned((number % 2) * tile), tile)
            emit(shards, 0, keep_ref, send_ref, (under, beside))
        else:
            gup_refs[0][:, cols] = gup
        gn_ref[...] += mm(gupper, up, NT)

    if side:
        gupper_ref = rest[2 * outs + 2]
        for i in range(4):
            number = quarter_place(2) ^ i
            cols = pl.ds(aligned(number * tile), tile)
            gupper_ref[:, cols] = down_part(number, down_refs[i][0:tile, :])
        for i in range(4):
            number = quarter_place(1) ^ i
            cols = pl.ds(aligned(number * tile), tile)
            up_part(number, gupper_ref[:, cols], up_refs[i][...])
    else:

        for number in range(fw // tile):
            cols = slice(number * tile, (number + 1) * tile)
            up_part(number, down_part(number, down_refs[0][cols, :]), up_refs[0][:, cols])


def norm_back_kernel(
    split,
    gn_ref,
    unit_ref,
    inv_ref,
    vec_ref,
    oa_ref,
    ob_ref,
    wa_ref,
    wb_ref,
    sums_in_ref,
    grad_ref,
    ga_ref,
    gb_ref,
    *rest,
):
    sums_ref = rest[-1]
    width = gn_ref.shape[1]
    gn = gn_ref[...]
    unit = unit_ref[...]
    sums_ref[...] = sums_in_ref[...]
    sums_ref[:, 4 * width : 5 * width] = jnp.sum(gn * unit, axis=0, keepdims=True)
    sums_ref[:, 5 * width : 6 * width] = jnp.sum(gn, axis=0, keepdims=True)
    scaled = gn * vec_ref[:, 4 * width : 5 * width]
    grad = inv_ref[...] * (
        scaled
        - jnp.mean(scaled, axis=1, keepdims=True)
        - unit * jnp.mean(scaled * unit, axis=1, keepdims=True)
    )
    sums_ref[:, 2 * width : 3 * width] = jnp.sum(grad, axis=0, keepdims=True)
    grad_ref[...] = grad
    low = grad.astype(BF16)
    ga_ref[...] = mm(low, wa_ref[...], NT).astype(BF16)
    gb_ref[...] = mm(low, wb_ref[...], NT).astype(BF16)
    for i, o_ref in enumerate((oa_ref, ob_ref)):
        gout = mm(o_ref[...], low, TN)
        if split:
            keep_ref, send_ref = rest[2 * i], rest[2 * i + 1]
            size = keep_ref.shape[1] // 2
            shards = []
            for j in range(gout.shape[0] // size):
                rows = gout[j * size : (j + 1) * size]
                shards.append(jnp.concatenate([rows[:, : width // 2], rows[:, width // 2 :]], axis=0).astype(BF16))
            emit(shards, 0, keep_ref, send_ref, ())
        else:
            rest[i][...] = gout.astype(BF16)


def combine_kernel(plans, *refs):
    total = sum(terms for pieces, _, _, _ in plans for terms, _ in pieces)
    ins, outs = refs[:total], refs[total:]
    for pieces, bit, where, count in plans:
        dests, outs = outs[:count], outs[count:]
        row = 0
        for terms, rows in pieces:
            here, ins = ins[:terms], ins[terms:]
            for j in range(dests[0].shape[0]):
                for number, dest in enumerate(dests):
                    spot = j + where
                    if count == 2:
                        odd = (lax.axis_index("dp") >> bit) % 2
                        side = odd if number == 0 else 1 - odd
                        spot = ((j >> where) << (where + 1)) + (side << where) + (j & ((1 << where) - 1))

                    def read(term):
                        cut = rows is not None and term.shape[1] > rows[1]
                        part = term[spot, rows[0] : rows[0] + rows[1], :] if cut else term[spot]
                        return part.astype(F32)

                    value = read(here[0])
                    for term in here[1:]:
                        value = value + read(term)
                    value = value.astype(dest.dtype)
                    if len(pieces) == 1:
                        dest[j] = value
                    else:
                        dest[j, row : row + value.shape[0], :] = value
            row += -(-(here[0].shape[1] if rows is None else rows[1]) // 16) * 16


def unswap_kernel(work_ref, got_ref, info_ref, out_ref):
    exchange_rows(info_ref, work_ref, got_ref, out_ref)


def flip(values, axis, bit, count):
    pairs = [(i, i ^ (1 << bit)) for i in range(count)]
    return lax.ppermute(values, axis, pairs)


def halve(values, bit):
    split = values.reshape((values.shape[0] // 2, 2) + values.shape[1:])
    keep = lax.dynamic_index_in_dim(split, bit, 1, keepdims=False)
    send = lax.dynamic_index_in_dim(split, 1 - bit, 1, keepdims=False)
    return keep, send


def body(
    tokens,
    cotangent,
    segment_ids,
    key_keep,
    in_weight,
    out_weight,
    up_weight,
    down_weight,
    in_master,
    out_master,
    up_master,
    down_master,
    in_first,
    out_first,
    up_first,
    down_first,
    in_second,
    out_second,
    up_second,
    down_second,
    vector_master,
    vector_first,
    vector_second,
):
    rows, width = tokens.shape
    d = lax.axis_index("dp")
    dp_count = lax.axis_size("dp")
    bits = dp_count.bit_length() - 1
    hw = in_weight.shape[2]
    fw = up_weight.shape[1]
    half = rows // 2
    smem = pltpu.SMEM
    length = vector_master.shape[0]
    vec = vector_master.reshape(1, length)
    in_own = jnp.transpose(in_weight, (1, 0, 2))
    split = (width // dp_count) % 16 == 0

    state = {"last": None}

    def run(kernel, outs, args, through=(), after=(), **options):
        before = () if state["last"] is None else (state["last"],)
        res = call(kernel, outs, args, after=tuple(after) + before, through=tuple(through), **options)
        state["last"] = res[-1] if through else res[0]
        return res

    s_tok, s_in, seg, code, info = run(
        prepare_kernel,
        [
            ((half, width), BF16),
            ((3, width // 4, hw), BF16),
            ((1, rows), jnp.int32),
            ((rows, 1), jnp.int32),
            ((8,), jnp.int32),
        ],
        (tokens, in_own, segment_ids, key_keep),
        scratch=[pltpu.SemaphoreType.DMA((2,))],
        limit=60,
        name="prepare",
        us=2,
        places={i: pltpu.HBM for i in range(2)},
        out_places={4: smem},
    )
    s_cot, s_out, s_up, s_down = run(
        prepare_rest_kernel,
        [
            ((half, width), BF16),
            ((hw // 4, width), BF16),
            ((width, fw // 4), BF16),
            ((fw // 4 + DOWN_PAD, width), BF16),
        ],
        (cotangent, out_weight, up_weight, down_weight, info),
        scratch=[pltpu.SemaphoreType.DMA((4,))],
        limit=60,
        name="prepare_rest",
        us=2,
        places={**{i: pltpu.HBM for i in range(4)}, 4: smem},
    )

    def relay(arrays, name, after=()):
        return run(lambda *refs: None, [], (), through=arrays, after=after, limit=4, name=name)

    def x_hop(values):
        return flip(values, "mp", 0, 2)

    def dp_hop(values, bit):
        return flip(values, "dp", bit, dp_count)

    def xy_hop(values):
        pairs = [(i, i ^ 5) for i in range(2 * dp_count)]
        return lax.ppermute(values, ("dp", "mp"), pairs)

    attn_flops = 2 * rows * width * 3 * hw + 4 * rows * rows * hw * 4
    wide = (rows, width)
    narrow = (rows, hw)
    hidden = (rows, fw)
    ffn_flops = 4 * rows * width * fw
    line = (1, length)
    attend_outs = [(narrow, BF16)] * 4 + [((8, rows), F32)]
    square = pltpu.VMEM((rows, rows), F32)

    got_tok = x_hop(s_tok)
    in_0 = x_hop(s_in)
    out_0 = x_hop(s_out)
    x, q_a, k_a, v_a, o_a, lse_a, s_up, s_down, s_cot = run(
        attend_forward_own_kernel,
        [(wide, BF16)] + attend_outs,
        (tokens, got_tok, info, in_own, vec, seg, code),
        through=(s_up, s_down, s_cot),
        scratch=[square],
        name="attend_forward_own",
        us=6,
        limit=OWN_LIMIT,
        places={2: smem},
    )
    up_0 = x_hop(s_up)
    in_0, out_0, s_down = relay((in_0, out_0, s_down), "relay_one")
    in_2 = dp_hop(in_0, 1)
    out_2 = dp_hop(out_0, 2)
    in_1 = dp_hop(in_0, 0)
    down_0 = x_hop(s_down)
    in_2, out_2, up_0, out_0 = relay((in_2, out_2, up_0, out_0), "relay_two")
    in_3 = dp_hop(in_2, 0)
    q_b, k_b, v_b, o_b, lse_b, in_other, s_cot, up_0, out_0, out_2 = run(
        attend_forward_other_kernel,
        attend_outs + [((3, width, hw), BF16)],
        (x, in_0, in_1, in_2, in_3, vec, seg, code),
        through=(s_cot, up_0, out_0, out_2),
        scratch=[square],
        name="attend_forward_other",
        us=6,
    )
    out_1 = dp_hop(out_0, 0)
    out_3 = dp_hop(out_2, 0)
    up_2 = dp_hop(up_0, 1)
    unit, inverse, low, out_other = run(
        out_norm_kernel,
        [(wide, F32), ((rows, 1), F32), (wide, BF16), ((hw, width), BF16)],
        (x, o_a, o_b, out_weight, out_0, out_1, out_2, out_3, vec),
        name="out_norm",
        us=1.5,
    )
    down_0, s_cot = relay((down_0, s_cot), "relay_down")
    down_2 = dp_hop(down_0, 2)
    got_cot = x_hop(s_cot)
    act_a, pull_a, part = run(
        ffn_own_kernel,
        [(hidden, BF16), (hidden, F32), (wide, F32)],
        (low, up_weight, down_weight, vec),
        name="ffn_own",
        us=8,
    )
    up_2, got_cot, up_0 = relay((up_2, got_cot, up_0), "relay_four")
    up_1 = dp_hop(up_0, 0)
    up_3 = dp_hop(up_2, 0)
    act_b, pull_b = run(
        ffn_other_kernel,
        [(hidden, BF16), (hidden, F32)],
        (low, up_0, up_1, up_2, up_3, vec),
        name="ffn_other",
        us=5,
    )
    down_2, down_0 = relay((down_2, down_0), "relay_five")
    down_1 = dp_hop(down_0, 0)
    down_3 = dp_hop(down_2, 0)
    ups = (up_0, up_1, up_2, up_3)
    downs = (down_0, down_1, down_2, down_3)
    out_work, s_layer, grad_two, glow, sums = run(
        ffn_finish_kernel,
        [(wide, BF16), ((half, width), BF16), (wide, F32), (wide, BF16), (line, F32)],
        (act_b, *downs, part, unit, vec, cotangent, got_cot, info),
        scratch=[pltpu.VMEM(wide, F32), pltpu.VMEM(wide, BF16)],
        name="ffn_finish",
        us=5,
        places={10: smem},
    )

    got_layer = x_hop(s_layer)

    def unswap(work, got, name):
        return run(unswap_kernel, [(wide, BF16)], (work, got, info), name=name, places={2: smem})[0]

    count = dp_count // 2
    down_shape = (fw // dp_count, width)
    up_shape = (2 * (width // dp_count), fw // 2)
    in_shape = (4, width // dp_count, hw)
    out_shape = (2 * (hw // dp_count), width // 2)

    def parts(shape):
        return [((count,) + shape, BF16)] * 2

    def ffn_back(side, act, pull, ups, downs, base, sums, name, after=()):
        kinds = parts(down_shape) + parts(up_shape) if split else [((fw, width), BF16), ((width, fw), BF16)]
        res = run(
            functools.partial(ffn_backward_kernel, split, side),
            kinds + [(wide, F32), (line, F32)],
            (low, glow, act, pull, base, sums, *ups, *downs),
            scratch=[pltpu.VMEM(hidden, BF16)] if side else [],
            name=name,
            us=10.5,
            after=after,
        )
        gn, sums = res[-2:]
        if split:
            return tuple(res[0:2]), tuple(res[2:4]), gn, sums
        down = halve(res[0].reshape((dp_count,) + down_shape), d & 1)
        up = jnp.transpose(res[1].reshape(dp_count, width // dp_count, 2, fw // 2), (0, 2, 1, 3))
        up = halve(up.reshape((dp_count,) + up_shape), d & 1)
        return down, up, gn, sums

    def pieces_of(terms):
        return terms if isinstance(terms, list) else [(terms, None)]

    def shape_of(pieces):
        rows = [t[0].shape[1] if r is None else r[1] for t, r in pieces]
        shape = pieces[0][0][0].shape
        if len(pieces) > 1:
            return (shape[0], sum(-(-r // 16) * 16 for r in rows), shape[2])
        return shape if pieces[0][1] is None else (shape[0], rows[0], shape[2])

    def halves(terms, bit, where=0, kinds=(F32, BF16)):
        pieces = pieces_of(terms)
        shape = shape_of(pieces)
        shape = (shape[0] // 2,) + shape[1:]
        return (pieces, bit, where, [(shape, kind) for kind in kinds])

    def whole(terms, kind=BF16, window=None):
        pieces = pieces_of(terms)
        shape = shape_of(pieces)
        if window is not None:
            shape = (window[1],) + shape[1:]
        return (pieces, None, 0 if window is None else window[0], [(shape, kind)])

    def combine(name, tensors, through=(), after=()):
        plans = tuple(
            (tuple((len(t), r) for t, r in pieces), bit, where, len(o)) for pieces, bit, where, o in tensors
        )
        res = run(
            functools.partial(combine_kernel, plans),
            [o for t in tensors for o in t[3]],
            [v for pieces, _, _, _ in tensors for t, _ in pieces for v in t],
            name=name,
            through=through,
            after=after,
        )
        res = list(res)
        made = []
        for t in tensors:
            made.append(tuple(res[: len(t[3])]) if len(t[3]) == 2 else res[0])
            res = res[len(t[3]) :]
        return made + res

    down_b, up_b, gn, sums = ffn_back(1, act_b, pull_b, ups, downs, grad_two, sums, "ffn_backward_other")
    core_down_b = dp_hop(down_b[1], 0)
    core_up_b = dp_hop(up_b[1], 0)
    down_a, up_a, gn, sums = ffn_back(
        0, act_a, pull_a, (up_weight,), (down_weight,), gn, sums, "ffn_backward_own"
    )
    core_down_a = dp_hop(down_a[1], 0)
    core_up_a = dp_hop(up_a[1], 0)
    (down_b_keep, down_b_send), (up_b_keep, up_b_send) = combine(
        "combine_ffn_other", [halves((down_b[0], core_down_b), 1), halves((up_b[0], core_up_b), 2, 1)]
    )
    y_down_b = dp_hop(down_b_send, 1)
    z_up_b = dp_hop(up_b_send, 2)

    kinds = parts(out_shape) * 2 if split else [((hw, width), BF16)] * 2
    grad_one, gatt_a, gatt_b, *gout, sums = run(
        functools.partial(norm_back_kernel, split),
        [(wide, F32), (narrow, BF16), (narrow, BF16)] + kinds + [(line, F32)],
        (gn, unit, inverse, vec, o_a, o_b, out_weight, out_other, sums),
        name="norm_back",
        us=2.5,
    )
    (down_a_keep, down_a_send), (up_a_keep, up_a_send) = combine(
        "combine_ffn_own", [halves((down_a[0], core_down_a), 1), halves((up_a[0], core_up_a), 2, 1)]
    )
    y_down_a = dp_hop(down_a_send, 1)
    z_up_a = dp_hop(up_a_send, 2)

    def attend_back(q, k, v, gatt, lse, name):
        return run(
            attend_backward_kernel,
            [(narrow, F32)] * 3,
            (q, k, v, gatt, lse, seg, code),
            scratch=[square],
            name=name,
            us=9,
        )

    def project_back(side, w, grads, base, kind, sums, gout, name, after=()):
        kinds = parts(in_shape) if split else [((3, width, hw), BF16)]
        res = run(
            functools.partial(project_backward_kernel, split, side),
            kinds + [(wide, kind), ((half, width), BF16), (line, F32)],
            (x, w, *grads, base, sums, info) + (tuple(gout) if split else ()),
            name=name,
            us=3,
            after=after,
            places={7: smem},
        )
        tg, back, sums = res[-3:]
        if split:
            return tuple(res[0:2]), tg, back, sums
        part = (dp_count, width // dp_count, hw)
        gout = jnp.transpose(gout[0].reshape(dp_count, hw // dp_count, 2, width // 2), (0, 2, 1, 3)).reshape(part)
        grads = jnp.concatenate([res[0].reshape((3,) + part), gout[None]])
        return halve(jnp.transpose(grads, (1, 0, 2, 3)), d & 1), tg, back, sums

    grads_b = attend_back(q_b, k_b, v_b, gatt_b, lse_b, "attend_backward_other")
    (sum_b,) = combine(
        "combine_ffn_x",
        [whole([((down_b_keep, y_down_b), None), ((up_b_keep, z_up_b), None)])],
        after=(got_layer,),
    )
    x_ffn = x_hop(sum_b)
    grads_a = attend_back(q_a, k_a, v_a, gatt_a, lse_a, "attend_backward_own")
    gout_a, gout_b = (gout[:2], gout[2:]) if split else (gout[:1], gout[1:])
    in_b, tg, _, sums = project_back(
        1, in_other, grads_b, grad_one, F32, sums, gout_b, "project_backward_other"
    )
    core_in_b = dp_hop(in_b[1], 0)
    in_a, tg, back, sums = project_back(0, in_own, grads_a, tg, BF16, sums, gout_a, "project_backward_own", (y_down_a, z_up_a))
    core_in_a = dp_hop(in_a[1], 0)
    sums = sums.reshape(1, length // 128, 128)
    z_sums = dp_hop(sums, 2)
    layer_out = unswap(out_work, got_layer, "unswap_out")
    (sums,) = combine("sums_z", [whole((sums, z_sums), F32)])
    for bit in range(4, bits):
        z_sums = dp_hop(sums, bit)
        (sums,) = combine("sums_z", [whole((sums, z_sums), F32)])
    z_sums = dp_hop(sums, 3)

    down_size, up_size = down_shape[0], up_shape[0]
    up_start = -(-down_size // 16) * 16
    down_t, up_t = combine(
        "tail_ffn",
        [
            halves([((down_a_keep, y_down_a, x_ffn), (0, down_size))], 2),
            halves([((up_a_keep, z_up_a, x_ffn), (up_start, up_size))], 1),
        ],
    )
    big = [((down_t[0], dp_hop(down_t[1], 2)), None), ((up_t[0], dp_hop(up_t[1], 1)), None)]
    (in_keep, in_y), (in_x, in_xy), sums = combine(
        "tail_core",
        [
            halves((in_a[0], core_in_a), 1),
            halves((in_b[0], core_in_b), 1, kinds=(BF16, BF16)),
            whole((sums, z_sums), F32),
        ],
    )
    in_terms = (in_keep, dp_hop(in_y, 1), x_hop(in_x), xy_hop(in_xy))
    for bit in range(2, bits):
        if bit == 2:
            in_t, sums, back = combine("tail_in", [halves(in_terms, bit)], through=(sums, back))
            x_sums = x_hop(sums)
            got_back = x_hop(back)
            in_terms = (in_t[0], dp_hop(in_t[1], bit))
            big_t, sums = combine("tail_more", [halves(big, bit + 1), whole((sums, x_sums), F32)])
            core_sums = dp_hop(sums, 0)
            big = (big_t[0], dp_hop(big_t[1], bit + 1))
        else:
            if bit == 3:
                in_t, sums = combine("tail_in_more", [halves(in_terms, bit), whole((sums, core_sums), F32)])
            else:
                in_t, big_t = combine("tail_in_more", [halves(in_terms, bit), halves(big, bit)])
                big = (big_t[0], dp_hop(big_t[1], bit))
            in_terms = (in_t[0], dp_hop(in_t[1], bit))
    sums = sums + dp_hop(sums, 1)
    token_grad = unswap(tg, got_back, "unswap_grad")

    def total(pair):
        keep, got = pair
        return (keep.astype(F32) + got.astype(F32)).reshape(keep.shape[1:])

    spot = 0
    grads = []
    for shape in (down_shape, up_shape):
        cut = tuple(v[:, spot : spot + shape[0]] for v in big)
        grads.append(total(cut))
        spot += -(-shape[0] // 16) * 16
    grad_down, grad_up = grads
    size = width // dp_count
    grad_up = jnp.concatenate([grad_up[:size], grad_up[size:]], axis=1)
    grad_in = total(in_terms)
    size = hw // dp_count
    grad_out = jnp.concatenate([grad_in[3, :size], grad_in[3, size:]], axis=1)
    grad_in = jnp.transpose(grad_in[:3], (1, 0, 2))
    grad_vector = sums.reshape(length)

    def matrix_step(grad, master, first, second):
        f, s, n = adam_step(grad, master, first, second, MATRIX_RATE, WEIGHT_DECAY)
        return (f, s, n, n.astype(BF16))

    return (
        layer_out,
        token_grad,
        *matrix_step(grad_in, in_master, in_first, in_second),
        *matrix_step(grad_out, out_master, out_first, out_second),
        *matrix_step(grad_up, up_master, up_first, up_second),
        *matrix_step(grad_down, down_master, down_first, down_second),
        *adam_step(grad_vector, vector_master, vector_first, vector_second, VECTOR_RATE, 0.0),
    )


def solution(mesh):
    tok = P(("dp", "mp"), None)
    line = P("dp", None)
    in_state = P("dp", None, "mp")
    out_state = P(("mp", "dp"), None)
    up_state = P("dp", "mp")
    states = (in_state, out_state, up_state, out_state)
    in_specs = (
        (tok, tok, line, line, P(None, None, "mp"), P("mp", None), P(None, "mp"), P("mp", None))
        + states * 3
        + (P(), P(), P())
    )
    out_specs = (
        (tok, tok)
        + (in_state,) * 4
        + (out_state,) * 4
        + (up_state,) * 4
        + (out_state,) * 4
        + (P(), P(), P())
    )
    return jax.shard_map(body, mesh=mesh, in_specs=in_specs, out_specs=out_specs, check_vma=False)
```

```python
import functools
import math

import jax
import jax.numpy as jnp
from jax import lax
from jax.experimental import pallas as pl
from jax.experimental.pallas import tpu as pltpu
from jax.sharding import PartitionSpec as P

HD = 64
STEP = 7
NORM_EPS = 1e-06
SCORE_SCALE = 0.125
NEG_FILL = -1e30
MOMENT_DECAY = 0.5
SQUARE_DECAY = 0.5
MATRIX_RATE = 0.03
VECTOR_RATE = 0.2
WEIGHT_DECAY = 0.01
ADAM_EPS = 1e-08
LOG2E = 1.4426950408889634
SCALE2 = SCORE_SCALE * LOG2E
F32 = jnp.float32
BF16 = jnp.bfloat16
MIB = 1024 * 1024
WORK = 1e6
SLACK = 16
OWN_LIMIT = 60
DOWN_PAD = 16

NN = (((1,), (0,)), ((), ()))
NT = (((1,), (1,)), ((), ()))
TN = (((0,), (0,)), ((), ()))


def mm(a, b, dims=NN):
    return lax.dot_general(a, b, dims, preferred_element_type=F32)


def padded_bytes(shape, dtype):
    rows = shape[-2] if len(shape) > 1 else 1
    tiles = -(-rows // 8) * 8 * -(-shape[-1] // 128) * 128
    return math.prod(shape[:-2]) * tiles * jnp.dtype(dtype).itemsize


def call(kernel, outs, args, scratch=(), limit=None, name=None, after=(), through=(), places=None, out_places=None, us=1):
    count = len(args)
    places = places or {}
    out_places = out_places or {}
    anywhere = pl.BlockSpec(memory_space=pl.ANY)
    specs = [pl.BlockSpec(memory_space=places.get(i, pltpu.VMEM)) for i in range(count)]
    specs += [anywhere] * (len(through) + len(after))
    made = len(outs)
    if limit is None:
        held = [(v.shape, v.dtype) for v in scratch if v.memory_space == pltpu.VMEM]
        limit = sum(padded_bytes(*v) for v in held) // MIB + SLACK

    def run(*refs):
        own = refs[count + len(through) + len(after) :]
        kernel(*refs[:count], *own[:made], *own[made + len(through) :])

    return pl.pallas_call(
        run,
        out_shape=[jax.ShapeDtypeStruct(s, d) for s, d in outs]
        + [jax.ShapeDtypeStruct(v.shape, v.dtype) for v in through],
        in_specs=specs,
        out_specs=[pl.BlockSpec(memory_space=out_places.get(i, pltpu.VMEM)) for i in range(made)] + [anywhere] * len(through),
        scratch_shapes=list(scratch),
        input_output_aliases={count + i: made + i for i in range(len(through))},
        compiler_params=pltpu.CompilerParams(vmem_limit_bytes=limit * MIB),
        cost_estimate=pl.CostEstimate(flops=int(us * WORK), bytes_accessed=0, transcendentals=0),
        name=name,
    )(*args, *through, *after)


def adam_step(grad, master, first, second, rate, decay):
    first_next = MOMENT_DECAY * first + (1.0 - MOMENT_DECAY) * grad
    second_next = SQUARE_DECAY * second + (1.0 - SQUARE_DECAY) * grad * grad
    first_fix = 1.0 - MOMENT_DECAY**STEP
    second_fix = 1.0 - SQUARE_DECAY**STEP
    update = first_next / first_fix / (jnp.sqrt(second_next / second_fix) + ADAM_EPS)
    master_next = master - rate * (update + decay * master)
    return (first_next, second_next, master_next)


def send_copies(pieces, sems):
    copies = []
    for i, (source, dest, axis, bit) in enumerate(pieces):
        size = source.shape[axis] // 4
        spot = pl.ds(pl.multiple_of(quarter_place(bit) * size, size), size)
        view = source.at[spot] if axis == 0 else source.at[:, spot]
        copies.append(pltpu.make_async_copy(view, dest.at[pl.ds(0, size)] if axis == 0 else dest, sems.at[i]))
    return copies


def prepare_kernel(tok_ref, in_ref, seg_ref, keep_ref, stok_ref, sin_ref, segrow_ref, code_ref, info_ref, sems):
    rows = tok_ref.shape[0]
    half = rows // 2
    m = lax.axis_index("mp")
    copies = send_copies([(in_ref, sin_ref, 1, 1)], sems)
    copies[0].start()
    seg = seg_ref[...]
    spot = lax.broadcasted_iota(jnp.int32, seg.shape, 1)
    later = jnp.roll(seg, rows + 1, axis=1)
    begin = jnp.sum(jnp.where((seg == later) & (spot <= rows), spot, 0))
    late = begin > half
    first = jnp.where(late, half, 0)
    info_ref[0] = begin
    info_ref[1] = first
    window = pl.ds(pl.multiple_of(first, half), half)
    copies.append(pltpu.make_async_copy(tok_ref.at[window], stok_ref, sems.at[1]))
    copies[1].start()
    own = pl.ds(pl.multiple_of(m * rows, rows), rows)
    other = pl.ds(pl.multiple_of((1 - m) * rows, rows), rows)
    local = lax.broadcasted_iota(jnp.int32, (1, rows), 1)
    swapped = jnp.where(late, local - begin, begin - 1 - local) >= 0
    mine = jnp.where(swapped, seg_ref[:, other], seg_ref[:, own])
    kept = jnp.where(swapped, keep_ref[:, other], keep_ref[:, own])
    segrow_ref[...] = mine
    code = jnp.where(kept == 1, mine, -1)
    code_ref[...] = jnp.broadcast_to(code.astype(F32), (8, rows)).T[:, 0:1].astype(jnp.int32)
    for copy in copies:
        copy.wait()


def prepare_rest_kernel(
    cot_ref, out_ref, up_ref, down_ref, info_ref, scot_ref, sout_ref, sup_ref, sdown_ref, sems
):
    half = scot_ref.shape[0]
    copies = send_copies([(out_ref, sout_ref, 0, 2), (down_ref, sdown_ref, 0, 2), (up_ref, sup_ref, 1, 1)], sems)
    window = pl.ds(pl.multiple_of(info_ref[1], half), half)
    copies.append(pltpu.make_async_copy(cot_ref.at[window], scot_ref, sems.at[3]))
    for copy in copies:
        copy.start()
    for copy in copies:
        copy.wait()


def swapped_rows(info_ref, shape):
    begin = info_ref[0]
    first = info_ref[1]
    local = first + lax.broadcasted_iota(jnp.int32, shape, 0)
    return jnp.where(first > 0, local - begin, begin - 1 - local) >= 0


def exchange_rows(info_ref, source_ref, got_ref, dest_ref):
    half = got_ref.shape[0]
    window = pl.ds(pl.multiple_of(info_ref[1], half), half)
    dest_ref[...] = source_ref[...]
    dest_ref[window, :] = jnp.where(swapped_rows(info_ref, got_ref.shape), got_ref[...], source_ref[window, :])


def fill_mask(seg_ref, code_ref, mask_ref):
    rows = mask_ref.shape[0]
    row = lax.broadcasted_iota(jnp.int32, (rows, rows), 0)
    col = lax.broadcasted_iota(jnp.int32, (rows, rows), 1)
    allowed = (code_ref[...] == seg_ref[...]) | (row == col)
    mask_ref[...] = jnp.where(allowed, 0.0, NEG_FILL)


def split_pair(block):
    lane = lax.broadcasted_iota(jnp.int32, block.shape, 1)
    zero = jnp.zeros_like(block)
    return (jnp.where(lane < HD, block, zero), jnp.where(lane < HD, zero, block))


def quarter_place(bit):
    d = lax.axis_index("dp")
    return 2 * ((d >> bit) % 2) + d % 2


def place_quarters(pieces, dest_ref, axis, bit):
    place = quarter_place(bit)
    for i, piece in enumerate(pieces):
        size = piece.shape[axis]
        spot = pl.ds(pl.multiple_of((place ^ i) * size, size), size)
        if axis == 0:
            dest_ref[spot, :] = piece[...]
        else:
            dest_ref[:, spot, :] = piece[...]


def attend_forward(which, width, x_ref, w_ref, vec_ref, seg_ref, code_ref, q_ref, k_ref, v_ref, o_ref, lse_ref, mask_ref):
    rows, hw = q_ref.shape
    fill_mask(seg_ref, code_ref, mask_ref)
    x = x_ref[...]
    for part, ref in enumerate((q_ref, k_ref, v_ref)):
        out = mm(x, w_ref[part])
        if part != 1:
            spot = pl.multiple_of((part // 2) * width + which * hw, 128)
            out = out + vec_ref[:, pl.ds(spot, hw)]
        ref[...] = out.astype(BF16)
    lse_ref[...] = jnp.zeros_like(lse_ref)
    for pair in range(hw // 128):
        cols = slice(pair * 128, (pair + 1) * 128)
        q = q_ref[:, cols]
        keys = split_pair(k_ref[:, cols])
        values = split_pair(v_ref[:, cols])
        mask = mask_ref[...]
        total = jnp.zeros((128, rows), F32)
        for head in range(2):
            scores = mm(keys[head], q, NT) * SCALE2 + mask
            highest = jnp.max(scores, axis=0, keepdims=True)
            weights = jnp.exp2(scores - highest)
            sums = jnp.sum(weights, axis=0, keepdims=True)
            probs = (weights * (1.0 / sums)).astype(BF16)
            total = total + mm(turned(values[head]), probs)
            lse_ref[2 * pair + head : 2 * pair + head + 1, :] = highest + jnp.log2(sums)
        o_ref[:, cols] = total.T.astype(BF16)


def attend_forward_own_kernel(
    tok_ref, got_ref, info_ref, w_ref, vec_ref, seg_ref, code_ref, x_ref, q_ref, k_ref, v_ref, o_ref, lse_ref, mask_ref
):
    exchange_rows(info_ref, tok_ref, got_ref, x_ref)
    which = lax.axis_index("mp")
    attend_forward(
        which, x_ref.shape[1], x_ref, w_ref, vec_ref, seg_ref, code_ref, q_ref, k_ref, v_ref, o_ref, lse_ref, mask_ref
    )


def attend_forward_other_kernel(
    x_ref, wa_ref, wb_ref, wc_ref, wd_ref, vec_ref, seg_ref, code_ref, q_ref, k_ref, v_ref, o_ref, lse_ref, w_ref, mask_ref
):
    place_quarters((wa_ref, wb_ref, wc_ref, wd_ref), w_ref, 1, 1)
    which = 1 - lax.axis_index("mp")
    attend_forward(
        which, x_ref.shape[1], x_ref, w_ref, vec_ref, seg_ref, code_ref, q_ref, k_ref, v_ref, o_ref, lse_ref, mask_ref
    )


def emit(value, index, keep_ref, send_ref, where):
    parity = lax.axis_index("dp") % 2
    for j in range(len(value) // 2):
        even, odd = value[2 * j], value[2 * j + 1]
        keep_ref[(index + j,) + where] = jnp.where(parity == 0, even, odd)
        send_ref[(index + j,) + where] = jnp.where(parity == 0, odd, even)


def turned(block):
    return block.astype(F32).T.astype(BF16)


def attend_backward_kernel(q_ref, k_ref, v_ref, do_ref, lse_ref, seg_ref, code_ref, dq_ref, dk_ref, dv_ref, mask_ref):
    rows, hw = q_ref.shape
    fill_mask(seg_ref, code_ref, mask_ref)
    for pair in range(hw // 128):
        cols = slice(pair * 128, (pair + 1) * 128)
        q = q_ref[:, cols]
        grad = do_ref[:, cols]
        keys = split_pair(k_ref[:, cols])
        values = split_pair(v_ref[:, cols])
        queries = split_pair(q)
        grads = split_pair(grad)
        mask = mask_ref[...]
        dq = jnp.zeros((128, rows), F32)
        dk = jnp.zeros((rows, 128), F32)
        dv = jnp.zeros((rows, 128), F32)
        for head in range(2):
            scores = mm(keys[head], q, NT) * SCALE2 + mask
            probs = jnp.exp2(scores - lse_ref[2 * pair + head : 2 * pair + head + 1, :])
            gprobs = mm(values[head], grad, NT)
            weighted = probs * gprobs
            delta = jnp.sum(weighted, axis=0, keepdims=True)
            gscores = ((weighted - probs * delta) * SCORE_SCALE).astype(BF16)
            dq = dq + mm(turned(keys[head]), gscores)
            dk = dk + mm(gscores, queries[head])
            dv = dv + mm(probs.astype(BF16), grads[head])
        dq_ref[:, cols] = dq.T
        dk_ref[:, cols] = dk
        dv_ref[:, cols] = dv


def project_backward_kernel(
    split, side, x_ref, w_ref, dq_ref, dk_ref, dv_ref, base_ref, sums_in_ref, info_ref, *rest
):
    if split:
        gout_refs, rest = rest[:2], rest[2:]
    outs = 2 if split else 1
    gin_refs = rest[:outs]
    tg_ref, back_ref, sums_ref = rest[outs:]
    hw = dq_ref.shape[1]
    width = x_ref.shape[1]
    half = back_ref.shape[0]
    if split:
        for dest, source in zip(gin_refs, gout_refs):
            for j in range(dest.shape[0]):
                dest[j, 3] = source[j]
    sums_ref[...] = sums_in_ref[...]
    m = lax.axis_index("mp")
    which = m if side == 0 else 1 - m
    x = x_ref[...]
    total = base_ref[...]
    for part, ref in enumerate((dq_ref, dk_ref, dv_ref)):
        grad = ref[...]
        if part != 1:
            spot = pl.multiple_of((part // 2) * width + which * hw, 128)
            sums_ref[:, pl.ds(spot, hw)] = jnp.sum(grad, axis=0, keepdims=True)
        grad_low = grad.astype(BF16)
        gin = mm(x, grad_low, TN).astype(BF16)
        if split:
            keep_ref, send_ref = gin_refs
            size = keep_ref.shape[2]
            emit([gin[i * size : (i + 1) * size] for i in range(width // size)], 0, keep_ref, send_ref, (part,))
        else:
            gin_refs[0][part] = gin
        total = total + mm(grad_low, w_ref[part], NT)
    tg_ref[...] = total.astype(tg_ref.dtype)
    if side == 0:
        window = pl.ds(pl.multiple_of(info_ref[1], half), half)
        back_ref[...] = tg_ref[window, :]
    else:
        back_ref[...] = jnp.zeros_like(back_ref)


def norm_stats(hidden):
    mean = jnp.mean(hidden, axis=1, keepdims=True)
    centred = hidden - mean
    inverse = lax.rsqrt(jnp.mean(centred * centred, axis=1, keepdims=True) + NORM_EPS)
    return centred * inverse, inverse


def out_norm_kernel(tok_ref, oa_ref, ob_ref, wo_ref, wa_ref, wb_ref, wc_ref, wd_ref, vec_ref, unit_ref, inv_ref, low_ref, w_ref):
    width = tok_ref.shape[1]
    place_quarters((wa_ref, wb_ref, wc_ref, wd_ref), w_ref, 0, 2)
    hidden = tok_ref[...].astype(F32) + (mm(oa_ref[...], wo_ref[...]) + mm(ob_ref[...], w_ref[...]))
    unit, inverse = norm_stats(hidden + vec_ref[:, 2 * width : 3 * width])
    unit_ref[...] = unit
    inv_ref[...] = inverse
    low_ref[...] = (unit * vec_ref[:, 4 * width : 5 * width] + vec_ref[:, 5 * width : 6 * width]).astype(BF16)


def gelu_parts(x):
    size = jnp.abs(x) * 0.7071067811865476
    bell = jnp.exp2(x * x * (-0.5 * LOG2E))
    t = 1.0 / (1.0 + 0.3275911 * size)
    poly = t * (
        0.254829592 + t * (-0.284496736 + t * (1.421413741 + t * (-1.453152027 + t * 1.061405429)))
    )
    tail = 0.5 * poly * bell
    below = jnp.where(x >= 0.0, 1.0 - tail, tail)
    return x * below, below + x * bell * 0.3989422804014327


def ffn_up(low, up, bias, act_ref, pull_ref, cols):
    upper = mm(low, up) + bias
    value, pull = gelu_parts(upper)
    act_ref[:, cols] = value.astype(BF16)
    pull_ref[:, cols] = pull


def ffn_own_kernel(low_ref, up_ref, down_ref, vec_ref, act_ref, pull_ref, total_ref):
    tile = 384
    width, fw = up_ref.shape
    low = low_ref[...]
    base = 8 * width + lax.axis_index("mp") * fw
    for step in range(fw // tile):
        cols = slice(step * tile, (step + 1) * tile)
        bias = vec_ref[:, pl.ds(pl.multiple_of(base + step * tile, 128), tile)]
        ffn_up(low, up_ref[:, cols], bias, act_ref, pull_ref, cols)
    total_ref[...] = mm(act_ref[...], down_ref[...])


def ffn_other_kernel(low_ref, ua_ref, ub_ref, uc_ref, ud_ref, vec_ref, act_ref, pull_ref):
    width, tile = ua_ref.shape
    low = low_ref[...]
    place = quarter_place(1)
    base = 8 * width + (1 - lax.axis_index("mp")) * 4 * tile
    for i, up_ref in enumerate((ua_ref, ub_ref, uc_ref, ud_ref)):
        spot = (place ^ i) * tile
        bias = vec_ref[:, pl.ds(pl.multiple_of(base + spot, 128), tile)]
        ffn_up(low, up_ref[...], bias, act_ref, pull_ref, pl.ds(pl.multiple_of(spot, 128), tile))


def ffn_finish_kernel(
    act_ref,
    da_ref,
    db_ref,
    dc_ref,
    dd_ref,
    part_ref,
    unit_ref,
    vec_ref,
    cot_ref,
    got_ref,
    info_ref,
    out_ref,
    send_ref,
    grad_ref,
    glow_ref,
    sums_ref,
    total_ref,
    cots_ref,
):
    width = part_ref.shape[1]
    half = got_ref.shape[0]
    tile = act_ref.shape[1] // 4
    place = quarter_place(2)
    total_ref[...] = part_ref[...]
    for i, down_ref in enumerate((da_ref, db_ref, dc_ref, dd_ref)):
        spot = pl.multiple_of((place ^ i) * tile, 128)
        total_ref[...] += mm(act_ref[:, pl.ds(spot, tile)], down_ref[0:tile, :])
    exchange_rows(info_ref, cot_ref, got_ref, cots_ref)
    normed = unit_ref[...] * vec_ref[:, 4 * width : 5 * width] + vec_ref[:, 5 * width : 6 * width]
    unit, inverse = norm_stats(normed + total_ref[...] + vec_ref[:, 3 * width : 4 * width])
    gain = vec_ref[:, 6 * width : 7 * width]
    out_ref[...] = (unit * gain + vec_ref[:, 7 * width : 8 * width]).astype(BF16)
    send_ref[...] = out_ref[pl.ds(pl.multiple_of(info_ref[1], half), half), :]
    cot = cots_ref[...].astype(F32)
    sums_ref[...] = jnp.zeros_like(sums_ref)
    sums_ref[:, 6 * width : 7 * width] = jnp.sum(cot * unit, axis=0, keepdims=True)
    sums_ref[:, 7 * width : 8 * width] = jnp.sum(cot, axis=0, keepdims=True)
    scaled = cot * gain
    grad = inverse * (
        scaled
        - jnp.mean(scaled, axis=1, keepdims=True)
        - unit * jnp.mean(scaled * unit, axis=1, keepdims=True)
    )
    sums_ref[:, 3 * width : 4 * width] = jnp.sum(grad, axis=0, keepdims=True)
    grad_ref[...] = grad
    glow_ref[...] = grad.astype(BF16)


def aligned(value, to=128):
    return value if isinstance(value, int) else pl.multiple_of(value, to)


def ffn_backward_kernel(split, side, low_ref, glow_ref, act_ref, pull_ref, base_ref, sums_in_ref, *rest):
    pieces = 4 if side else 1
    up_refs, down_refs, rest = rest[:pieces], rest[pieces : 2 * pieces], rest[2 * pieces :]
    outs = 2 if split else 1
    gdown_refs, gup_refs, (gn_ref, sums_ref) = rest[:outs], rest[outs : 2 * outs], rest[2 * outs : 2 * outs + 2]
    rows, width = low_ref.shape
    fw = act_ref.shape[1]
    tile = 384
    low = low_ref[...]
    glow = glow_ref[...]
    gn_ref[...] = base_ref[...]
    sums_ref[...] = sums_in_ref[...]
    m = lax.axis_index("mp")
    base = 8 * width + (1 - m if side else m) * fw

    def down_part(number, down):
        spot = aligned(number * tile)
        cols = pl.ds(spot, tile)
        gdown = mm(act_ref[:, cols], glow, TN).astype(BF16)
        if split:
            keep_ref, send_ref = gdown_refs
            size = keep_ref.shape[1]
            per = tile // size
            emit([gdown[i * size : (i + 1) * size] for i in range(per)], number * (per // 2), keep_ref, send_ref, ())
        else:
            gdown_refs[0][cols, :] = gdown
        gupper = mm(glow, down, NT) * pull_ref[:, cols]
        sums_ref[:, pl.ds(pl.multiple_of(base + spot, 128), tile)] = jnp.sum(gupper, axis=0, keepdims=True)
        return gupper.astype(BF16)

    def up_part(number, gupper, up):
        cols = pl.ds(aligned(number * tile), tile)
        gup = mm(low, gupper, TN).astype(BF16)
        if split:
            keep_ref, send_ref = gup_refs
            size = keep_ref.shape[1] // 2
            shards = [gup[i * size : (i + 1) * size] for i in range(width // size)]
            under = pl.ds(aligned((number // 2) * size, 16), size)
            beside = pl.ds(aligned((number % 2) * tile), tile)
            emit(shards, 0, keep_ref, send_ref, (under, beside))
        else:
            gup_refs[0][:, cols] = gup
        gn_ref[...] += mm(gupper, up, NT)

    if side:
        gupper_ref = rest[2 * outs + 2]
        for i in range(4):
            number = quarter_place(2) ^ i
            cols = pl.ds(aligned(number * tile), tile)
            gupper_ref[:, cols] = down_part(number, down_refs[i][0:tile, :])
        for i in range(4):
            number = quarter_place(1) ^ i
            cols = pl.ds(aligned(number * tile), tile)
            up_part(number, gupper_ref[:, cols], up_refs[i][...])
    else:

        for number in range(fw // tile):
            cols = slice(number * tile, (number + 1) * tile)
            up_part(number, down_part(number, down_refs[0][cols, :]), up_refs[0][:, cols])


def norm_back_kernel(
    split,
    gn_ref,
    unit_ref,
    inv_ref,
    vec_ref,
    oa_ref,
    ob_ref,
    wa_ref,
    wb_ref,
    sums_in_ref,
    grad_ref,
    ga_ref,
    gb_ref,
    *rest,
):
    sums_ref = rest[-1]
    width = gn_ref.shape[1]
    gn = gn_ref[...]
    unit = unit_ref[...]
    sums_ref[...] = sums_in_ref[...]
    sums_ref[:, 4 * width : 5 * width] = jnp.sum(gn * unit, axis=0, keepdims=True)
    sums_ref[:, 5 * width : 6 * width] = jnp.sum(gn, axis=0, keepdims=True)
    scaled = gn * vec_ref[:, 4 * width : 5 * width]
    grad = inv_ref[...] * (
        scaled
        - jnp.mean(scaled, axis=1, keepdims=True)
        - unit * jnp.mean(scaled * unit, axis=1, keepdims=True)
    )
    sums_ref[:, 2 * width : 3 * width] = jnp.sum(grad, axis=0, keepdims=True)
    grad_ref[...] = grad
    low = grad.astype(BF16)
    ga_ref[...] = mm(low, wa_ref[...], NT).astype(BF16)
    gb_ref[...] = mm(low, wb_ref[...], NT).astype(BF16)
    for i, o_ref in enumerate((oa_ref, ob_ref)):
        gout = mm(o_ref[...], low, TN)
        if split:
            keep_ref, send_ref = rest[2 * i], rest[2 * i + 1]
            size = keep_ref.shape[1] // 2
            shards = []
            for j in range(gout.shape[0] // size):
                rows = gout[j * size : (j + 1) * size]
                shards.append(jnp.concatenate([rows[:, : width // 2], rows[:, width // 2 :]], axis=0).astype(BF16))
            emit(shards, 0, keep_ref, send_ref, ())
        else:
            rest[i][...] = gout.astype(BF16)


def combine_kernel(plans, *refs):
    total = sum(terms for pieces, _, _, _ in plans for terms, _ in pieces)
    ins, outs = refs[:total], refs[total:]
    for pieces, bit, where, count in plans:
        dests, outs = outs[:count], outs[count:]
        row = 0
        for terms, rows in pieces:
            here, ins = ins[:terms], ins[terms:]
            for j in range(dests[0].shape[0]):
                for number, dest in enumerate(dests):
                    spot = j + where
                    if count == 2:
                        odd = (lax.axis_index("dp") >> bit) % 2
                        side = odd if number == 0 else 1 - odd
                        spot = ((j >> where) << (where + 1)) + (side << where) + (j & ((1 << where) - 1))

                    def read(term):
                        cut = rows is not None and term.shape[1] > rows[1]
                        part = term[spot, rows[0] : rows[0] + rows[1], :] if cut else term[spot]
                        return part.astype(F32)

                    value = read(here[0])
                    for term in here[1:]:
                        value = value + read(term)
                    value = value.astype(dest.dtype)
                    if len(pieces) == 1:
                        dest[j] = value
                    else:
                        dest[j, row : row + value.shape[0], :] = value
            row += -(-(here[0].shape[1] if rows is None else rows[1]) // 16) * 16


def matrix_step(states, outs, number, grad, at):
    master, first, second = (ref[at] for ref in states[3 * number : 3 * number + 3])
    f, s, n = adam_step(grad, master, first, second, MATRIX_RATE, WEIGHT_DECAY)
    for ref, value in zip(outs[4 * number : 4 * number + 4], (f, s, n, n.astype(BF16))):
        ref[at] = value


def ffn_steps_kernel(down_ref, down_got_ref, up_ref, up_got_ref, *rest):
    states, outs = rest[:6], rest[6:]
    rows = states[0].shape[0]
    width = down_ref.shape[2]
    matrix_step(states, outs, 1, down_ref[0] + down_got_ref[0].astype(F32), (slice(None), slice(None)))
    grad = up_ref[0] + up_got_ref[0].astype(F32)
    for side in range(2):
        cols = slice(side * width, (side + 1) * width)
        matrix_step(states, outs, 0, grad[side * rows : (side + 1) * rows], (slice(None), cols))


def in_steps_kernel(in_ref, in_got_ref, sums_ref, sums_got_ref, *rest):
    states, vectors, outs = rest[:6], rest[6:9], rest[9:]
    grad_in = in_ref[0] + in_got_ref[0].astype(F32)
    for part in range(3):
        matrix_step(states, outs, 0, grad_in[part], (part,))
    rows, width = states[3].shape
    for side in range(2):
        cols = slice(side * width // 2, (side + 1) * width // 2)
        matrix_step(states, outs, 1, grad_in[3][side * rows : (side + 1) * rows], (slice(None), cols))
    made = adam_step(sums_ref[0] + sums_got_ref[0], *(ref[...] for ref in vectors), VECTOR_RATE, 0.0)
    for ref, value in zip(outs[8:], made):
        ref[...] = value


def unswap_kernel(work_ref, got_ref, info_ref, out_ref):
    exchange_rows(info_ref, work_ref, got_ref, out_ref)


def flip(values, axis, bit, count):
    pairs = [(i, i ^ (1 << bit)) for i in range(count)]
    return lax.ppermute(values, axis, pairs)


def halve(values, bit):
    split = values.reshape((values.shape[0] // 2, 2) + values.shape[1:])
    keep = lax.dynamic_index_in_dim(split, bit, 1, keepdims=False)
    send = lax.dynamic_index_in_dim(split, 1 - bit, 1, keepdims=False)
    return keep, send


def body(
    tokens,
    cotangent,
    segment_ids,
    key_keep,
    in_weight,
    out_weight,
    up_weight,
    down_weight,
    in_master,
    out_master,
    up_master,
    down_master,
    in_first,
    out_first,
    up_first,
    down_first,
    in_second,
    out_second,
    up_second,
    down_second,
    vector_master,
    vector_first,
    vector_second,
):
    rows, width = tokens.shape
    d = lax.axis_index("dp")
    dp_count = lax.axis_size("dp")
    bits = dp_count.bit_length() - 1
    hw = in_weight.shape[2]
    fw = up_weight.shape[1]
    half = rows // 2
    smem = pltpu.SMEM
    length = vector_master.shape[0]
    vec = vector_master.reshape(1, length)
    in_own = jnp.transpose(in_weight, (1, 0, 2))
    split = (width // dp_count) % 16 == 0

    state = {"last": None}

    def run(kernel, outs, args, through=(), after=(), **options):
        before = () if state["last"] is None else (state["last"],)
        res = call(kernel, outs, args, after=tuple(after) + before, through=tuple(through), **options)
        state["last"] = res[-1] if through else res[0]
        return res

    s_tok, s_in, seg, code, info = run(
        prepare_kernel,
        [
            ((half, width), BF16),
            ((3, width // 4, hw), BF16),
            ((1, rows), jnp.int32),
            ((rows, 1), jnp.int32),
            ((8,), jnp.int32),
        ],
        (tokens, in_own, segment_ids, key_keep),
        scratch=[pltpu.SemaphoreType.DMA((2,))],
        limit=60,
        name="prepare",
        us=2,
        places={i: pltpu.HBM for i in range(2)},
        out_places={4: smem},
    )
    s_cot, s_out, s_up, s_down = run(
        prepare_rest_kernel,
        [
            ((half, width), BF16),
            ((hw // 4, width), BF16),
            ((width, fw // 4), BF16),
            ((fw // 4 + DOWN_PAD, width), BF16),
        ],
        (cotangent, out_weight, up_weight, down_weight, info),
        scratch=[pltpu.SemaphoreType.DMA((4,))],
        limit=60,
        name="prepare_rest",
        us=2,
        places={**{i: pltpu.HBM for i in range(4)}, 4: smem},
    )

    def relay(arrays, name, after=()):
        return run(lambda *refs: None, [], (), through=arrays, after=after, limit=4, name=name)

    def x_hop(values):
        return flip(values, "mp", 0, 2)

    def dp_hop(values, bit):
        return flip(values, "dp", bit, dp_count)

    def xy_hop(values):
        pairs = [(i, i ^ 5) for i in range(2 * dp_count)]
        return lax.ppermute(values, ("dp", "mp"), pairs)

    attn_flops = 2 * rows * width * 3 * hw + 4 * rows * rows * hw * 4
    wide = (rows, width)
    narrow = (rows, hw)
    hidden = (rows, fw)
    ffn_flops = 4 * rows * width * fw
    line = (1, length)
    attend_outs = [(narrow, BF16)] * 4 + [((8, rows), F32)]
    square = pltpu.VMEM((rows, rows), F32)

    got_tok = x_hop(s_tok)
    in_0 = x_hop(s_in)
    out_0 = x_hop(s_out)
    x, q_a, k_a, v_a, o_a, lse_a, s_up, s_down, s_cot = run(
        attend_forward_own_kernel,
        [(wide, BF16)] + attend_outs,
        (tokens, got_tok, info, in_own, vec, seg, code),
        through=(s_up, s_down, s_cot),
        scratch=[square],
        name="attend_forward_own",
        us=6,
        limit=OWN_LIMIT,
        places={2: smem},
    )
    up_0 = x_hop(s_up)
    in_0, out_0, s_down = relay((in_0, out_0, s_down), "relay_one")
    in_2 = dp_hop(in_0, 1)
    out_2 = dp_hop(out_0, 2)
    in_1 = dp_hop(in_0, 0)
    down_0 = x_hop(s_down)
    in_2, out_2, up_0, out_0 = relay((in_2, out_2, up_0, out_0), "relay_two")
    in_3 = dp_hop(in_2, 0)
    q_b, k_b, v_b, o_b, lse_b, in_other, s_cot, up_0, out_0, out_2 = run(
        attend_forward_other_kernel,
        attend_outs + [((3, width, hw), BF16)],
        (x, in_0, in_1, in_2, in_3, vec, seg, code),
        through=(s_cot, up_0, out_0, out_2),
        scratch=[square],
        name="attend_forward_other",
        us=6,
    )
    out_1 = dp_hop(out_0, 0)
    out_3 = dp_hop(out_2, 0)
    up_2 = dp_hop(up_0, 1)
    unit, inverse, low, out_other = run(
        out_norm_kernel,
        [(wide, F32), ((rows, 1), F32), (wide, BF16), ((hw, width), BF16)],
        (x, o_a, o_b, out_weight, out_0, out_1, out_2, out_3, vec),
        name="out_norm",
        us=1.5,
    )
    down_0, s_cot = relay((down_0, s_cot), "relay_down")
    down_2 = dp_hop(down_0, 2)
    got_cot = x_hop(s_cot)
    act_a, pull_a, part = run(
        ffn_own_kernel,
        [(hidden, BF16), (hidden, F32), (wide, F32)],
        (low, up_weight, down_weight, vec),
        name="ffn_own",
        us=8,
    )
    up_2, got_cot, up_0 = relay((up_2, got_cot, up_0), "relay_four")
    up_1 = dp_hop(up_0, 0)
    up_3 = dp_hop(up_2, 0)
    act_b, pull_b = run(
        ffn_other_kernel,
        [(hidden, BF16), (hidden, F32)],
        (low, up_0, up_1, up_2, up_3, vec),
        name="ffn_other",
        us=5,
    )
    down_2, down_0 = relay((down_2, down_0), "relay_five")
    down_1 = dp_hop(down_0, 0)
    down_3 = dp_hop(down_2, 0)
    ups = (up_0, up_1, up_2, up_3)
    downs = (down_0, down_1, down_2, down_3)
    out_work, s_layer, grad_two, glow, sums = run(
        ffn_finish_kernel,
        [(wide, BF16), ((half, width), BF16), (wide, F32), (wide, BF16), (line, F32)],
        (act_b, *downs, part, unit, vec, cotangent, got_cot, info),
        scratch=[pltpu.VMEM(wide, F32), pltpu.VMEM(wide, BF16)],
        name="ffn_finish",
        us=5,
        places={10: smem},
    )

    got_layer = x_hop(s_layer)

    def unswap(work, got, name):
        return run(unswap_kernel, [(wide, BF16)], (work, got, info), name=name, places={2: smem})[0]

    count = dp_count // 2
    down_shape = (fw // dp_count, width)
    up_shape = (2 * (width // dp_count), fw // 2)
    in_shape = (4, width // dp_count, hw)
    out_shape = (2 * (hw // dp_count), width // 2)

    def parts(shape):
        return [((count,) + shape, BF16)] * 2

    def ffn_back(side, act, pull, ups, downs, base, sums, name, after=()):
        kinds = parts(down_shape) + parts(up_shape) if split else [((fw, width), BF16), ((width, fw), BF16)]
        res = run(
            functools.partial(ffn_backward_kernel, split, side),
            kinds + [(wide, F32), (line, F32)],
            (low, glow, act, pull, base, sums, *ups, *downs),
            scratch=[pltpu.VMEM(hidden, BF16)] if side else [],
            name=name,
            us=10.5,
            after=after,
        )
        gn, sums = res[-2:]
        if split:
            return tuple(res[0:2]), tuple(res[2:4]), gn, sums
        down = halve(res[0].reshape((dp_count,) + down_shape), d & 1)
        up = jnp.transpose(res[1].reshape(dp_count, width // dp_count, 2, fw // 2), (0, 2, 1, 3))
        up = halve(up.reshape((dp_count,) + up_shape), d & 1)
        return down, up, gn, sums

    def pieces_of(terms):
        return terms if isinstance(terms, list) else [(terms, None)]

    def shape_of(pieces):
        rows = [t[0].shape[1] if r is None else r[1] for t, r in pieces]
        shape = pieces[0][0][0].shape
        if len(pieces) > 1:
            return (shape[0], sum(-(-r // 16) * 16 for r in rows), shape[2])
        return shape if pieces[0][1] is None else (shape[0], rows[0], shape[2])

    def halves(terms, bit, where=0, kinds=(F32, BF16)):
        pieces = pieces_of(terms)
        shape = shape_of(pieces)
        shape = (shape[0] // 2,) + shape[1:]
        return (pieces, bit, where, [(shape, kind) for kind in kinds])

    def whole(terms, kind=BF16, window=None):
        pieces = pieces_of(terms)
        shape = shape_of(pieces)
        if window is not None:
            shape = (window[1],) + shape[1:]
        return (pieces, None, 0 if window is None else window[0], [(shape, kind)])

    def combine(name, tensors, through=(), after=()):
        plans = tuple(
            (tuple((len(t), r) for t, r in pieces), bit, where, len(o)) for pieces, bit, where, o in tensors
        )
        res = run(
            functools.partial(combine_kernel, plans),
            [o for t in tensors for o in t[3]],
            [v for pieces, _, _, _ in tensors for t, _ in pieces for v in t],
            name=name,
            through=through,
            after=after,
        )
        res = list(res)
        made = []
        for t in tensors:
            made.append(tuple(res[: len(t[3])]) if len(t[3]) == 2 else res[0])
            res = res[len(t[3]) :]
        return made + res

    down_b, up_b, gn, sums = ffn_back(1, act_b, pull_b, ups, downs, grad_two, sums, "ffn_backward_other")
    core_down_b = dp_hop(down_b[1], 0)
    core_up_b = dp_hop(up_b[1], 0)
    down_a, up_a, gn, sums = ffn_back(
        0, act_a, pull_a, (up_weight,), (down_weight,), gn, sums, "ffn_backward_own"
    )
    core_down_a = dp_hop(down_a[1], 0)
    core_up_a = dp_hop(up_a[1], 0)
    (down_b_keep, down_b_send), (up_b_keep, up_b_send) = combine(
        "combine_ffn_other", [halves((down_b[0], core_down_b), 1), halves((up_b[0], core_up_b), 2, 1)]
    )
    y_down_b = dp_hop(down_b_send, 1)
    z_up_b = dp_hop(up_b_send, 2)

    kinds = parts(out_shape) * 2 if split else [((hw, width), BF16)] * 2
    grad_one, gatt_a, gatt_b, *gout, sums = run(
        functools.partial(norm_back_kernel, split),
        [(wide, F32), (narrow, BF16), (narrow, BF16)] + kinds + [(line, F32)],
        (gn, unit, inverse, vec, o_a, o_b, out_weight, out_other, sums),
        name="norm_back",
        us=2.5,
    )
    (down_a_keep, down_a_send), (up_a_keep, up_a_send) = combine(
        "combine_ffn_own", [halves((down_a[0], core_down_a), 1), halves((up_a[0], core_up_a), 2, 1)]
    )
    y_down_a = dp_hop(down_a_send, 1)
    z_up_a = dp_hop(up_a_send, 2)

    def attend_back(q, k, v, gatt, lse, name):
        return run(
            attend_backward_kernel,
            [(narrow, F32)] * 3,
            (q, k, v, gatt, lse, seg, code),
            scratch=[square],
            name=name,
            us=9,
        )

    def project_back(side, w, grads, base, kind, sums, gout, name, after=()):
        kinds = parts(in_shape) if split else [((3, width, hw), BF16)]
        res = run(
            functools.partial(project_backward_kernel, split, side),
            kinds + [(wide, kind), ((half, width), BF16), (line, F32)],
            (x, w, *grads, base, sums, info) + (tuple(gout) if split else ()),
            name=name,
            us=3,
            after=after,
            places={7: smem},
        )
        tg, back, sums = res[-3:]
        if split:
            return tuple(res[0:2]), tg, back, sums
        part = (dp_count, width // dp_count, hw)
        gout = jnp.transpose(gout[0].reshape(dp_count, hw // dp_count, 2, width // 2), (0, 2, 1, 3)).reshape(part)
        grads = jnp.concatenate([res[0].reshape((3,) + part), gout[None]])
        return halve(jnp.transpose(grads, (1, 0, 2, 3)), d & 1), tg, back, sums

    grads_b = attend_back(q_b, k_b, v_b, gatt_b, lse_b, "attend_backward_other")
    (sum_b,) = combine(
        "combine_ffn_x",
        [whole([((down_b_keep, y_down_b), None), ((up_b_keep, z_up_b), None)])],
        after=(got_layer,),
    )
    x_ffn = x_hop(sum_b)
    grads_a = attend_back(q_a, k_a, v_a, gatt_a, lse_a, "attend_backward_own")
    gout_a, gout_b = (gout[:2], gout[2:]) if split else (gout[:1], gout[1:])
    in_b, tg, _, sums = project_back(
        1, in_other, grads_b, grad_one, F32, sums, gout_b, "project_backward_other"
    )
    core_in_b = dp_hop(in_b[1], 0)
    in_a, tg, back, sums = project_back(0, in_own, grads_a, tg, BF16, sums, gout_a, "project_backward_own", (y_down_a, z_up_a))
    core_in_a = dp_hop(in_a[1], 0)
    sums = sums.reshape(1, length // 128, 128)
    z_sums = dp_hop(sums, 2)
    layer_out = unswap(out_work, got_layer, "unswap_out")
    (sums,) = combine("sums_z", [whole((sums, z_sums), F32)])
    for bit in range(4, bits):
        z_sums = dp_hop(sums, bit)
        (sums,) = combine("sums_z", [whole((sums, z_sums), F32)])
    z_sums = dp_hop(sums, 3)

    down_size, up_size = down_shape[0], up_shape[0]
    up_start = -(-down_size // 16) * 16
    down_t, up_t = combine(
        "tail_ffn",
        [
            halves([((down_a_keep, y_down_a, x_ffn), (0, down_size))], 2),
            halves([((up_a_keep, z_up_a, x_ffn), (up_start, up_size))], 3, 1),
        ],
    )
    down_terms = (down_t[0], dp_hop(down_t[1], 2))
    up_terms = (up_t[0], dp_hop(up_t[1], 3))
    (in_keep, in_y), (in_x, in_xy), sums = combine(
        "tail_core",
        [
            halves((in_a[0], core_in_a), 1),
            halves((in_b[0], core_in_b), 1, kinds=(BF16, BF16)),
            whole((sums, z_sums), F32),
        ],
    )
    in_terms = (in_keep, dp_hop(in_y, 1), x_hop(in_x), xy_hop(in_xy))
    in_t, down_t, up_t, sums, back = combine(
        "tail_two", [halves(in_terms, 2), halves(down_terms, 3), halves(up_terms, 1)], through=(sums, back)
    )
    in_terms = (in_t[0], dp_hop(in_t[1], 2))
    down_terms = (down_t[0], dp_hop(down_t[1], 3))
    up_terms = (up_t[0], dp_hop(up_t[1], 1))
    core_sums = dp_hop(sums, 0)
    got_back = x_hop(back)
    in_t, sums = combine("tail_in", [halves(in_terms, 3), whole((sums, core_sums), F32)])
    in_terms = (in_t[0], dp_hop(in_t[1], 3))
    y_sums = dp_hop(sums, 1)
    big = [(down_terms, None), (up_terms, None)]
    for bit in range(4, bits):
        in_t, big_t = combine("tail_more", [halves(in_terms, bit), halves(big, bit)])
        big = (big_t[0], dp_hop(big_t[1], bit))
        in_terms = (in_t[0], dp_hop(in_t[1], bit))
    token_grad = unswap(tg, got_back, "unswap_grad")
    (sums,) = combine("sums_y", [whole((sums, y_sums), F32)])
    x_sums = x_hop(sums)

    state_in = [jnp.transpose(v, (1, 0, 2)) for v in (in_master, in_first, in_second)]
    states = (
        *state_in,
        *(out_master, out_first, out_second),
        *(up_master, up_first, up_second),
        *(down_master, down_first, down_second),
    )
    if split:
        kinds = []
        for v in states[::3]:
            kinds += [(v.shape, F32)] * 3 + [(v.shape, BF16)]
        line = (length // 128, 128)
        vectors = [v.reshape(line) for v in (vector_master, vector_first, vector_second)]
        steps_ffn = run(ffn_steps_kernel, kinds[8:], (*down_terms, *up_terms, *states[6:]), name="steps_ffn")
        steps_in = run(
            in_steps_kernel,
            kinds[:8] + [(line, F32)] * 3,
            (*in_terms, sums, x_sums, *states[:6], *vectors),
            name="steps_in",
        )
        steps = list(steps_in[:8]) + list(steps_ffn)
        vector_steps = [v.reshape(length) for v in steps_in[8:]]
    else:

        def total(pair):
            keep, got = pair
            return (keep.astype(F32) + got.astype(F32)).reshape(keep.shape[1:])

        spot = 0
        grads = []
        for shape in (down_shape, up_shape):
            cut = tuple(v[:, spot : spot + shape[0]] for v in big)
            grads.append(total(cut))
            spot += -(-shape[0] // 16) * 16
        grad_down, grad_up = grads
        size = width // dp_count
        grad_up = jnp.concatenate([grad_up[:size], grad_up[size:]], axis=1)
        grad_in = total(in_terms)
        size = hw // dp_count
        grad_out = jnp.concatenate([grad_in[3, :size], grad_in[3, size:]], axis=1)
        steps = []
        for number, grad in enumerate((grad_in[:3], grad_out, grad_up, grad_down)):
            f, s, n = adam_step(grad, *states[3 * number : 3 * number + 3], MATRIX_RATE, WEIGHT_DECAY)
            steps += [f, s, n, n.astype(BF16)]
        grad_vector = (sums + x_sums).reshape(length)
        vector_steps = adam_step(grad_vector, vector_master, vector_first, vector_second, VECTOR_RATE, 0.0)
    steps = [jnp.transpose(v, (1, 0, 2)) for v in steps[:4]] + list(steps[4:])

    return (
        layer_out,
        token_grad,
        *steps,
        *vector_steps,
    )


def solution(mesh):
    tok = P(("dp", "mp"), None)
    line = P("dp", None)
    in_state = P("dp", None, "mp")
    out_state = P(("mp", "dp"), None)
    up_state = P("dp", "mp")
    states = (in_state, out_state, up_state, out_state)
    in_specs = (
        (tok, tok, line, line, P(None, None, "mp"), P("mp", None), P(None, "mp"), P("mp", None))
        + states * 3
        + (P(), P(), P())
    )
    out_specs = (
        (tok, tok)
        + (in_state,) * 4
        + (out_state,) * 4
        + (up_state,) * 4
        + (out_state,) * 4
        + (P(), P(), P())
    )
    return jax.shard_map(body, mesh=mesh, in_specs=in_specs, out_specs=out_specs, check_vma=False)
```
